128 devices in a mesh: tm: 8 (over y, core), tensor: 16 (over z, x).
Axes of the slice: x: 4, y: 4, z: 4, core: 2. Of those that a mesh axis runs over, the one named last changes fastest.
Arguments:
- queries: bfloat16 [5120, 4096], P('tm', 'tensor'), may hold values from -6 to 6
- keys: bfloat16 [5120, 4096], P('tm', 'tensor'), may hold values from -6 to 6
- values: bfloat16 [5120, 4096], P('tm', 'tensor'), may hold values from -6 to 6
- grad_out: bfloat16 [5120, 5120], P('tm', 'tensor'), may hold values from -18 to 18
- frame_map: int32 [8], replicated, may hold values from 0 to 7, as said below
- band: int32 [8, 8], replicated, may hold values from -1 to 640, as said below
- w_query: bfloat16 [5120, 4096], P(None, 'tensor'), may hold values from -0.75 to 0.75
- w_key: bfloat16 [5120, 4096], P(None, 'tensor'), may hold values from -0.75 to 0.75
- w_value: bfloat16 [5120, 4096], P(None, 'tensor'), may hold values from -0.75 to 0.75
- w_out: bfloat16 [4096, 5120], P('tensor'), may hold values from -0.09375 to 0.09375
Outputs:
- input_grad: bfloat16 [5120, 5120], P('tensor', 'tm')
The draws below stay inside these ranges and needn't reach their ends.
Inputs may be any that keep to these rules, and one draw needn't show every extreme that they name: `frame_map`: each latent frame is held by exactly one slot. band[i][j] is 640 where i == j, -1 (nothing attends) where |i - j| > 4, and otherwise between half of and all of 640 // 2**ceil(log2 |i - j|), rounded down.
All inputs are finite; a program needn't handle non-finite values.
Results may differ from the reference program's by a relative error of at most 0.023.
Values may be sent and summed in bfloat16 or wider, within the bound.
A program may use at most 192 MiB of HBM per device.

```python
import jax
import jax.numpy as jnp
from jax import lax

D = 5120
HD = 128
FRAME_TOK = 640
HEADS = 32
FRAMES = 8
TOKENS = 5120
REACH = 4


def draw_queries(key, part):
    key = jax.random.fold_in(key, 3)
    return jnp.clip(jax.random.normal(key, (TOKENS, HEADS * HD), jnp.float32), -4.0, 4.0).astype(jnp.bfloat16)


def draw_keys(key, part):
    key = jax.random.fold_in(key, 7)
    return jnp.clip(jax.random.normal(key, (TOKENS, HEADS * HD), jnp.float32), -4.0, 4.0).astype(jnp.bfloat16)


def draw_frame_map(key, part):
    key = jax.random.fold_in(key, 11)
    return jax.random.permutation(key, jnp.arange(FRAMES, dtype=jnp.int32)).astype(jnp.int32)


def draw_band(key, part):
    key = jax.random.fold_in(key, 5)
    frame_ids = jnp.arange(FRAMES, dtype=jnp.int32)
    distance = jnp.abs(frame_ids[:, None] - frame_ids[None, :])
    level = jnp.zeros((FRAMES, FRAMES), jnp.int32)
    for power in range(16):
        level = level + (distance > 2 ** power).astype(jnp.int32)
    upper = jnp.right_shift(jnp.full((FRAMES, FRAMES), FRAME_TOK, jnp.int32), level)
    lower = upper // 2
    widths = jax.random.randint(key, (FRAMES, FRAMES), lower, upper + 1, dtype=jnp.int32)
    widths = jnp.where(distance > REACH, -1, widths)
    return jnp.where(distance == 0, FRAME_TOK, widths).astype(jnp.int32)


def spiked(entries, rng, source, target, parts, factor):
    owner, partner = [(jnp.arange(entries.shape[axis_at]) // (entries.shape[axis_at] // parts)).reshape([-1 if axis == axis_at else 1 for axis in range(entries.ndim)]) for axis_at in (source, target)]
    chosen = jax.random.permutation(rng, parts)[partner]
    strong = (owner == chosen) | (owner == (partner + parts // 2) % parts)
    return jnp.where(strong, factor * entries, entries)


def block_scale(rng, extent, pieces, smallest, top_value):
    gain, own = 1.0, jax.random.fold_in(rng, 6)
    for dim, blocks in pieces:
        heights = jnp.exp(jax.random.uniform(jax.random.fold_in(own, dim), (blocks,), jnp.float32, smallest / len(pieces), top_value / len(pieces)))
        gain = gain * jnp.repeat(heights, extent[dim] // blocks).reshape([-1 if axis == dim else 1 for axis in range(len(extent))])
    return gain


def noise(rng, shape, spread, bound, cuts=(), kind=jnp.bfloat16):
    factor_of = block_scale(rng, shape, cuts, -0.22, 0.18) if cuts else 1.0
    drawn = jax.random.normal(rng, shape, jnp.float32) * spread * factor_of
    return jnp.minimum(jnp.maximum(drawn, -bound), bound).astype(kind)


def bell_draw_with(own_key, dims, scale, most, cuts, heavy, kind=jnp.bfloat16):
    values = scale * jax.random.normal(own_key, dims, jnp.float32)
    if cuts:
        values = values * block_scale(own_key, dims, cuts, -0.22, 0.18)
    return jnp.clip(spiked(values, jax.random.fold_in(own_key, 3), *heavy), -most, most).astype(kind)


def setup_inputs(seed: int = 0) -> dict:
    key_of = jax.random.split(jax.random.key(seed), 11)
    queries = draw_queries(jax.random.fold_in(key_of[10], 71), 0)
    keys = draw_keys(jax.random.fold_in(key_of[10], 71), 0)
    values = noise(key_of[2], (TOKENS, HEADS * HD), 1.0, 6.0, ((0, 8), (1, 16)))
    grad_out = noise(key_of[3], (TOKENS, D), 3.0, 18.0, ((0, 8), (1, 16)))
    frame_map = draw_frame_map(jax.random.fold_in(key_of[10], 71), 0)
    band = draw_band(jax.random.fold_in(key_of[10], 71), 0)
    w_query = bell_draw_with(key_of[6], (D, HEADS * HD), HD ** -0.5, 0.75, ((1, 16),), (1, 0, 16, 2.0))
    w_key = bell_draw_with(key_of[7], (D, HEADS * HD), HD ** -0.5, 0.75, ((1, 16),), (1, 0, 16, 2.0))
    w_value = bell_draw_with(key_of[8], (D, HEADS * HD), HD ** -0.5, 0.75, ((1, 16),), (1, 0, 16, 2.0))
    w_out = noise(key_of[9], (HEADS * HD, D), (HEADS * HD) ** -0.5, 0.09375, ((0, 16),))
    return {"queries": queries, "keys": keys, "values": values, "grad_out": grad_out, "frame_map": frame_map, "band": band, "w_query": w_query, "w_key": w_key, "w_value": w_value, "w_out": w_out}


masked_score = -1.0e30


def reference(queries, keys, values, grad_out, frame_map, band, w_query, w_key, w_value, w_out):
    score_scale = HD ** -0.5
    positions = jnp.arange(TOKENS, dtype=jnp.int32)
    token_frame = frame_map[positions // FRAME_TOK]
    inner = positions % FRAME_TOK
    widths = band[token_frame[:, None], token_frame[None, :]]
    allowed = jnp.abs(inner[:, None] - inner[None, :]) <= widths
    d_output = jnp.dot(grad_out, w_out.T, preferred_element_type=jnp.float32).astype(jnp.bfloat16)

    def split_heads(array):
        return array.reshape(TOKENS, HEADS, HD).transpose(1, 0, 2)

    def merge_heads(array):
        return array.transpose(1, 0, 2).reshape(TOKENS, HEADS * HD)

    def one_head(operands):
        query, key_rows, value_rows, grad_rows = operands
        scores = jnp.dot(query, key_rows.T, preferred_element_type=jnp.float32) * score_scale
        scores = jnp.where(allowed, scores, masked_score)
        row_max = jnp.max(scores, axis=1)
        shifted = jnp.where(allowed, jnp.exp(scores - row_max[:, None]), 0.0)
        row_total = jnp.sum(shifted, axis=1)
        attended = jnp.dot(shifted.astype(jnp.bfloat16), value_rows, preferred_element_type=jnp.float32) / row_total[:, None]
        row_dot = jnp.sum(grad_rows.astype(jnp.float32) * attended, axis=1)
        log_total = row_max + jnp.log(row_total)
        probs = jnp.where(allowed, jnp.exp(scores - log_total[:, None]), 0.0)
        grad_value = jnp.dot(probs.astype(jnp.bfloat16).T, grad_rows, preferred_element_type=jnp.float32)
        grad_probs = jnp.dot(grad_rows, value_rows.T, preferred_element_type=jnp.float32)
        grad_scores = (probs * (grad_probs - row_dot[:, None])).astype(jnp.bfloat16)
        grad_query = jnp.dot(grad_scores, key_rows, preferred_element_type=jnp.float32) * score_scale
        grad_key = jnp.dot(grad_scores.T, query, preferred_element_type=jnp.float32) * score_scale
        return grad_query.astype(jnp.bfloat16), grad_key.astype(jnp.bfloat16), grad_value.astype(jnp.bfloat16)

    grad_query, grad_key, grad_value = lax.map(one_head, (split_heads(queries), split_heads(keys), split_heads(values), split_heads(d_output)))
    total = jnp.dot(w_query, merge_heads(grad_query).T, preferred_element_type=jnp.float32)
    total = total + jnp.dot(w_key, merge_heads(grad_key).T, preferred_element_type=jnp.float32)
    total = total + jnp.dot(w_value, merge_heads(grad_value).T, preferred_element_type=jnp.float32)
    return total.astype(jnp.bfloat16)
```

```python
import functools

import jax
import jax.numpy as jnp
from jax import lax
from jax.experimental import pallas as pl
from jax.experimental.pallas import tpu as pltpu
from jax.sharding import PartitionSpec as P

HD = 128
F = 640
MESH = pl.DeviceIdType.MESH
NT = (((1,), (1,)), ((), ()))
masked_score = -1e30


def dot(a, b):
    return jnp.dot(a, b, preferred_element_type=jnp.float32)


def dot_nt(a, b):
    return lax.dot_general(a, b, NT, preferred_element_type=jnp.float32)


def ring(position, step):
    return lax.rem(position + step + 4, 4)


def scatter_kernel(
    wq_hbm, wk_hbm, wv_hbm, gq_ref, gk_ref, gv_ref, out_ref,
    wq, wk, wv, gt, part, out1, in1, out2, in2, load_sem, s1, r1, s2, r2,
):
    g = lax.axis_index("tensor")
    z, x = g // 4, g % 4

    def block(half, d, e):
        zz = ring(z, d * (1 - half) + e * half)
        xx = ring(x, d * half + e * (1 - half))
        return zz * 4 + xx

    loads = [
        pltpu.make_async_copy(src, dst, load_sem.at[n])
        for n, (src, dst) in enumerate(((wq_hbm, wq), (wk_hbm, wk), (wv_hbm, wv)))
    ]
    for load in loads:
        load.start()
    barrier = pltpu.get_barrier_semaphore()
    for half in (0, 1):
        for step in (1, -1):
            pl.semaphore_signal(
                barrier, inc=1, device_id={"tensor": block(half, step, 0)}, device_id_type=MESH
            )
    for n, ref in enumerate((gq_ref, gk_ref, gv_ref)):
        gt[pl.ds(n * 256, 256), :] = ref[...].astype(jnp.float32).T.astype(jnp.bfloat16)
    for load in loads:
        load.wait()
    pl.semaphore_wait(barrier, 4)

    def first(m, half, step):
        return pltpu.make_async_remote_copy(
            src_ref=out1.at[m], dst_ref=in1.at[m], send_sem=s1.at[m], recv_sem=r1.at[m],
            device_id={"tensor": block(half, step, 0)}, device_id_type=MESH,
        )

    def second(m, half, step):
        return pltpu.make_async_remote_copy(
            src_ref=out2.at[m], dst_ref=in2.at[m], send_sem=s2.at[m], recv_sem=r2.at[m],
            device_id={"tensor": block(half, 0, step)}, device_id_type=MESH,
        )

    def body(i, carry):
        t, half = i // 2, i % 2
        group, u = t // 4, t % 4
        odd = u % 2
        own_only = (group % 2) * (1 - group // 2)
        par = (odd + own_only) % 2
        e = par * (1 - u // 2) + (1 - par) * (2 + u // 2)
        near = ((group + 1) // 2) % 2
        d = near * (1 + 2 * odd) + (1 - near) * (2 - 2 * (group // 3))
        row = pl.multiple_of(block(half, d, e) * 320 + half * 160, 16)
        rows = pl.ds(row, 160)
        part[...] = (
            dot(wq[rows, :], gt[0:256, :])
            + dot(wk[rows, :], gt[256:512, :])
            + dot(wv[rows, :], gt[512:768, :])
        )
        step = 1 - 2 * odd

        @pl.when(group < 2)
        def _():
            m = half * 12 + t
            out1[m] = part[...].astype(jnp.bfloat16)
            first(m, half, step).start()

        @pl.when(group == 2)
        def _():
            m = half * 12 + t
            first(m - 8, half, step).wait_recv()
            out1[m] = (part[...] + in1[m - 8].astype(jnp.float32)).astype(jnp.bfloat16)
            first(m, half, step).start()

        @pl.when(group == 3)
        def _():
            up = half * 12 + 8 - 4 * odd + 2 * (u // 2)
            down = half * 12 + 5 + 4 * odd + 2 * (u // 2)
            first(up, half, 1).wait_recv()
            first(down, half, 1).wait_recv()
            part[...] += in1[up].astype(jnp.float32) + in1[down].astype(jnp.float32)
            m = half * 6

            @pl.when(u == 0)
            def _():
                out2[m] = part[0:80, :].astype(jnp.bfloat16)
                second(m, half, 1).start()
                out2[m + 1] = part[80:160, :].astype(jnp.bfloat16)
                second(m + 1, half, -1).start()

            @pl.when(u == 1)
            def _():
                out2[m + 2] = part[80:160, :].astype(jnp.bfloat16)
                second(m + 2, half, 1).start()
                second(m, half, 1).wait_recv()
                out2[m + 3] = (part[0:80, :] + in2[m].astype(jnp.float32)).astype(jnp.bfloat16)
                second(m + 3, half, 1).start()

            @pl.when(u == 2)
            def _():
                out2[m + 4] = part[0:80, :].astype(jnp.bfloat16)
                second(m + 4, half, -1).start()
                second(m + 1, half, 1).wait_recv()
                out2[m + 5] = (part[80:160, :] + in2[m + 1].astype(jnp.float32)).astype(jnp.bfloat16)
                second(m + 5, half, -1).start()

            @pl.when(u == 3)
            def _():
                for n in (2, 3, 4, 5):
                    second(m + n, half, 1).wait_recv()
                at = pl.multiple_of(half * 160, 16)
                low = in2[m + 3].astype(jnp.float32) + in2[m + 4].astype(jnp.float32)
                high = in2[m + 2].astype(jnp.float32) + in2[m + 5].astype(jnp.float32)
                out_ref[pl.ds(at, 80), :] = (part[0:80, :] + low).astype(jnp.bfloat16)
                out_ref[pl.ds(at + 80, 80), :] = (part[80:160, :] + high).astype(jnp.bfloat16)

        return carry

    lax.fori_loop(0, 32, body, 0)

    def drain1(m, carry):
        first(m, 0, 1).wait_send()
        return carry

    def drain2(m, carry):
        second(m, 0, 1).wait_send()
        return carry

    lax.fori_loop(0, 24, drain1, 0)
    lax.fori_loop(0, 12, drain2, 0)


def weigh_and_scatter(w_query, w_key, w_value, gq, gk, gv):
    vmem = pl.BlockSpec(memory_space=pltpu.VMEM)
    hbm = pl.BlockSpec(memory_space=pl.ANY)
    weight = pltpu.VMEM((5120, 256), jnp.bfloat16)
    return pl.pallas_call(
        scatter_kernel,
        out_shape=jax.ShapeDtypeStruct((320, F), jnp.bfloat16),
        in_specs=[hbm] * 3 + [vmem] * 3,
        out_specs=vmem,
        scratch_shapes=[
            weight, weight, weight,
            pltpu.VMEM((768, F), jnp.bfloat16),
            pltpu.VMEM((160, F), jnp.float32),
            pltpu.VMEM((24, 160, F), jnp.bfloat16),
            pltpu.VMEM((24, 160, F), jnp.bfloat16),
            pltpu.VMEM((12, 80, F), jnp.bfloat16),
            pltpu.VMEM((12, 80, F), jnp.bfloat16),
            pltpu.SemaphoreType.DMA((3,)),
            pltpu.SemaphoreType.DMA((24,)),
            pltpu.SemaphoreType.DMA((24,)),
            pltpu.SemaphoreType.DMA((12,)),
            pltpu.SemaphoreType.DMA((12,)),
        ],
        compiler_params=pltpu.CompilerParams(
            collective_id=1, has_side_effects=True, vmem_limit_bytes=48 * 1024 * 1024
        ),
        cost_estimate=pl.CostEstimate(flops=5_033_164_800, bytes_accessed=9_000_000, transcendentals=0),
    )(w_query, w_key, w_value, gq, gk, gv)


SCALE = HD ** -0.5
POWER = SCALE * 1.4426950408889634
ARRAYS = 6


def attend_kernel(
    frame_map, band, go_hbm, wo_hbm, q_hbm, k_hbm, v_hbm, gq_out, gk_out, gv_out,
    go, wo, wt, qall, kall, vall, dall, logs, dots, p, pt, sbuf, dist, dacc, att, gq, gk, gv,
    inv_total, row_dot, load_sem, zs, zr, ys, yr,
):
    g = lax.axis_index("tensor")
    z, x = g // 4, g % 4
    me = lax.axis_index("tm")
    y, core = me // 2, me % 2
    my_frame = frame_map[me]

    loads = [
        pltpu.make_async_copy(src, dst, load_sem.at[n])
        for n, (src, dst) in enumerate((
            (go_hbm, go.at[g]), (k_hbm, kall.at[me]), (q_hbm, qall.at[me]), (v_hbm, vall.at[me]),
            (wo_hbm, wo),
        ))
    ]
    for load in loads:
        load.start()

    def block(half, d, e):
        zz = ring(z, d * half + e * (1 - half))
        xx = ring(x, d * (1 - half) + e * half)
        return zz * 4 + xx

    def piece(half, j, kind):
        start = half * 320 + (160 if kind == 3 else 0)
        return go.at[j, pl.ds(pl.multiple_of(start, 32), 320 if kind < 2 else 160)]

    def tensor_copy(half, m, j, kind, target):
        ref = piece(half, j, kind)
        n = half * 20 + m
        return pltpu.make_async_remote_copy(
            src_ref=ref, dst_ref=ref, send_sem=zs.at[n], recv_sem=zr.at[n],
            device_id={"tensor": target}, device_id_type=MESH,
        )

    def both(step):
        def one(half, carry):
            step(half)
            return carry

        lax.fori_loop(0, 2, one, 0)

    def spread(half, index, d):
        j = block(half, d, 0)
        m = 4 + 4 * index
        tensor_copy(half, m, j, 0, block(half, 0, 1)).start()
        tensor_copy(half, m + 1, j, 1, block(half, 0, -1)).start()

    def tensor_start(half):
        tensor_copy(half, 0, g, 0, block(half, 1, 0)).start()
        tensor_copy(half, 1, g, 1, block(half, -1, 0)).start()
        spread(half, 0, 0)

    def tensor_near(half):
        j = block(half, -1, 0)
        tensor_copy(half, 0, j, 0, g).wait_recv()
        tensor_copy(half, 2, j, 2, block(half, 1, 0)).start()
        spread(half, 1, -1)
        j = block(half, 1, 0)
        tensor_copy(half, 1, j, 1, g).wait_recv()
        tensor_copy(half, 3, j, 3, block(half, -1, 0)).start()
        spread(half, 2, 1)

    def tensor_far(half):
        j = block(half, 2, 0)
        tensor_copy(half, 2, j, 2, g).wait_recv()
        tensor_copy(half, 3, j, 3, g).wait_recv()
        spread(half, 3, 2)

    offsets = (0, -1, 1, 2)

    def forward(index):
        def step(half):
            m, d = 4 + 4 * index, offsets[index]
            j = block(half, d, -1)
            tensor_copy(half, m, j, 0, g).wait_recv()
            tensor_copy(half, m + 2, j, 2, block(half, 0, 1)).start()
            j = block(half, d, 1)
            tensor_copy(half, m + 1, j, 1, g).wait_recv()
            tensor_copy(half, m + 3, j, 3, block(half, 0, -1)).start()

        both(step)

    def finish(index):
        def step(half):
            m, d = 4 + 4 * index, offsets[index]
            j = block(half, d, 2)
            tensor_copy(half, m + 2, j, 2, g).wait_recv()
            tensor_copy(half, m + 3, j, 3, g).wait_recv()

        both(step)

        def add(i, carry):
            half = i // 4
            j = block(half, offsets[index], i % 4)
            rows = pl.ds(pl.multiple_of(half * 320, 64), 320)
            dacc[rows, :] += dot_nt(go[j, rows, :], wt[j])
            return carry

        lax.fori_loop(0, 8, add, 0)

    sibling = y * 2 + 1 - core

    def at_y(step):
        return ring(y, step) * 2 + core

    def tm_copy(array, ref, m, slot, target):
        half = ref.shape[1] // 2
        part = ref.at[slot]
        if m in (2, 3):
            part = ref.at[slot, pl.ds((m - 2) * half, half)]
        n = array * 8 + m
        return pltpu.make_async_remote_copy(
            src_ref=part, dst_ref=part, send_sem=ys.at[n], recv_sem=yr.at[n],
            device_id={"tm": target}, device_id_type=MESH,
        )

    def tm_start(array, ref):
        tm_copy(array, ref, 0, me, at_y(1)).start()
        tm_copy(array, ref, 1, me, at_y(-1)).start()
        tm_copy(array, ref, 4, me, sibling).start()

    def tm_near(array, ref):
        tm_copy(array, ref, 0, at_y(-1), me).wait_recv()
        tm_copy(array, ref, 2, at_y(-1), at_y(1)).start()
        tm_copy(array, ref, 5, at_y(-1), sibling).start()
        tm_copy(array, ref, 1, at_y(1), me).wait_recv()
        tm_copy(array, ref, 3, at_y(1), at_y(-1)).start()
        tm_copy(array, ref, 6, at_y(1), sibling).start()

    def tm_far(array, ref):
        tm_copy(array, ref, 2, at_y(2), me).wait_recv()
        tm_copy(array, ref, 3, at_y(2), me).wait_recv()
        tm_copy(array, ref, 7, at_y(2), sibling).start()

    def tm_finish(array, ref):
        for m, step in ((4, 0), (5, -1), (6, 1), (7, 2)):
            slot = ring(y, step) * 2 + 1 - core
            tm_copy(array, ref, m, slot, me).wait_recv()

    keys, queries, values, grads, totals, products = range(ARRAYS)

    def lanes(h):
        return pl.ds(pl.multiple_of(h * HD, HD), HD)

    def stat_row(ref, s, h):
        return ref[s, pl.ds(pl.multiple_of(h * 8, 8), 8), :][0:1, :]

    def to_row(ref, h, column):
        wide = jnp.broadcast_to(column, (F, HD))
        ref[me, h * 8:(h + 1) * 8, :] = wide.T[0:8, :]

    def softmax(i, carry):
        h = i // 2
        rows = pl.ds(pl.multiple_of((i % 2) * 320, 64), 320)
        query = qall[me, rows, lanes(h)]

        def score(s, top):
            scores = dot_nt(query, kall[s, :, lanes(h)])
            width = band[my_frame, frame_map[s]]
            scores = jnp.where(dist[rows, :] <= width, scores, masked_score)
            sbuf[s] = scores
            for n in range(5):
                top = jnp.maximum(top, scores[:, n * 128:(n + 1) * 128])
            return top

        top = lax.fori_loop(0, 8, score, jnp.full((320, 128), masked_score, jnp.float32))
        top = jnp.max(top, axis=1, keepdims=True) * POWER

        def weigh(s, total):
            shifted = jnp.exp2(sbuf[s] * POWER - top)
            p[h, s, rows, :] = shifted.astype(jnp.bfloat16)
            for n in range(5):
                total = total + shifted[:, n * 128:(n + 1) * 128]
            return total

        total = lax.fori_loop(0, 8, weigh, jnp.zeros((320, 128), jnp.float32))
        total = jnp.sum(total, axis=1, keepdims=True)
        inv_total[h, rows, :] = jnp.broadcast_to(1.0 / total, (320, HD))
        row_dot[h, rows, :] = jnp.broadcast_to(top + jnp.log2(total), (320, HD))
        return carry

    def key_side(i, carry):
        h, s = i // 16, (i // 2) % 8
        rows = pl.ds(pl.multiple_of((i % 2) * 320, 64), 320)
        scores = dot_nt(kall[me, rows, lanes(h)], qall[s, :, lanes(h)])
        width = band[frame_map[s], my_frame]
        power = jnp.where(
            dist[rows, :] <= width, scores * POWER - stat_row(logs, s, h), masked_score
        )
        pt[h, s, rows, :] = jnp.exp2(power).astype(jnp.bfloat16)
        return carry

    def attend(i, carry):
        h, s = i // 8, i % 8
        att[h] += dot(p[h, s], vall[s, :, lanes(h)])
        return carry

    def query_grad(i, carry):
        h, s = i // 16, (i // 2) % 8
        rows = pl.ds(pl.multiple_of((i % 2) * 320, 64), 320)
        grad = dot_nt(dall[me, rows, lanes(h)], vall[s, :, lanes(h)])
        weight = p[h, s, rows, :].astype(jnp.float32)
        grad = weight * ((grad - row_dot[h, rows, 0:1]) * inv_total[h, rows, 0:1])
        gq[h, rows, :] += dot(grad.astype(jnp.bfloat16), kall[s, :, lanes(h)])
        return carry

    def key_grad(i, carry):
        h, s = i // 16, (i // 2) % 8
        rows = pl.ds(pl.multiple_of((i % 2) * 320, 64), 320)
        grad_rows = dall[s, :, lanes(h)]
        weight = pt[h, s, rows, :]
        grad = dot_nt(vall[me, rows, lanes(h)], grad_rows)
        grad = weight.astype(jnp.float32) * (grad - stat_row(dots, s, h))
        gv[h, rows, :] += dot(weight, grad_rows)
        gk[h, rows, :] += dot(grad.astype(jnp.bfloat16), qall[s, :, lanes(h)])
        return carry

    barrier = pltpu.get_barrier_semaphore()
    for half in (0, 1):
        for step in (1, -1):
            pl.semaphore_signal(
                barrier, inc=1, device_id={"tensor": block(half, step, 0)}, device_id_type=MESH
            )
    for target in (at_y(1), at_y(-1), sibling):
        pl.semaphore_signal(barrier, inc=1, device_id={"tm": target}, device_id_type=MESH)
    loads[0].wait()
    loads[1].wait()
    pl.semaphore_wait(barrier, 7)
    both(tensor_start)
    tm_start(keys, kall)
    across = lax.broadcasted_iota(jnp.int32, (F, F), 0) - lax.broadcasted_iota(jnp.int32, (F, F), 1)
    dist[...] = jnp.abs(across)
    for ref in (dacc, att, gq, gk, gv):
        ref[...] = jnp.zeros_like(ref)
    loads[2].wait()
    loads[3].wait()
    loads[4].wait()
    both(tensor_near)
    tm_near(keys, kall)
    tm_start(queries, qall)
    for j in range(16):
        wt[j] = wo[:, j * 320:(j + 1) * 320]
    both(tensor_far)
    tm_far(keys, kall)
    tm_finish(keys, kall)
    lax.fori_loop(0, 1, softmax, 0)
    forward(0)
    tm_near(queries, qall)
    tm_start(values, vall)
    lax.fori_loop(1, 3, softmax, 0)
    forward(1)
    tm_far(queries, qall)
    lax.fori_loop(3, 4, softmax, 0)
    for h in (0, 1):
        to_row(logs, h, row_dot[h, :, 0:1])
    tm_start(totals, logs)
    forward(2)
    tm_near(values, vall)
    tm_near(totals, logs)
    tm_finish(queries, qall)
    finish(0)
    tm_far(totals, logs)
    tm_finish(totals, logs)
    lax.fori_loop(0, 16, key_side, 0)
    forward(3)
    tm_far(values, vall)
    finish(1)
    lax.fori_loop(16, 32, key_side, 0)
    tm_finish(values, vall)
    lax.fori_loop(0, 16, attend, 0)
    finish(2)
    finish(3)

    dall[me] = dacc[...].astype(jnp.bfloat16)
    tm_start(grads, dall)
    for h in (0, 1):
        grad_rows = dall[me, :, h * HD:(h + 1) * HD].astype(jnp.float32)
        column = jnp.sum(grad_rows * att[h], axis=1, keepdims=True) * inv_total[h, :, 0:1]
        row_dot[h] = jnp.broadcast_to(column, (F, HD))
        to_row(dots, h, column)
    tm_start(products, dots)
    lax.fori_loop(0, 20, query_grad, 0)
    tm_near(grads, dall)
    tm_near(products, dots)
    lax.fori_loop(20, 32, query_grad, 0)
    tm_far(grads, dall)
    tm_far(products, dots)
    for h in (0, 1):
        gq_out[:, h * HD:(h + 1) * HD] = (gq[h] * SCALE).astype(jnp.bfloat16)
    tm_finish(grads, dall)
    tm_finish(products, dots)
    lax.fori_loop(0, 32, key_grad, 0)
    for h in (0, 1):
        gk_out[:, h * HD:(h + 1) * HD] = (gk[h] * SCALE).astype(jnp.bfloat16)
        gv_out[:, h * HD:(h + 1) * HD] = gv[h].astype(jnp.bfloat16)

    def drain(half):
        def one(i, carry):
            for kind in range(4):
                tensor_copy(half, 4 * i + kind, g, kind, g).wait_send()
            return carry

        lax.fori_loop(0, 5, one, 0)

    both(drain)
    gathered = (kall, qall, vall, dall, logs, dots)
    for array, ref in enumerate(gathered):
        for m in range(8):
            tm_copy(array, ref, m, me, me).wait_send()


def attend(frame_map, band, grad_out, w_out, queries, keys, values):
    vmem = pl.BlockSpec(memory_space=pltpu.VMEM)
    hbm = pl.BlockSpec(memory_space=pl.ANY)
    smem = pl.BlockSpec(memory_space=pltpu.SMEM)
    grad = jax.ShapeDtypeStruct((F, 256), jnp.bfloat16)
    gathered = pltpu.VMEM((8, F, 256), jnp.bfloat16)
    stats = pltpu.VMEM((8, 16, F), jnp.float32)
    pairs = pltpu.VMEM((2, 8, F, F), jnp.bfloat16)
    heads = pltpu.VMEM((2, F, HD), jnp.float32)
    return pl.pallas_call(
        attend_kernel,
        out_shape=(grad, grad, grad),
        in_specs=[smem] * 2 + [hbm] * 5,
        out_specs=(vmem, vmem, vmem),
        scratch_shapes=[
            pltpu.VMEM((16, F, 320), jnp.bfloat16),
            pltpu.VMEM((256, 5120), jnp.bfloat16),
            pltpu.VMEM((16, 256, 320), jnp.bfloat16),
            gathered, gathered, gathered, gathered,
            stats, stats,
            pairs, pairs,
            pltpu.VMEM((8, 320, F), jnp.float32),
            pltpu.VMEM((F, F), jnp.int32),
            pltpu.VMEM((F, 256), jnp.float32),
            heads, heads, heads, heads, heads, heads,
            pltpu.SemaphoreType.DMA((5,)),
            pltpu.SemaphoreType.DMA((40,)),
            pltpu.SemaphoreType.DMA((40,)),
            pltpu.SemaphoreType.DMA((8 * ARRAYS,)),
            pltpu.SemaphoreType.DMA((8 * ARRAYS,)),
        ],
        compiler_params=pltpu.CompilerParams(
            collective_id=0, has_side_effects=True, vmem_limit_bytes=64 * 1024 * 1024
        ),
        cost_estimate=pl.CostEstimate(
            flops=16_000_000_000, bytes_accessed=6_000_000, transcendentals=13_000_000
        ),
    )(frame_map, band, grad_out, w_out, queries, keys, values)


def per_device(queries, keys, values, grad_out, frame_map, band, w_query, w_key, w_value, w_out):
    gq, gk, gv = attend(frame_map, band, grad_out, w_out, queries, keys, values)
    return weigh_and_scatter(w_query, w_key, w_value, gq, gk, gv)


def solution(mesh):
    placed = (
        P("tm", "tensor"),
        P("tm", "tensor"),
        P("tm", "tensor"),
        P("tm", "tensor"),
        P(),
        P(),
        P(None, "tensor"),
        P(None, "tensor"),
        P(None, "tensor"),
        P("tensor", None),
    )
    return jax.shard_map(
        per_device, mesh=mesh, in_specs=placed, out_specs=P("tensor", "tm"), check_vma=False
    )
```

```python
import jax
import jax.numpy as jnp
from jax import lax
from jax.experimental import pallas as pl
from jax.experimental.pallas import tpu as pltpu
from jax.sharding import PartitionSpec as P

HD = 128
F = 640
SCALE = HD ** -0.5
POWER = SCALE * 1.4426950408889634
ARRAYS = 6
MESH = pl.DeviceIdType.MESH
NT = (((1,), (1,)), ((), ()))
masked_score = -1e30


def dot(a, b):
    return jnp.dot(a, b, preferred_element_type=jnp.float32)


def dot_nt(a, b):
    return lax.dot_general(a, b, NT, preferred_element_type=jnp.float32)


def ring(position, step):
    return lax.rem(position + step + 4, 4)


def low(value):
    return value.astype(jnp.bfloat16)


def wide(value):
    return value.astype(jnp.float32)


def kernel(
    frame_map, band, go_hbm, wo_hbm, q_hbm, k_hbm, v_hbm, wq_hbm, wk_hbm, wv_hbm, out_ref,
    go, wo, wq, kall, qall, vall, dall, vown, logs, dots, p, pt, dist, dacc, att, gq, gk, gv,
    tops, sums, row_dot, part, in1, in2,
    load_sem, zs, zr, ys, yr, s1, r1, s2, r2,
):
    g = lax.axis_index("tensor")
    z, x = g // 4, g % 4
    me = lax.axis_index("tm")
    y, core = me // 2, me % 2
    my_frame = frame_map[me]

    def slot_rows(s):
        return pl.ds(pl.multiple_of(s * F, F), F)

    mine = slot_rows(me)

    def load(n, src, dst):
        return pltpu.make_async_copy(src, dst, load_sem.at[n])

    loads = [
        load(0, go_hbm, go.at[pl.ds(pl.multiple_of(g * 320, 320), 320)]),
        load(1, k_hbm, kall.at[mine]),
        load(2, q_hbm, qall.at[mine]),
        load(3, v_hbm, vall.at[mine]),
        load(4, v_hbm, vown),
        load(5, wo_hbm, wo),
        load(6, wq_hbm, wq),
    ]
    for item in loads:
        item.start()

    def block(half, d, e):
        zz = ring(z, d * half + e * (1 - half))
        xx = ring(x, d * (1 - half) + e * half)
        return zz * 4 + xx

    def tensor_copy(half, m, j, kind, target):
        start = j * 320 + half * 160 + (80 if kind == 3 else 0)
        ref = go.at[pl.ds(pl.multiple_of(start, 16), 160 if kind < 2 else 80)]
        n = half * 20 + m
        return pltpu.make_async_remote_copy(
            src_ref=ref, dst_ref=ref, send_sem=zs.at[n], recv_sem=zr.at[n],
            device_id={"tensor": target}, device_id_type=MESH,
        )

    def both(step):
        def one(half, carry):
            step(half)
            return carry

        lax.fori_loop(0, 2, one, 0)

    def spread(half, index, d):
        j = block(half, d, 0)
        m = 4 + 4 * index
        tensor_copy(half, m, j, 0, block(half, 0, 1)).start()
        tensor_copy(half, m + 1, j, 1, block(half, 0, -1)).start()

    def tensor_start(half):
        tensor_copy(half, 0, g, 0, block(half, 1, 0)).start()
        tensor_copy(half, 1, g, 1, block(half, -1, 0)).start()

    def tensor_next(half):
        spread(half, 0, 0)

    def tensor_near(half):
        j = block(half, -1, 0)
        tensor_copy(half, 0, j, 0, g).wait_recv()
        tensor_copy(half, 2, j, 2, block(half, 1, 0)).start()
        spread(half, 1, -1)
        j = block(half, 1, 0)
        tensor_copy(half, 1, j, 1, g).wait_recv()
        tensor_copy(half, 3, j, 3, block(half, -1, 0)).start()
        spread(half, 2, 1)

    def tensor_far(half):
        j = block(half, 2, 0)
        tensor_copy(half, 2, j, 2, g).wait_recv()
        tensor_copy(half, 3, j, 3, g).wait_recv()
        spread(half, 3, 2)

    offsets = (0, -1, 1, 2)

    def forward(index):
        def step(half):
            m, d = 4 + 4 * index, offsets[index]
            j = block(half, d, -1)
            tensor_copy(half, m, j, 0, g).wait_recv()
            tensor_copy(half, m + 2, j, 2, block(half, 0, 1)).start()
            j = block(half, d, 1)
            tensor_copy(half, m + 1, j, 1, g).wait_recv()
            tensor_copy(half, m + 3, j, 3, block(half, 0, -1)).start()

        both(step)

    def finish(half, index):
        m, d = 4 + 4 * index, offsets[index]
        j = block(half, d, 2)
        tensor_copy(half, m + 2, j, 2, g).wait_recv()
        tensor_copy(half, m + 3, j, 3, g).wait_recv()

    def add_row(index):
        cols = pl.ds(pl.multiple_of(ring(z, offsets[index]) * 1280, 1280), 1280)
        dacc[...] += dot(wo[:, cols], go[cols, :])

    sibling = y * 2 + 1 - core

    def at_y(step):
        return ring(y, step) * 2 + core

    class Gather:
        def __init__(self, array, ref, rows):
            self.array, self.ref, self.rows = array, ref, rows

        def copy(self, m, slot, target):
            start, count = slot * self.rows, self.rows
            if m in (2, 3):
                count = self.rows // 2
                start = start + (m - 2) * count
            ref = self.ref.at[pl.ds(pl.multiple_of(start, count), count)]
            n = self.array * 8 + m
            return pltpu.make_async_remote_copy(
                src_ref=ref, dst_ref=ref, send_sem=ys.at[n], recv_sem=yr.at[n],
                device_id={"tm": target}, device_id_type=MESH,
            )

        def start(self):
            self.copy(0, me, at_y(1)).start()
            self.copy(1, me, at_y(-1)).start()
            self.copy(4, me, sibling).start()

        def near(self):
            self.copy(0, at_y(-1), me).wait_recv()
            self.copy(2, at_y(-1), at_y(1)).start()
            self.copy(5, at_y(-1), sibling).start()
            self.copy(1, at_y(1), me).wait_recv()
            self.copy(3, at_y(1), at_y(-1)).start()
            self.copy(6, at_y(1), sibling).start()

        def far(self):
            self.copy(2, at_y(2), me).wait_recv()
            self.copy(3, at_y(2), me).wait_recv()
            self.copy(7, at_y(2), sibling).start()

        def from_sibling(self, *messages):
            for m in messages:
                slot = ring(y, (0, -1, 1, 2)[m - 4]) * 2 + 1 - core
                self.copy(m, slot, me).wait_recv()

        def drain(self):
            for m in range(8):
                self.copy(m, me, me).wait_send()

    keys, queries = Gather(0, kall, F), Gather(1, qall, F)
    values, grads = Gather(2, vall, F), Gather(3, dall, F)
    totals, products = Gather(4, logs, 16), Gather(5, dots, 16)

    def by_arrival(gathers, body, events):
        def step(n, carry):
            ring_at = (n + 2) // 4
            hop = (ring_at % 2) * (2 * (n % 2) - 1) + (ring_at // 2) * 2
            other = (1 - ring_at % 2) * (n % 2) + (ring_at % 2) * (((n + 2) // 2) % 2)
            slot = ring(y, hop) * 2 + (core + other) % 2
            waits = {
                1: lambda item: item.from_sibling(4),
                4: lambda item: item.from_sibling(5, 6),
                6: lambda item: item.far(),
                7: lambda item: item.from_sibling(7),
            }
            for when in range(8):
                if when in waits or when in events:
                    @pl.when(n == when)
                    def _(when=when):
                        if when in events:
                            events[when]()
                        if when in waits:
                            for item in gathers:
                                waits[when](item)

            body(slot)
            return carry

        lax.fori_loop(0, 8, step, 0)

    lane = lax.broadcasted_iota(jnp.int32, (F, HD), 1)

    def head(ref, rows, h):
        return ref[rows, h * HD:(h + 1) * HD]

    def stat_row(ref, s, h):
        return ref[pl.ds(pl.multiple_of(s * 16 + h * 8, 8), 8), :][0:1, :]

    def to_row(ref, h, column):
        rows = pl.ds(pl.multiple_of(me * 16 + h * 8, 8), 8)
        ref[rows, :] = jnp.broadcast_to(column, (F, HD)).T[0:8, :]

    def factor(h, s):
        return jnp.sum(jnp.where(lane == s, sums[h], 0.0), axis=1, keepdims=True)

    def softmax(s):
        width = band[my_frame, frame_map[s]]
        for h in (0, 1):
            scores = dot_nt(head(qall, mine, h), head(kall, slot_rows(s), h))
            scores = jnp.where(dist[...] <= width, scores, masked_score)
            top = jnp.max(scores, axis=1, keepdims=True) * POWER
            shifted = jnp.exp2(scores * POWER - top)
            total = jnp.sum(shifted, axis=1, keepdims=True)
            p[h, s] = low(shifted)
            tops[h] = jnp.where(lane == s, top, tops[h])
            sums[h] = jnp.where(lane == s, total, sums[h])

    def combine():
        for h in (0, 1):
            top = jnp.max(tops[h], axis=1, keepdims=True)
            shares = jnp.exp2(tops[h] - top)
            total = jnp.sum(shares * sums[h], axis=1, keepdims=True)
            sums[h] = shares / total
            to_row(logs, h, top + jnp.log2(total))

    def key_side(s):
        width = band[frame_map[s], my_frame]
        for h in (0, 1):
            scores = dot_nt(head(kall, mine, h), head(qall, slot_rows(s), h))
            power = jnp.where(
                dist[...] <= width, scores * POWER - stat_row(logs, s, h), masked_score
            )
            pt[h, s] = low(jnp.exp2(power))

    def attend(s):
        for h in (0, 1):
            att[h] += factor(h, s) * dot(p[h, s], head(vall, slot_rows(s), h))

    def query_grad(s):
        for h in (0, 1):
            grad = dot_nt(head(dall, mine, h), head(vall, slot_rows(s), h))
            grad = wide(p[h, s]) * ((grad - row_dot[h, :, 0:1]) * factor(h, s))
            gq[h] += dot(low(grad), head(kall, slot_rows(s), h))

    def key_grad(s):
        for h in (0, 1):
            grad_rows = head(dall, slot_rows(s), h)
            weight = pt[h, s]
            grad = dot_nt(head(vown, slice(None), h), grad_rows)
            grad = wide(weight) * (grad - stat_row(dots, s, h))
            gv[h] += dot(weight, grad_rows)
            gk[h] += dot(low(grad), head(qall, slot_rows(s), h))

    barrier = pltpu.get_barrier_semaphore()
    for half in (0, 1):
        for step in (1, -1):
            pl.semaphore_signal(
                barrier, inc=1, device_id={"tensor": block(half, step, 0)}, device_id_type=MESH
            )
    for target in (at_y(1), at_y(-1), sibling):
        pl.semaphore_signal(barrier, inc=1, device_id={"tm": target}, device_id_type=MESH)
    loads[0].wait()
    loads[1].wait()
    pl.semaphore_wait(barrier, 7)
    both(tensor_start)
    keys.start()
    both(tensor_next)
    across = lax.broadcasted_iota(jnp.int32, (F, F), 0) - lax.broadcasted_iota(jnp.int32, (F, F), 1)
    dist[...] = jnp.abs(across)
    for ref in (dacc, att, gq, gk, gv, sums):
        ref[...] = jnp.zeros_like(ref)
    tops[...] = jnp.full_like(tops, masked_score)
    for item in loads[2:]:
        item.wait()

    def keys_near():
        both(tensor_near)
        keys.near()
        queries.start()

    by_arrival(
        (keys,), softmax,
        {2: keys_near, 5: lambda: both(tensor_far), 7: lambda: forward(0)},
    )
    combine()
    totals.start()

    def queries_near():
        queries.near()
        values.start()
        totals.near()

    by_arrival(
        (queries, totals), key_side,
        {2: queries_near, 4: lambda: forward(1), 7: lambda: forward(2)},
    )
    forward(3)

    def values_near():
        values.near()

    by_arrival((values,), attend, {2: values_near})
    for index in range(4):
        finish(0, index)
    for index in range(4):
        finish(1, index)
        add_row(index)
    dall[mine, :] = low(dacc[...].T)
    grads.start()
    for h in (0, 1):
        column = jnp.sum(wide(head(dall, mine, h)) * att[h], axis=1, keepdims=True)
        row_dot[h] = jnp.broadcast_to(column, (F, HD))
        to_row(dots, h, column)
    products.start()

    def query_step(s, carry):
        query_grad(s)

        @pl.when(s == 5)
        def _():
            grads.near()
            products.near()

        return carry

    lax.fori_loop(0, 8, query_step, 0)
    keys.drain()
    values.drain()
    loads = [load(0, wk_hbm, kall), load(1, wv_hbm, vall)]
    for item in loads:
        item.start()
    gt = [p.at[0, n, 0:256] for n in range(3)]

    def to_gt(n, ref, scale):
        for h in (0, 1):
            gt[n][h * HD:(h + 1) * HD, :] = low((ref[h] * scale).T)

    to_gt(0, gq, SCALE)
    by_arrival((grads, products), key_grad, {})
    to_gt(1, gk, SCALE)
    to_gt(2, gv, 1.0)

    def drain(half):
        def one(i, carry):
            for kind in range(4):
                tensor_copy(half, 4 * i + kind, g, kind, g).wait_send()
            return carry

        lax.fori_loop(0, 5, one, 0)

    both(drain)
    for item in loads:
        item.wait()

    def target(half, d, e):
        return block(1 - half, d, e)

    def out_rows(m):
        return pl.ds(pl.multiple_of(m * 160, 32), 160)

    def out_half(m):
        return pl.ds(pl.multiple_of(3840 + m * 80, 16), 80)

    def first(m, half, step):
        return pltpu.make_async_remote_copy(
            src_ref=go.at[out_rows(m)], dst_ref=in1.at[m], send_sem=s1.at[m], recv_sem=r1.at[m],
            device_id={"tensor": target(half, step, 0)}, device_id_type=MESH,
        )

    def second(m, half, step):
        return pltpu.make_async_remote_copy(
            src_ref=go.at[out_half(m)], dst_ref=in2.at[m], send_sem=s2.at[m], recv_sem=r2.at[m],
            device_id={"tensor": target(half, 0, step)}, device_id_type=MESH,
        )

    def body(i, carry):
        t, half = i // 2, i % 2
        group, u = t // 4, t % 4
        odd = u % 2
        own_only = (group % 2) * (1 - group // 2)
        par = (odd + own_only) % 2
        e = par * (1 - u // 2) + (1 - par) * (2 + u // 2)
        near = ((group + 1) // 2) % 2
        d = near * (1 + 2 * odd) + (1 - near) * (2 - 2 * (group // 3))
        rows = pl.ds(pl.multiple_of(target(half, d, e) * 320 + half * 160, 16), 160)
        part[...] = (
            dot(wq[rows, :], gt[0][...]) + dot(kall[rows, :], gt[1][...]) + dot(vall[rows, :], gt[2][...])
        )
        step = 1 - 2 * odd

        @pl.when(group < 2)
        def _():
            m = half * 12 + t
            go[out_rows(m), :] = low(part[...])
            first(m, half, step).start()

        @pl.when(group == 2)
        def _():
            m = half * 12 + t
            first(m - 8, half, step).wait_recv()
            go[out_rows(m), :] = low(part[...] + wide(in1[m - 8]))
            first(m, half, step).start()

        @pl.when(group == 3)
        def _():
            up = half * 12 + 8 - 4 * odd + 2 * (u // 2)
            down = half * 12 + 5 + 4 * odd + 2 * (u // 2)
            first(up, half, 1).wait_recv()
            first(down, half, 1).wait_recv()
            part[...] += wide(in1[up]) + wide(in1[down])
            m = half * 6

            @pl.when(u == 0)
            def _():
                go[out_half(m), :] = low(part[0:80, :])
                second(m, half, 1).start()
                go[out_half(m + 1), :] = low(part[80:160, :])
                second(m + 1, half, -1).start()

            @pl.when(u == 1)
            def _():
                go[out_half(m + 2), :] = low(part[80:160, :])
                second(m + 2, half, 1).start()
                second(m, half, 1).wait_recv()
                go[out_half(m + 3), :] = low(part[0:80, :] + wide(in2[m]))
                second(m + 3, half, 1).start()

            @pl.when(u == 2)
            def _():
                go[out_half(m + 4), :] = low(part[0:80, :])
                second(m + 4, half, -1).start()
                second(m + 1, half, 1).wait_recv()
                go[out_half(m + 5), :] = low(part[80:160, :] + wide(in2[m + 1]))
                second(m + 5, half, -1).start()

            @pl.when(u == 3)
            def _():
                for n in (2, 3, 4, 5):
                    second(m + n, half, 1).wait_recv()
                at = pl.multiple_of(half * 160, 16)
                out_ref[pl.ds(at, 80), :] = low(part[0:80, :] + (wide(in2[m + 3]) + wide(in2[m + 4])))
                out_ref[pl.ds(at + 80, 80), :] = low(
                    part[80:160, :] + (wide(in2[m + 2]) + wide(in2[m + 5]))
                )

        return carry

    lax.fori_loop(0, 32, body, 0)

    def drain1(m, carry):
        first(m, 0, 1).wait_send()
        return carry

    def drain2(m, carry):
        second(m, 0, 1).wait_send()
        return carry

    lax.fori_loop(0, 24, drain1, 0)
    lax.fori_loop(0, 12, drain2, 0)
    for item in (queries, grads, totals, products):
        item.drain()


def per_device(queries, keys, values, grad_out, frame_map, band, w_query, w_key, w_value, w_out):
    vmem = pl.BlockSpec(memory_space=pltpu.VMEM)
    hbm = pl.BlockSpec(memory_space=pl.ANY)
    smem = pl.BlockSpec(memory_space=pltpu.SMEM)
    gathered = pltpu.VMEM((8 * F, 256), jnp.bfloat16)
    stats = pltpu.VMEM((128, F), jnp.float32)
    pairs = pltpu.VMEM((2, 8, F, F), jnp.bfloat16)
    heads = pltpu.VMEM((2, F, HD), jnp.float32)
    sems = pltpu.SemaphoreType.DMA
    return pl.pallas_call(
        kernel,
        out_shape=jax.ShapeDtypeStruct((320, F), jnp.bfloat16),
        in_specs=[smem] * 2 + [hbm] * 8,
        out_specs=vmem,
        scratch_shapes=[
            pltpu.VMEM((5120, F), jnp.bfloat16),
            pltpu.VMEM((256, 5120), jnp.bfloat16),
            gathered, gathered, gathered, gathered, gathered,
            pltpu.VMEM((F, 256), jnp.bfloat16),
            stats, stats,
            pairs, pairs,
            pltpu.VMEM((F, F), jnp.int32),
            pltpu.VMEM((256, F), jnp.float32),
            heads, heads, heads, heads, heads, heads, heads,
            pltpu.VMEM((160, F), jnp.float32),
            pltpu.VMEM((24, 160, F), jnp.bfloat16),
            pltpu.VMEM((12, 80, F), jnp.bfloat16),
            sems((7,)), sems((40,)), sems((40,)), sems((8 * ARRAYS,)), sems((8 * ARRAYS,)),
            sems((24,)), sems((24,)), sems((12,)), sems((12,)),
        ],
        compiler_params=pltpu.CompilerParams(
            collective_id=0, has_side_effects=True, vmem_limit_bytes=64 * 1024 * 1024
        ),
        cost_estimate=pl.CostEstimate(
            flops=21_000_000_000, bytes_accessed=14_000_000, transcendentals=13_000_000
        ),
    )(frame_map, band, grad_out.T, w_out, queries, keys, values, w_query, w_key, w_value)


def solution(mesh):
    placed = (
        P("tm", "tensor"),
        P("tm", "tensor"),
        P("tm", "tensor"),
        P("tm", "tensor"),
        P(),
        P(),
        P(None, "tensor"),
        P(None, "tensor"),
        P(None, "tensor"),
        P("tensor", None),
    )
    return jax.shard_map(
        per_device, mesh=mesh, in_specs=placed, out_specs=P("tensor", "tm"), check_vma=False
    )
```

```python
import jax
import jax.numpy as jnp
from jax import lax
from jax.experimental import pallas as pl
from jax.experimental.pallas import tpu as pltpu
from jax.sharding import PartitionSpec as P

HD = 128
F = 640
SCALE = HD ** -0.5
POWER = SCALE * 1.4426950408889634
ARRAYS = 6
MESH = pl.DeviceIdType.MESH
NT = (((1,), (1,)), ((), ()))
masked_score = -1e30


def dot(a, b):
    return jnp.dot(a, b, preferred_element_type=jnp.float32)


def dot_nt(a, b):
    return lax.dot_general(a, b, NT, preferred_element_type=jnp.float32)


def ring(position, step):
    return lax.rem(position + step + 4, 4)


def low(value):
    return value.astype(jnp.bfloat16)


def wide(value):
    return value.astype(jnp.float32)


def kernel(
    frame_map, band, go_hbm, wo_hbm, q_hbm, k_hbm, v_hbm, wq_hbm, wk_hbm, wv_hbm, out_ref,
    go, wo, kall, qall, vall, dall, vown, logs, dots, p, pt, dist, dacc, att, gq,
    tops, sums, row_dot, in1, in2,
    load_sem, zs, zr, ys, yr, s1, r1, s2, r2,
):
    g = lax.axis_index("tensor")
    z, x = g // 4, g % 4
    me = lax.axis_index("tm")
    y, core = me // 2, me % 2
    my_frame = frame_map[me]

    def slot_rows(s):
        return pl.ds(pl.multiple_of(s * F, F), F)

    mine = slot_rows(me)

    def load(n, src, dst):
        return pltpu.make_async_copy(src, dst, load_sem.at[n])

    loads = [
        load(0, go_hbm, go.at[pl.ds(pl.multiple_of(g * 320, 320), 320)]),
        load(1, k_hbm, kall.at[mine]),
        load(2, q_hbm, qall.at[mine]),
        load(3, v_hbm, vall.at[mine]),
        load(4, v_hbm, vown),
        load(5, wo_hbm, wo),
    ]
    for item in loads:
        item.start()

    def block(half, d, e):
        zz = ring(z, d * half + e * (1 - half))
        xx = ring(x, d * (1 - half) + e * half)
        return zz * 4 + xx

    def tensor_copy(half, m, j, kind, target):
        start = j * 320 + half * 160 + (80 if kind == 3 else 0)
        ref = go.at[pl.ds(pl.multiple_of(start, 16), 160 if kind < 2 else 80)]
        n = half * 20 + m
        return pltpu.make_async_remote_copy(
            src_ref=ref, dst_ref=ref, send_sem=zs.at[n], recv_sem=zr.at[n],
            device_id={"tensor": target}, device_id_type=MESH,
        )

    def both(step):
        def one(half, carry):
            step(half)
            return carry

        lax.fori_loop(0, 2, one, 0)

    def spread(half, index, d):
        j = block(half, d, 0)
        m = 4 + 4 * index
        tensor_copy(half, m, j, 0, block(half, 0, 1)).start()
        tensor_copy(half, m + 1, j, 1, block(half, 0, -1)).start()

    def tensor_start(half):
        tensor_copy(half, 0, g, 0, block(half, 1, 0)).start()
        tensor_copy(half, 1, g, 1, block(half, -1, 0)).start()

    def tensor_next(half):
        spread(half, 0, 0)

    def tensor_near(half):
        j = block(half, -1, 0)
        tensor_copy(half, 0, j, 0, g).wait_recv()
        tensor_copy(half, 2, j, 2, block(half, 1, 0)).start()
        spread(half, 1, -1)
        j = block(half, 1, 0)
        tensor_copy(half, 1, j, 1, g).wait_recv()
        tensor_copy(half, 3, j, 3, block(half, -1, 0)).start()
        spread(half, 2, 1)

    def tensor_far(half):
        j = block(half, 2, 0)
        tensor_copy(half, 2, j, 2, g).wait_recv()
        tensor_copy(half, 3, j, 3, g).wait_recv()
        spread(half, 3, 2)

    offsets = (0, -1, 1, 2)

    def forward(index):
        def step(half):
            m, d = 4 + 4 * index, offsets[index]
            j = block(half, d, -1)
            tensor_copy(half, m, j, 0, g).wait_recv()
            tensor_copy(half, m + 2, j, 2, block(half, 0, 1)).start()
            j = block(half, d, 1)
            tensor_copy(half, m + 1, j, 1, g).wait_recv()
            tensor_copy(half, m + 3, j, 3, block(half, 0, -1)).start()

        both(step)

    def finish(half, index):
        m, d = 4 + 4 * index, offsets[index]
        j = block(half, d, 2)
        tensor_copy(half, m + 2, j, 2, g).wait_recv()
        tensor_copy(half, m + 3, j, 3, g).wait_recv()

    def add_row(index):
        cols = pl.ds(pl.multiple_of(ring(z, offsets[index]) * 1280, 1280), 1280)
        dacc[...] += dot(wo[:, cols], go[cols, :])

    sibling = y * 2 + 1 - core

    def at_y(step):
        return ring(y, step) * 2 + core

    class Gather:
        def __init__(self, array, ref, rows):
            self.array, self.ref, self.rows = array, ref, rows

        def copy(self, m, slot, target):
            start, count = slot * self.rows, self.rows
            if m in (2, 3):
                count = self.rows // 2
                start = start + (m - 2) * count
            ref = self.ref.at[pl.ds(pl.multiple_of(start, count), count)]
            n = self.array * 8 + m
            return pltpu.make_async_remote_copy(
                src_ref=ref, dst_ref=ref, send_sem=ys.at[n], recv_sem=yr.at[n],
                device_id={"tm": target}, device_id_type=MESH,
            )

        def start(self):
            self.copy(0, me, at_y(1)).start()
            self.copy(1, me, at_y(-1)).start()
            self.copy(4, me, sibling).start()

        def near(self):
            self.copy(0, at_y(-1), me).wait_recv()
            self.copy(2, at_y(-1), at_y(1)).start()
            self.copy(5, at_y(-1), sibling).start()
            self.copy(1, at_y(1), me).wait_recv()
            self.copy(3, at_y(1), at_y(-1)).start()
            self.copy(6, at_y(1), sibling).start()

        def far(self):
            self.copy(2, at_y(2), me).wait_recv()
            self.copy(3, at_y(2), me).wait_recv()
            self.copy(7, at_y(2), sibling).start()

        def from_sibling(self, *messages):
            for m in messages:
                slot = ring(y, (0, -1, 1, 2)[m - 4]) * 2 + 1 - core
                self.copy(m, slot, me).wait_recv()

        def drain(self):
            for m in range(8):
                self.copy(m, me, me).wait_send()

    keys, queries = Gather(0, kall, F), Gather(1, qall, F)
    values, grads = Gather(2, vall, F), Gather(3, dall, F)
    totals, products = Gather(4, logs, 16), Gather(5, dots, 16)

    def by_arrival(gathers, body, events):
        def step(i, carry):
            n = i // 2
            ring_at = (n + 1) // 2
            hop = (ring_at % 2) * (2 * n - 3) + (ring_at // 2) * 2
            waits = {
                0: lambda item: item.from_sibling(4),
                2: lambda item: item.from_sibling(5),
                4: lambda item: item.from_sibling(6),
                5: lambda item: item.far(),
                6: lambda item: item.from_sibling(7),
            }
            for when in range(8):
                if when in waits or when in events:
                    @pl.when(i == when)
                    def _(when=when):
                        if when in events:
                            events[when]()
                        if when in waits:
                            for item in gathers:
                                waits[when](item)

            body(ring(y, hop), i % 2)
            return carry

        lax.fori_loop(0, 8, step, 0)

    lane = lax.broadcasted_iota(jnp.int32, (F, HD), 1)

    def pair_rows(n):
        return pl.ds(pl.multiple_of(n * 2 * F, 2 * F), 2 * F)

    def head(ref, rows, h):
        return ref[rows, pl.ds(pl.multiple_of(h * HD, HD), HD)]

    def stat_row(ref, n, h):
        one = ref[pl.ds(pl.multiple_of(n * 32 + h * 8, 8), 8), :][0:1, :]
        two = ref[pl.ds(pl.multiple_of(n * 32 + 16 + h * 8, 8), 8), :][0:1, :]
        return jnp.concatenate([one, two], axis=1)

    def to_row(ref, h, column):
        rows = pl.ds(pl.multiple_of(me * 16 + h * 8, 8), 8)
        ref[rows, :] = jnp.broadcast_to(column, (F, HD)).T[0:8, :]

    def factor(h, n):
        return jnp.sum(jnp.where(lane == n, sums[h], 0.0), axis=1, keepdims=True)

    def masked(scores, first, second):
        one = jnp.where(dist[...] <= first, scores[:, :F], masked_score)
        two = jnp.where(dist[...] <= second, scores[:, F:], masked_score)
        return jnp.concatenate([one, two], axis=1)

    def softmax(n, h):
        widths = [band[my_frame, frame_map[2 * n + k]] for k in (0, 1)]
        scores = masked(dot_nt(head(qall, mine, h), head(kall, pair_rows(n), h)), *widths)
        top = jnp.max(scores, axis=1, keepdims=True) * POWER
        shifted = jnp.exp2(scores * POWER - top)
        total = jnp.sum(shifted, axis=1, keepdims=True)
        p[h, n] = low(shifted)
        tops[h] = jnp.where(lane == n, top, tops[h])
        sums[h] = jnp.where(lane == n, total, sums[h])

    def combine():
        for h in (0, 1):
            top = jnp.max(tops[h], axis=1, keepdims=True)
            shares = jnp.exp2(tops[h] - top)
            total = jnp.sum(shares * sums[h], axis=1, keepdims=True)
            sums[h] = shares / total
            to_row(logs, h, top + jnp.log2(total))

    def key_side(n, h):
        widths = [band[frame_map[2 * n + k], my_frame] for k in (0, 1)]
        scores = dot_nt(head(kall, mine, h), head(qall, pair_rows(n), h))
        power = masked(scores * POWER - stat_row(logs, n, h), *widths)
        pt[h, n] = low(jnp.exp2(power))

    def attend(n, h):
        att[h] += factor(h, n) * dot(p[h, n], head(vall, pair_rows(n), h))

    def query_grad(n, h):
        grad = dot_nt(head(dall, mine, h), head(vall, pair_rows(n), h))
        grad = low(grad - jnp.concatenate([row_dot[h]] * 10, axis=1))
        gq[h] += factor(h, n) * dot(p[h, n] * grad, head(kall, pair_rows(n), h))

    def key_grad(n, h):
        grad_rows = head(dall, pair_rows(n), h)
        weight = pt[h, n]
        grad = low(dot_nt(head(vown, slice(None), h), grad_rows) - stat_row(dots, n, h))
        gv[h] += dot(weight, grad_rows)
        gk[h] += dot(weight * grad, head(qall, pair_rows(n), h))

    barrier = pltpu.get_barrier_semaphore()
    for half in (0, 1):
        for step in (1, -1):
            pl.semaphore_signal(
                barrier, inc=1, device_id={"tensor": block(half, step, 0)}, device_id_type=MESH
            )
    for target in (at_y(1), at_y(-1), sibling):
        pl.semaphore_signal(barrier, inc=1, device_id={"tm": target}, device_id_type=MESH)
    loads[0].wait()
    loads[1].wait()
    pl.semaphore_wait(barrier, 7)
    both(tensor_start)
    keys.start()
    both(tensor_next)
    across = lax.broadcasted_iota(jnp.int32, (F, F), 0) - lax.broadcasted_iota(jnp.int32, (F, F), 1)
    dist[...] = jnp.abs(across)
    for ref in (dacc, att, gq, sums):
        ref[...] = jnp.zeros_like(ref)
    tops[...] = jnp.full_like(tops, masked_score)
    for item in loads[2:]:
        item.wait()

    def keys_near():
        both(tensor_near)
        keys.near()
        queries.start()

    by_arrival(
        (keys,), softmax,
        {2: keys_near, 5: lambda: both(tensor_far), 7: lambda: forward(0)},
    )
    combine()
    totals.start()

    def queries_near():
        queries.near()
        values.start()
        totals.near()

    by_arrival(
        (queries, totals), key_side,
        {2: queries_near, 4: lambda: forward(1), 7: lambda: forward(2)},
    )
    forward(3)

    def values_near():
        values.near()

    by_arrival((values,), attend, {2: values_near})
    for index in range(4):
        finish(0, index)
    for index in range(4):
        finish(1, index)
        add_row(index)
    dall[mine, :] = low(dacc[...].T)
    grads.start()
    for h in (0, 1):
        column = jnp.sum(wide(head(dall, mine, h)) * att[h], axis=1, keepdims=True)
        row_dot[h] = jnp.broadcast_to(column, (F, HD))
        to_row(dots, h, column)
    products.start()
    gk, gv = tops, att
    for ref in (gk, gv):
        ref[...] = jnp.zeros_like(ref)

    def query_step(i, carry):
        query_grad(i // 2, i % 2)

        @pl.when(i == 5)
        def _():
            grads.near()
            products.near()

        return carry

    lax.fori_loop(0, 8, query_step, 0)
    keys.drain()
    values.drain()
    loads = [load(0, wq_hbm, kall), load(1, wk_hbm, vall)]
    for item in loads:
        item.start()
    gt = [p.at[0, n, 0:256, 0:F] for n in range(3)]

    def to_gt(n, ref, scale):
        for h in (0, 1):
            gt[n][h * HD:(h + 1) * HD, :] = low((ref[h] * scale).T)

    to_gt(0, gq, SCALE)
    by_arrival((grads, products), key_grad, {})
    queries.drain()
    loads.append(load(2, wv_hbm, qall))
    loads[2].start()
    to_gt(1, gk, SCALE)
    to_gt(2, gv, 1.0)
    for item in loads:
        item.wait()

    def drain(half):
        def one(i, carry):
            for kind in range(4):
                tensor_copy(half, 4 * i + kind, g, kind, g).wait_send()
            return carry

        lax.fori_loop(0, 5, one, 0)

    both(drain)

    def target(half, d, e):
        return block(1 - half, d, e)

    def part(half, d, e, skip=0, count=160):
        start = target(half, d, e) * 320 + half * 160 + skip
        return go.at[pl.ds(pl.multiple_of(start, 16), count)]

    def multiply(dz):
        def one(i, carry):
            rows = pl.ds(pl.multiple_of(ring(z, dz) * 1280 + i * F, F), F)
            total = dot(kall[rows, :], gt[0][...]) + dot(vall[rows, :], gt[1][...])
            go[rows, :] = low(total + dot(qall[rows, :], gt[2][...]))
            return carry

        lax.fori_loop(0, 2, one, 0)

    def first(m, half, d, e, step):
        n = half * 12 + m
        return pltpu.make_async_remote_copy(
            src_ref=part(half, d, e), dst_ref=in1.at[n], send_sem=s1.at[n], recv_sem=r1.at[n],
            device_id={"tensor": target(half, step, 0)}, device_id_type=MESH,
        )

    def second(m, half, e, skip, step):
        n = half * 6 + m
        return pltpu.make_async_remote_copy(
            src_ref=part(half, 0, e, skip, 80), dst_ref=in2.at[n], send_sem=s2.at[n], recv_sem=r2.at[n],
            device_id={"tensor": target(half, 0, step)}, device_id_type=MESH,
        )

    far = ((0, 2, 2, 1), (1, 2, 1, -1), (2, 2, 3, 1), (3, 2, 0, -1))
    alone = ((4, 1, 1, 1), (5, 3, 2, -1), (6, 1, 0, 1), (7, 3, 3, -1))
    summed = ((8, 1, 2, 1), (9, 3, 1, -1), (10, 1, 3, 1), (11, 3, 0, -1))

    def send(half, messages):
        for m, d, e, step in messages:
            first(m, half, d, e, step).start()

    multiply(2)
    send(0, far)
    send(1, (far[0], alone[1]))
    multiply(1)
    send(1, (far[1],))
    send(0, (alone[0], alone[2]))
    send(1, (alone[0], ))
    multiply(3)
    send(1, (far[2], alone[3]))
    send(0, (alone[1], alone[3]))
    multiply(0)
    send(1, (far[3], alone[2]))

    def pass_on(m, d, e, step):
        def one(half):
            first(m - 8, half, d, e, step).wait_recv()
            ref = part(half, d, e)
            ref[...] = low(wide(ref[...]) + wide(in1[half * 12 + m - 8]))
            first(m, half, d, e, step).start()

        both(one)

    for message in summed:
        pass_on(*message)

    def collect(half, e, up, down):
        first(up, half, 0, e, 1).wait_recv()
        first(down, half, 0, e, 1).wait_recv()
        return wide(part(half, 0, e)[...]) + wide(in1[half * 12 + up]) + wide(in1[half * 12 + down])

    def collect_far(half):
        total = collect(half, 2, 8, 5)
        part(half, 0, 2)[...] = low(total)
        second(0, half, 2, 0, 1).start()
        second(1, half, 2, 80, -1).start()

    def collect_next(half):
        total = collect(half, 1, 4, 9)
        part(half, 0, 1)[...] = low(total)
        second(2, half, 1, 80, 1).start()
        total_low = total[0:80]
        second(0, half, 1, 0, 1).wait_recv()
        part(half, 0, 1, 0, 80)[...] = low(total_low + wide(in2[half * 6]))
        second(3, half, 1, 0, 1).start()

    def collect_last(half):
        total = collect(half, 3, 10, 7)
        part(half, 0, 3)[...] = low(total)
        second(4, half, 3, 0, -1).start()
        total_high = total[80:160]
        second(1, half, 3, 80, -1).wait_recv()
        part(half, 0, 3, 80, 80)[...] = low(total_high + wide(in2[half * 6 + 1]))
        second(5, half, 3, 80, -1).start()

    def collect_own(half):
        total = collect(half, 0, 6, 11)
        for m in (2, 3, 4, 5):
            second(m, half, 0, 0, 1).wait_recv()
        at = pl.multiple_of(half * 160, 16)
        n = half * 6
        out_ref[pl.ds(at, 80), :] = low(total[0:80] + (wide(in2[n + 3]) + wide(in2[n + 4])))
        out_ref[pl.ds(at + 80, 80), :] = low(total[80:160] + (wide(in2[n + 2]) + wide(in2[n + 5])))

    for step in (collect_far, collect_next, collect_last, collect_own):
        both(step)

    def sent1(m, carry):
        first(m, 0, 0, 0, 1).wait_send()
        return carry

    def sent2(m, carry):
        second(m, 0, 0, 0, 1).wait_send()
        return carry

    lax.fori_loop(0, 24, sent1, 0)
    lax.fori_loop(0, 12, sent2, 0)
    for item in (grads, totals, products):
        item.drain()


def per_device(queries, keys, values, grad_out, frame_map, band, w_query, w_key, w_value, w_out):
    vmem = pl.BlockSpec(memory_space=pltpu.VMEM)
    hbm = pl.BlockSpec(memory_space=pl.ANY)
    smem = pl.BlockSpec(memory_space=pltpu.SMEM)
    gathered = pltpu.VMEM((8 * F, 256), jnp.bfloat16)
    stats = pltpu.VMEM((128, F), jnp.float32)
    pairs = pltpu.VMEM((2, 4, F, 2 * F), jnp.bfloat16)
    heads = pltpu.VMEM((2, F, HD), jnp.float32)
    sems = pltpu.SemaphoreType.DMA
    return pl.pallas_call(
        kernel,
        out_shape=jax.ShapeDtypeStruct((320, F), jnp.bfloat16),
        in_specs=[smem] * 2 + [hbm] * 8,
        out_specs=vmem,
        scratch_shapes=[
            pltpu.VMEM((5120, F), jnp.bfloat16),
            pltpu.VMEM((256, 5120), jnp.bfloat16),
            gathered, gathered, gathered, gathered,
            pltpu.VMEM((F, 256), jnp.bfloat16),
            stats, stats,
            pairs, pairs,
            pltpu.VMEM((F, F), jnp.int32),
            pltpu.VMEM((256, F), jnp.float32),
            heads, heads, heads, heads, heads,
            pltpu.VMEM((24, 160, F), jnp.bfloat16),
            pltpu.VMEM((12, 80, F), jnp.bfloat16),
            sems((6,)), sems((40,)), sems((40,)), sems((8 * ARRAYS,)), sems((8 * ARRAYS,)),
            sems((24,)), sems((24,)), sems((12,)), sems((12,)),
        ],
        compiler_params=pltpu.CompilerParams(
            collective_id=0, has_side_effects=True, vmem_limit_bytes=64 * 1024 * 1024
        ),
        cost_estimate=pl.CostEstimate(
            flops=21_000_000_000, bytes_accessed=14_000_000, transcendentals=13_000_000
        ),
    )(frame_map, band, grad_out.T, w_out, queries, keys, values, w_query, w_key, w_value)


def solution(mesh):
    placed = (
        P("tm", "tensor"),
        P("tm", "tensor"),
        P("tm", "tensor"),
        P("tm", "tensor"),
        P(),
        P(),
        P(None, "tensor"),
        P(None, "tensor"),
        P(None, "tensor"),
        P("tensor", None),
    )
    return jax.shard_map(
        per_device, mesh=mesh, in_specs=placed, out_specs=P("tensor", "tm"), check_vma=False
    )
```

```python
import jax
import jax.numpy as jnp
from jax import lax
from jax.experimental import pallas as pl
from jax.experimental.pallas import tpu as pltpu
from jax.sharding import PartitionSpec as P

HD = 128
F = 640
SCALE = HD ** -0.5
POWER = SCALE * 1.4426950408889634
ARRAYS = 6
MESH = pl.DeviceIdType.MESH
NT = (((1,), (1,)), ((), ()))
masked_score = -1e30


def dot(a, b):
    return jnp.dot(a, b, preferred_element_type=jnp.float32)


def dot_nt(a, b):
    return lax.dot_general(a, b, NT, preferred_element_type=jnp.float32)


def ring(position, step):
    return lax.rem(position + step + 4, 4)


def low(value):
    return value.astype(jnp.bfloat16)


def wide(value):
    return value.astype(jnp.float32)


def kernel(
    frame_map, band, go_hbm, wo_hbm, q_hbm, k_hbm, v_hbm, wq_hbm, wk_hbm, wv_hbm, out_ref,
    go, wo, kall, qall, vall, dall, vown, logs, dots, p, pt, dist, dacc, att, gq,
    tops, sums, row_dot, in1, in2,
    load_sem, zs, zr, ys, yr, s1, r1, s2, r2,
):
    g = lax.axis_index("tensor")
    z, x = g // 4, g % 4
    me = lax.axis_index("tm")
    y, core = me // 2, me % 2
    my_frame = frame_map[me]

    def slot_rows(s):
        return pl.ds(pl.multiple_of(s * F, F), F)

    mine = slot_rows(me)

    def load(n, src, dst):
        return pltpu.make_async_copy(src, dst, load_sem.at[n])

    loads = [
        load(0, go_hbm, go.at[pl.ds(pl.multiple_of(g * 320, 320), 320)]),
        load(1, k_hbm, kall.at[mine]),
        load(2, q_hbm, qall.at[mine]),
        load(3, v_hbm, vall.at[mine]),
        load(4, v_hbm, vown),
        load(5, wo_hbm, wo),
    ]
    for item in loads:
        item.start()

    def block(half, d, e):
        zz = ring(z, d * half + e * (1 - half))
        xx = ring(x, d * (1 - half) + e * half)
        return zz * 4 + xx

    def tensor_copy(half, m, j, kind, target):
        start = j * 320 + half * 160 + (80 if kind == 3 else 0)
        ref = go.at[pl.ds(pl.multiple_of(start, 16), 160 if kind < 2 else 80)]
        n = half * 20 + m
        return pltpu.make_async_remote_copy(
            src_ref=ref, dst_ref=ref, send_sem=zs.at[n], recv_sem=zr.at[n],
            device_id={"tensor": target}, device_id_type=MESH,
        )

    def both(step):
        def one(half, carry):
            step(half)
            return carry

        lax.fori_loop(0, 2, one, 0)

    def spread(half, index, d):
        j = block(half, d, 0)
        m = 4 + 4 * index
        tensor_copy(half, m, j, 0, block(half, 0, 1)).start()
        tensor_copy(half, m + 1, j, 1, block(half, 0, -1)).start()

    def tensor_start(half):
        tensor_copy(half, 0, g, 0, block(half, 1, 0)).start()
        tensor_copy(half, 1, g, 1, block(half, -1, 0)).start()

    def tensor_next(half):
        spread(half, 0, 0)

    def tensor_near(half):
        j = block(half, -1, 0)
        tensor_copy(half, 0, j, 0, g).wait_recv()
        tensor_copy(half, 2, j, 2, block(half, 1, 0)).start()
        spread(half, 1, -1)
        j = block(half, 1, 0)
        tensor_copy(half, 1, j, 1, g).wait_recv()
        tensor_copy(half, 3, j, 3, block(half, -1, 0)).start()
        spread(half, 2, 1)

    def tensor_far(half):
        j = block(half, 2, 0)
        tensor_copy(half, 2, j, 2, g).wait_recv()
        tensor_copy(half, 3, j, 3, g).wait_recv()
        spread(half, 3, 2)

    offsets = (0, -1, 1, 2)

    def forward(index):
        def step(half):
            m, d = 4 + 4 * index, offsets[index]
            j = block(half, d, -1)
            tensor_copy(half, m, j, 0, g).wait_recv()
            tensor_copy(half, m + 2, j, 2, block(half, 0, 1)).start()
            j = block(half, d, 1)
            tensor_copy(half, m + 1, j, 1, g).wait_recv()
            tensor_copy(half, m + 3, j, 3, block(half, 0, -1)).start()

        both(step)

    def finish(half, index):
        m, d = 4 + 4 * index, offsets[index]
        j = block(half, d, 2)
        tensor_copy(half, m + 2, j, 2, g).wait_recv()
        tensor_copy(half, m + 3, j, 3, g).wait_recv()

    def add_row(index):
        cols = pl.ds(pl.multiple_of(ring(z, offsets[index]) * 1280, 1280), 1280)
        dacc[...] += dot(wo[:, cols], go[cols, :])

    sibling = y * 2 + 1 - core

    def at_y(step):
        return ring(y, step) * 2 + core

    class Gather:
        def __init__(self, array, ref, rows):
            self.array, self.ref, self.rows = array, ref, rows

        def copy(self, m, slot, target):
            start, count = slot * self.rows, self.rows
            if m in (2, 3):
                count = self.rows // 2
                start = start + (m - 2) * count
            ref = self.ref.at[pl.ds(pl.multiple_of(start, count), count)]
            n = self.array * 8 + m
            return pltpu.make_async_remote_copy(
                src_ref=ref, dst_ref=ref, send_sem=ys.at[n], recv_sem=yr.at[n],
                device_id={"tm": target}, device_id_type=MESH,
            )

        def start(self):
            self.copy(0, me, at_y(1)).start()
            self.copy(1, me, at_y(-1)).start()
            self.copy(4, me, sibling).start()

        def near(self):
            self.copy(0, at_y(-1), me).wait_recv()
            self.copy(2, at_y(-1), at_y(1)).start()
            self.copy(5, at_y(-1), sibling).start()
            self.copy(1, at_y(1), me).wait_recv()
            self.copy(3, at_y(1), at_y(-1)).start()
            self.copy(6, at_y(1), sibling).start()

        def far(self):
            self.copy(2, at_y(2), me).wait_recv()
            self.copy(3, at_y(2), me).wait_recv()
            self.copy(7, at_y(2), sibling).start()

        def from_sibling(self, *messages):
            for m in messages:
                slot = ring(y, (0, -1, 1, 2)[m - 4]) * 2 + 1 - core
                self.copy(m, slot, me).wait_recv()

        def drain(self):
            for m in range(8):
                self.copy(m, me, me).wait_send()

    keys, queries = Gather(0, kall, F), Gather(1, qall, F)
    values, grads = Gather(2, vall, F), Gather(3, dall, F)
    totals, products = Gather(4, logs, 16), Gather(5, dots, 16)

    def by_arrival(gathers, body, events):
        def step(n, carry):
            ring_at = (n + 2) // 4
            hop = (ring_at % 2) * (2 * (n % 2) - 1) + (ring_at // 2) * 2
            other = (1 - ring_at % 2) * (n % 2) + (ring_at % 2) * (((n + 2) // 2) % 2)
            slot = ring(y, hop) * 2 + (core + other) % 2
            waits = {
                1: lambda item: item.from_sibling(4),
                4: lambda item: item.from_sibling(5, 6),
                6: lambda item: item.far(),
                7: lambda item: item.from_sibling(7),
            }
            for when in range(8):
                if when in waits or when in events:
                    @pl.when(n == when)
                    def _(when=when):
                        if when in events:
                            events[when]()
                        if when in waits:
                            for item in gathers:
                                waits[when](item)

            body(slot)
            return carry

        lax.fori_loop(0, 8, step, 0)

    lane = lax.broadcasted_iota(jnp.int32, (F, HD), 1)

    def head(ref, rows, h):
        return ref[rows, h * HD:(h + 1) * HD]

    def stat_row(ref, s, h):
        return ref[pl.ds(pl.multiple_of(s * 16 + h * 8, 8), 8), :][0:1, :]

    def to_row(ref, h, column):
        rows = pl.ds(pl.multiple_of(me * 16 + h * 8, 8), 8)
        ref[rows, :] = jnp.broadcast_to(column, (F, HD)).T[0:8, :]

    def factor(h, s):
        return jnp.sum(jnp.where(lane == s, sums[h], 0.0), axis=1, keepdims=True)

    def softmax(s):
        width = band[my_frame, frame_map[s]]
        for h in (0, 1):
            scores = dot_nt(head(qall, mine, h), head(kall, slot_rows(s), h))
            scores = jnp.where(dist[...] <= width, scores, masked_score)
            top = jnp.max(scores, axis=1, keepdims=True) * POWER
            shifted = jnp.exp2(scores * POWER - top)
            total = jnp.sum(shifted, axis=1, keepdims=True)
            p[h, s] = low(shifted)
            tops[h] = jnp.where(lane == s, top, tops[h])
            sums[h] = jnp.where(lane == s, total, sums[h])

    def combine():
        for h in (0, 1):
            top = jnp.max(tops[h], axis=1, keepdims=True)
            shares = jnp.exp2(tops[h] - top)
            total = jnp.sum(shares * sums[h], axis=1, keepdims=True)
            sums[h] = shares / total
            to_row(logs, h, top + jnp.log2(total))

    def key_side(s):
        width = band[frame_map[s], my_frame]
        for h in (0, 1):
            scores = dot_nt(head(kall, mine, h), head(qall, slot_rows(s), h))
            power = jnp.where(
                dist[...] <= width, scores * POWER - stat_row(logs, s, h), masked_score
            )
            pt[h, s] = low(jnp.exp2(power))

    def attend(s):
        for h in (0, 1):
            att[h] += factor(h, s) * dot(p[h, s], head(vall, slot_rows(s), h))

    def query_grad(s):
        for h in (0, 1):
            grad = dot_nt(head(dall, mine, h), head(vall, slot_rows(s), h))
            grad = wide(p[h, s]) * ((grad - row_dot[h, :, 0:1]) * factor(h, s))
            gq[h] += dot(low(grad), head(kall, slot_rows(s), h))

    def key_grad(s):
        for h in (0, 1):
            grad_rows = head(dall, slot_rows(s), h)
            weight = pt[h, s]
            grad = dot_nt(head(vown, slice(None), h), grad_rows)
            grad = wide(weight) * (grad - stat_row(dots, s, h))
            gv[h] += dot(weight, grad_rows)
            gk[h] += dot(low(grad), head(qall, slot_rows(s), h))

    barrier = pltpu.get_barrier_semaphore()
    for half in (0, 1):
        for step in (1, -1):
            pl.semaphore_signal(
                barrier, inc=1, device_id={"tensor": block(half, step, 0)}, device_id_type=MESH
            )
    for target in (at_y(1), at_y(-1), sibling):
        pl.semaphore_signal(barrier, inc=1, device_id={"tm": target}, device_id_type=MESH)
    loads[0].wait()
    loads[1].wait()
    pl.semaphore_wait(barrier, 7)
    both(tensor_start)
    keys.start()
    both(tensor_next)
    across = lax.broadcasted_iota(jnp.int32, (F, F), 0) - lax.broadcasted_iota(jnp.int32, (F, F), 1)
    dist[...] = jnp.abs(across)
    for ref in (dacc, att, gq, sums):
        ref[...] = jnp.zeros_like(ref)
    tops[...] = jnp.full_like(tops, masked_score)
    for item in loads[2:]:
        item.wait()

    def keys_near():
        both(tensor_near)
        keys.near()
        queries.start()

    by_arrival(
        (keys,), softmax,
        {2: keys_near, 5: lambda: both(tensor_far), 7: lambda: forward(0)},
    )
    combine()
    totals.start()

    def queries_near():
        queries.near()
        values.start()
        totals.near()

    by_arrival(
        (queries, totals), key_side,
        {2: queries_near, 4: lambda: forward(1), 7: lambda: forward(2)},
    )
    forward(3)

    def values_near():
        values.near()

    by_arrival((values,), attend, {2: values_near})
    for index in range(4):
        finish(0, index)
    for index in range(4):
        finish(1, index)
        add_row(index)
    dall[mine, :] = low(dacc[...].T)
    grads.start()
    for h in (0, 1):
        column = jnp.sum(wide(head(dall, mine, h)) * att[h], axis=1, keepdims=True)
        row_dot[h] = jnp.broadcast_to(column, (F, HD))
        to_row(dots, h, column)
    products.start()
    gk, gv = tops, att
    for ref in (gk, gv):
        ref[...] = jnp.zeros_like(ref)

    def query_step(s, carry):
        query_grad(s)

        @pl.when(s == 5)
        def _():
            grads.near()
            products.near()

        return carry

    lax.fori_loop(0, 8, query_step, 0)
    keys.drain()
    values.drain()
    loads = [load(0, wq_hbm, kall), load(1, wk_hbm, vall)]
    for item in loads:
        item.start()
    gt = [p.at[0, n, 0:256] for n in range(3)]

    def to_gt(n, ref, scale):
        for h in (0, 1):
            gt[n][h * HD:(h + 1) * HD, :] = low((ref[h] * scale).T)

    to_gt(0, gq, SCALE)
    by_arrival((grads, products), key_grad, {})
    queries.drain()
    loads.append(load(2, wv_hbm, qall))
    loads[2].start()
    to_gt(1, gk, SCALE)
    to_gt(2, gv, 1.0)
    for item in loads:
        item.wait()

    def drain(half):
        def one(i, carry):
            for kind in range(4):
                tensor_copy(half, 4 * i + kind, g, kind, g).wait_send()
            return carry

        lax.fori_loop(0, 5, one, 0)

    both(drain)

    def target(half, d, e):
        return block(1 - half, d, e)

    def part(half, d, e, skip=0, count=160):
        start = target(half, d, e) * 320 + half * 160 + skip
        return go.at[pl.ds(pl.multiple_of(start, 16), count)]

    def multiply(dz):
        def one(i, carry):
            rows = pl.ds(pl.multiple_of(ring(z, dz) * 1280 + i * F, F), F)
            total = dot(kall[rows, :], gt[0][...]) + dot(vall[rows, :], gt[1][...])
            go[rows, :] = low(total + dot(qall[rows, :], gt[2][...]))
            return carry

        lax.fori_loop(0, 2, one, 0)

    def first(m, half, d, e, step):
        n = half * 12 + m
        return pltpu.make_async_remote_copy(
            src_ref=part(half, d, e), dst_ref=in1.at[n], send_sem=s1.at[n], recv_sem=r1.at[n],
            device_id={"tensor": target(half, step, 0)}, device_id_type=MESH,
        )

    def second(m, half, e, skip, step):
        n = half * 6 + m
        return pltpu.make_async_remote_copy(
            src_ref=part(half, 0, e, skip, 80), dst_ref=in2.at[n], send_sem=s2.at[n], recv_sem=r2.at[n],
            device_id={"tensor": target(half, 0, step)}, device_id_type=MESH,
        )

    far = ((0, 2, 2, 1), (1, 2, 1, -1), (2, 2, 3, 1), (3, 2, 0, -1))
    alone = ((4, 1, 1, 1), (5, 3, 2, -1), (6, 1, 0, 1), (7, 3, 3, -1))
    summed = ((8, 1, 2, 1), (9, 3, 1, -1), (10, 1, 3, 1), (11, 3, 0, -1))

    def send(half, messages):
        for m, d, e, step in messages:
            first(m, half, d, e, step).start()

    multiply(2)
    send(0, far)
    send(1, (far[0], alone[1]))
    multiply(1)
    send(1, (far[1],))
    send(0, (alone[0], alone[2]))
    send(1, (alone[0], ))
    multiply(3)
    send(1, (far[2], alone[3]))
    send(0, (alone[1], alone[3]))
    multiply(0)
    send(1, (far[3], alone[2]))

    def pass_on(m, d, e, step):
        def one(half):
            first(m - 8, half, d, e, step).wait_recv()
            ref = part(half, d, e)
            ref[...] = low(wide(ref[...]) + wide(in1[half * 12 + m - 8]))
            first(m, half, d, e, step).start()

        both(one)

    for message in summed:
        pass_on(*message)

    def collect(half, e, up, down):
        first(up, half, 0, e, 1).wait_recv()
        first(down, half, 0, e, 1).wait_recv()
        return wide(part(half, 0, e)[...]) + wide(in1[half * 12 + up]) + wide(in1[half * 12 + down])

    def collect_far(half):
        total = collect(half, 2, 8, 5)
        part(half, 0, 2)[...] = low(total)
        second(0, half, 2, 0, 1).start()
        second(1, half, 2, 80, -1).start()

    def collect_next(half):
        total = collect(half, 1, 4, 9)
        part(half, 0, 1)[...] = low(total)
        second(2, half, 1, 80, 1).start()
        total_low = total[0:80]
        second(0, half, 1, 0, 1).wait_recv()
        part(half, 0, 1, 0, 80)[...] = low(total_low + wide(in2[half * 6]))
        second(3, half, 1, 0, 1).start()

    def collect_last(half):
        total = collect(half, 3, 10, 7)
        part(half, 0, 3)[...] = low(total)
        second(4, half, 3, 0, -1).start()
        total_high = total[80:160]
        second(1, half, 3, 80, -1).wait_recv()
        part(half, 0, 3, 80, 80)[...] = low(total_high + wide(in2[half * 6 + 1]))
        second(5, half, 3, 80, -1).start()

    def collect_own(half):
        total = collect(half, 0, 6, 11)
        for m in (2, 3, 4, 5):
            second(m, half, 0, 0, 1).wait_recv()
        at = pl.multiple_of(half * 160, 16)
        n = half * 6
        out_ref[pl.ds(at, 80), :] = low(total[0:80] + (wide(in2[n + 3]) + wide(in2[n + 4])))
        out_ref[pl.ds(at + 80, 80), :] = low(total[80:160] + (wide(in2[n + 2]) + wide(in2[n + 5])))

    for step in (collect_far, collect_next, collect_last, collect_own):
        both(step)

    def sent1(m, carry):
        first(m, 0, 0, 0, 1).wait_send()
        return carry

    def sent2(m, carry):
        second(m, 0, 0, 0, 1).wait_send()
        return carry

    lax.fori_loop(0, 24, sent1, 0)
    lax.fori_loop(0, 12, sent2, 0)
    for item in (grads, totals, products):
        item.drain()


def per_device(queries, keys, values, grad_out, frame_map, band, w_query, w_key, w_value, w_out):
    vmem = pl.BlockSpec(memory_space=pltpu.VMEM)
    hbm = pl.BlockSpec(memory_space=pl.ANY)
    smem = pl.BlockSpec(memory_space=pltpu.SMEM)
    gathered = pltpu.VMEM((8 * F, 256), jnp.bfloat16)
    stats = pltpu.VMEM((128, F), jnp.float32)
    pairs = pltpu.VMEM((2, 8, F, F), jnp.bfloat16)
    heads = pltpu.VMEM((2, F, HD), jnp.float32)
    sems = pltpu.SemaphoreType.DMA
    return pl.pallas_call(
        kernel,
        out_shape=jax.ShapeDtypeStruct((320, F), jnp.bfloat16),
        in_specs=[smem] * 2 + [hbm] * 8,
        out_specs=vmem,
        scratch_shapes=[
            pltpu.VMEM((5120, F), jnp.bfloat16),
            pltpu.VMEM((256, 5120), jnp.bfloat16),
            gathered, gathered, gathered, gathered,
            pltpu.VMEM((F, 256), jnp.bfloat16),
            stats, stats,
            pairs, pairs,
            pltpu.VMEM((F, F), jnp.int32),
            pltpu.VMEM((256, F), jnp.float32),
            heads, heads, heads, heads, heads,
            pltpu.VMEM((24, 160, F), jnp.bfloat16),
            pltpu.VMEM((12, 80, F), jnp.bfloat16),
            sems((6,)), sems((40,)), sems((40,)), sems((8 * ARRAYS,)), sems((8 * ARRAYS,)),
            sems((24,)), sems((24,)), sems((12,)), sems((12,)),
        ],
        compiler_params=pltpu.CompilerParams(
            collective_id=0, has_side_effects=True, vmem_limit_bytes=64 * 1024 * 1024
        ),
        cost_estimate=pl.CostEstimate(
            flops=21_000_000_000, bytes_accessed=14_000_000, transcendentals=13_000_000
        ),
    )(frame_map, band, grad_out.T, w_out, queries, keys, values, w_query, w_key, w_value)


def solution(mesh):
    placed = (
        P("tm", "tensor"),
        P("tm", "tensor"),
        P("tm", "tensor"),
        P("tm", "tensor"),
        P(),
        P(),
        P(None, "tensor"),
        P(None, "tensor"),
        P(None, "tensor"),
        P("tensor", None),
    )
    return jax.shard_map(
        per_device, mesh=mesh, in_specs=placed, out_specs=P("tensor", "tm"), check_vma=False
    )
```

```python
import jax
import jax.numpy as jnp
from jax import lax
from jax.experimental import pallas as pl
from jax.experimental.pallas import tpu as pltpu
from jax.sharding import PartitionSpec as P

HD = 128
F = 640
SCALE = HD ** -0.5
POWER = SCALE * 1.4426950408889634
ARRAYS = 6
CHUNKS = ((0, 384), (384, 256))
MESH = pl.DeviceIdType.MESH
NT = (((1,), (1,)), ((), ()))
masked_score = -1e30


def dot(a, b):
    return jnp.dot(a, b, preferred_element_type=jnp.float32)


def dot_nt(a, b):
    return lax.dot_general(a, b, NT, preferred_element_type=jnp.float32)


def ring(position, step):
    return lax.rem(position + step + 4, 4)


def low(value):
    return value.astype(jnp.bfloat16)


def wide(value):
    return value.astype(jnp.float32)


def kernel(
    frame_map, band, go_hbm, wo_hbm, q_hbm, k_hbm, v_hbm, wq_hbm, wk_hbm, wv_hbm, out_ref,
    go, wo, wq, wk, wv, qall, dall, kown, vown, ktr, vtr, stage, stats, shares, dots0, dots1, pt, dist,
    dacc, att, gk, gv, abuf, asib, aopp, afin, qbuf0, qsib0, qopp0, qfin0, qbuf1, qsib1, qopp1, qfin1, gt, in1, in2,
    load_sem, zs, zr, ys, yr, ts, tr, s1, r1, s2, r2,
):
    g = lax.axis_index("tensor")
    z, x = g // 4, g % 4
    me = lax.axis_index("tm")
    y, core = me // 2, me % 2
    my_frame = frame_map[me]

    def slot_rows(s):
        return pl.ds(pl.multiple_of(s * F, F), F)

    mine = slot_rows(me)

    def load(n, src, dst):
        return pltpu.make_async_copy(src, dst, load_sem.at[n])

    loads = [
        load(0, go_hbm, go.at[pl.ds(pl.multiple_of(g * 320, 320), 320)]),
        load(1, q_hbm, qall.at[mine]),
        load(2, k_hbm, kown),
        load(3, v_hbm, vown),
        load(4, wo_hbm, wo),
        load(5, wq_hbm, wq),
        load(6, wk_hbm, wk),
        load(7, wv_hbm, wv),
    ]
    for item in loads:
        item.start()

    def block(half, d, e):
        zz = ring(z, d * half + e * (1 - half))
        xx = ring(x, d * (1 - half) + e * half)
        return zz * 4 + xx

    def tokens(c):
        return slice(CHUNKS[c][0], sum(CHUNKS[c]))

    def tensor_copy(c, half, m, j, kind, target):
        start = j * 320 + half * 160 + (80 if kind == 3 else 0)
        ref = go.at[pl.ds(pl.multiple_of(start, 16), 160 if kind < 2 else 80), tokens(c)]
        n = c * 40 + half * 20 + m
        return pltpu.make_async_remote_copy(
            src_ref=ref, dst_ref=ref, send_sem=zs.at[n], recv_sem=zr.at[n],
            device_id={"tensor": target}, device_id_type=MESH,
        )

    def both(step):
        def one(half, carry):
            step(half)
            return carry

        lax.fori_loop(0, 2, one, 0)

    def spread(c, half, index, d):
        j = block(half, d, 0)
        m = 4 + 4 * index
        tensor_copy(c, half, m, j, 0, block(half, 0, 1)).start()
        tensor_copy(c, half, m + 1, j, 1, block(half, 0, -1)).start()

    def tensor_start(c):
        def step(half):
            tensor_copy(c, half, 0, g, 0, block(half, 1, 0)).start()
            tensor_copy(c, half, 1, g, 1, block(half, -1, 0)).start()

        both(step)

    def tensor_next(c):
        both(lambda half: spread(c, half, 0, 0))

    def tensor_near(c):
        def step(half):
            j = block(half, -1, 0)
            tensor_copy(c, half, 0, j, 0, g).wait_recv()
            tensor_copy(c, half, 2, j, 2, block(half, 1, 0)).start()
            spread(c, half, 1, -1)
            j = block(half, 1, 0)
            tensor_copy(c, half, 1, j, 1, g).wait_recv()
            tensor_copy(c, half, 3, j, 3, block(half, -1, 0)).start()
            spread(c, half, 2, 1)

        both(step)

    def tensor_far(c):
        def step(half):
            j = block(half, 2, 0)
            tensor_copy(c, half, 2, j, 2, g).wait_recv()
            tensor_copy(c, half, 3, j, 3, g).wait_recv()
            spread(c, half, 3, 2)

        both(step)

    offsets = (0, -1, 1, 2)

    def forward(c, index):
        def step(half):
            m, d = 4 + 4 * index, offsets[index]
            j = block(half, d, -1)
            tensor_copy(c, half, m, j, 0, g).wait_recv()
            tensor_copy(c, half, m + 2, j, 2, block(half, 0, 1)).start()
            j = block(half, d, 1)
            tensor_copy(c, half, m + 1, j, 1, g).wait_recv()
            tensor_copy(c, half, m + 3, j, 3, block(half, 0, -1)).start()

        both(step)

    def finish(c, half, index):
        m, d = 4 + 4 * index, offsets[index]
        j = block(half, d, 2)
        tensor_copy(c, half, m + 2, j, 2, g).wait_recv()
        tensor_copy(c, half, m + 3, j, 3, g).wait_recv()

    def add_row(c, index):
        cols = pl.ds(pl.multiple_of(ring(z, offsets[index]) * 1280, 1280), 1280)
        dacc[:, tokens(c)] += dot(wo[:, cols], go[cols, tokens(c)])

    sibling = y * 2 + 1 - core

    def at_y(step):
        return ring(y, step) * 2 + core

    class Gather:
        def __init__(self, array, ref, rows, stride=None, offset=0):
            self.array, self.ref, self.rows = array, ref, rows
            self.stride, self.offset = stride or rows, offset

        def copy(self, m, slot, target):
            start, count = slot * self.stride + self.offset, self.rows
            if m in (2, 3):
                count = self.rows // 2
                start = start + (m - 2) * count
            ref = self.ref.at[pl.ds(pl.multiple_of(start, 16 if count % 16 == 0 else 8), count)]
            n = self.array * 8 + m
            return pltpu.make_async_remote_copy(
                src_ref=ref, dst_ref=ref, send_sem=ys.at[n], recv_sem=yr.at[n],
                device_id={"tm": target}, device_id_type=MESH,
            )

        def start(self):
            self.copy(0, me, at_y(1)).start()
            self.copy(1, me, at_y(-1)).start()
            self.copy(4, me, sibling).start()

        def near(self):
            self.copy(0, at_y(-1), me).wait_recv()
            self.copy(2, at_y(-1), at_y(1)).start()
            self.copy(5, at_y(-1), sibling).start()
            self.copy(1, at_y(1), me).wait_recv()
            self.copy(3, at_y(1), at_y(-1)).start()
            self.copy(6, at_y(1), sibling).start()

        def far(self):
            self.copy(2, at_y(2), me).wait_recv()
            self.copy(3, at_y(2), me).wait_recv()
            self.copy(7, at_y(2), sibling).start()

        def from_sibling(self, *messages):
            for m in messages:
                slot = ring(y, (0, -1, 1, 2)[m - 4]) * 2 + 1 - core
                self.copy(m, slot, me).wait_recv()

        def drain(self):
            for m in range(8):
                self.copy(m, me, me).wait_send()

    queries, blocks = Gather(0, qall, F), Gather(1, stats, 32)
    grads = [Gather(2 + c, dall, CHUNKS[c][1], F, CHUNKS[c][0]) for c in (0, 1)]
    dots = (dots0, dots1)
    products = [Gather(4 + c, dots[c], 16) for c in (0, 1)]

    class Scatter:
        def __init__(self, array, buf, from_core, far, last):
            self.array, self.buf, self.from_core, self.far, self.last = array, buf, from_core, far, last

        def rows(self, k, other, skip=0, count=256):
            slot = ring(y, (2, 1, -1, 0)[k]) * 2 + (core + other) % 2
            return pl.ds(pl.multiple_of(slot * 256 + skip, 128), count)

        def copy(self, m, src, dst, target):
            n = self.array * 10 + m
            return pltpu.make_async_remote_copy(
                src_ref=self.buf.at[src], dst_ref=dst, send_sem=ts.at[n], recv_sem=tr.at[n],
                device_id={"tm": target}, device_id_type=MESH,
            )

        def core_copy(self, k):
            return self.copy(k, self.rows(k, 1), self.from_core.at[k], sibling)

        def half_copy(self, m):
            k = {4: 0, 5: 0, 6: 1, 7: 1, 8: 2, 9: 2}[m]
            skip = {4: 0, 5: 128, 6: 128, 7: 0, 8: 0, 9: 128}[m]
            up = m in (4, 6, 7)
            if m < 6:
                dst = self.far.at[m - 4]
            else:
                dst = self.last.at[0 if up else 1, skip:skip + 128]
            return self.copy(m, self.rows(k, 0, skip, 128), dst, at_y(1 if up else -1))

        def merge(self, k):
            self.core_copy(k).wait_recv()
            rows = self.rows(k, 0)
            total = wide(self.buf[rows, :]) + wide(self.from_core[k])
            if k == 3:
                for m in (6, 7, 8, 9):
                    self.half_copy(m).wait_recv()
                return total + (wide(self.last[0]) + wide(self.last[1]))
            self.buf[rows, :] = low(total)
            if k == 0:
                self.half_copy(4).start()
                self.half_copy(5).start()
                return None
            ready, later, wait, skip = ((6, 7, 4, 0), (8, 9, 5, 128))[k - 1]
            self.half_copy(ready).start()
            self.half_copy(wait).wait_recv()
            self.buf[self.rows(k, 0, skip, 128), :] = low(total[skip:skip + 128] + wide(self.far[wait - 4]))
            self.half_copy(later).start()
            return None

        def drain(self):
            for k in range(4):
                self.core_copy(k).wait_send()
            for m in range(4, 10):
                self.half_copy(m).wait_send()

    attended = Scatter(0, abuf, asib, aopp, afin)
    query_grads = (Scatter(1, qbuf0, qsib0, qopp0, qfin0), Scatter(2, qbuf1, qsib1, qopp1, qfin1))
    qbuf = (qbuf0, qbuf1)

    def by_arrival(body, before, after):
        def step(n, carry):
            def run(events):
                for when in events:
                    @pl.when(n == when)
                    def _(when=when):
                        events[when]()

            run(before)
            body(ring(y, (4 - n // 2) % 4) * 2 + (core + n % 2) % 2)
            run(after)
            return carry

        lax.fori_loop(0, 8, step, 0)

    def slot_waits(gathers, events):
        def at(n):
            def run():
                if n in events:
                    events[n]()
                for item in gathers:
                    if n == 4:
                        item.far()
                    if n in (1, 3, 5, 7):
                        item.from_sibling({1: 4, 3: 5, 5: 7, 7: 6}[n])

            return run

        return {n: at(n) for n in range(1, 8)}

    def rows_of(h):
        return slice(h * HD, (h + 1) * HD)

    def head(ref, rows, h):
        return ref[rows, rows_of(h)]

    def stat_row(ref, s, h):
        return ref[pl.ds(pl.multiple_of(s * 16 + h * 8, 8), 8), :][0:1, :]

    def slot_lanes(s, h):
        return pl.ds(pl.multiple_of(s * 256 + h * HD, HD), HD)

    def scores_side(s):
        width = band[frame_map[s], my_frame]
        rows = []
        for h in (0, 1):
            scores = dot_nt(kown[:, rows_of(h)], head(qall, slot_rows(s), h))
            scores = jnp.where(dist[...] <= width, scores, masked_score)
            top = jnp.max(scores, axis=0, keepdims=True) * POWER
            shifted = jnp.exp2(scores * POWER - top)
            weight = low(shifted)
            pt[h, s] = weight
            abuf[slot_lanes(s, h), :] = low(dot(vtr[rows_of(h), :], weight))
            rows.append((top, jnp.sum(shifted, axis=0, keepdims=True)))
        (top0, sum0), (top1, sum1) = rows
        stage[pl.ds(pl.multiple_of(s * 8, 8), 8), :] = jnp.concatenate(
            [top0, top1, sum0, sum1, top0, top1, sum0, sum1], axis=0
        )

    def share_blocks():
        base = me * 32
        for k in (0, 1):
            for first_row, skip in ((0, 0), (16, 2)):
                tile = [stage[s * 8 + skip:s * 8 + skip + 2, :] for s in range(4 * k, 4 * k + 4)]
                at = pl.ds(pl.multiple_of(base + first_row + 8 * k, 8), 8)
                stats[at, :] = jnp.concatenate(tile, axis=0)

    def combine():
        tops = [stats[s * 32:s * 32 + 16, :] for s in range(8)]
        top = tops[0]
        for one in tops[1:]:
            top = jnp.maximum(top, one)
        total = jnp.zeros_like(top)
        for s in range(8):
            total += stats[s * 32 + 16:s * 32 + 32, :] * jnp.exp2(tops[s] - top)
        own = stats[pl.ds(pl.multiple_of(me * 32, 16), 16), :]
        share = jnp.exp2(own - (top + jnp.log2(total)))
        for n in range(16):
            shares[n * 8:(n + 1) * 8, :] = jnp.broadcast_to(share[n:n + 1, :], (8, F))

    def scale_attended(s):
        for h in (0, 1):
            rows = slot_lanes(s, h)
            abuf[rows, :] = low(wide(abuf[rows, :]) * stat_row(shares, s, h))

    def scale_probs(s):
        for h in (0, 1):
            pt[h, s] = low(wide(pt[h, s]) * stat_row(shares, s, h))

    def gradients(c):
        at, count = CHUNKS[c]

        def step(s):
            rows = pl.ds(pl.multiple_of(s * F + at, 128), count)
            for h in (0, 1):
                grad_rows = head(dall, rows, h)
                weight = pt[h, s, :, tokens(c)]
                grad = low(dot_nt(vown[:, rows_of(h)], grad_rows) - stat_row(dots[c], s, h))
                grad = weight * grad
                gv[h] += dot(weight, grad_rows)
                gk[h] += dot(grad, head(qall, rows, h))
                qbuf[c][slot_lanes(s, h), :] = low(dot(ktr[rows_of(h), :], grad) * SCALE)

        return step

    barrier = pltpu.get_barrier_semaphore()
    for half in (0, 1):
        for step in (1, -1):
            pl.semaphore_signal(
                barrier, inc=1, device_id={"tensor": block(half, step, 0)}, device_id_type=MESH
            )
    for target in (at_y(1), at_y(-1), sibling):
        pl.semaphore_signal(barrier, inc=1, device_id={"tm": target}, device_id_type=MESH)
    loads[0].wait()
    loads[1].wait()
    pl.semaphore_wait(barrier, 7)
    tensor_start(0)
    queries.start()
    tensor_next(0)
    across = lax.broadcasted_iota(jnp.int32, (F, F), 0) - lax.broadcasted_iota(jnp.int32, (F, F), 1)
    dist[...] = jnp.abs(across)
    for ref in (dacc, gk, gv):
        ref[...] = jnp.zeros_like(ref)
    for item in loads[2:]:
        item.wait()
    ktr[...] = low(wide(kown[...]).T)
    vtr[...] = low(wide(vown[...]).T)

    def queries_near():
        tensor_near(0)
        queries.near()

    by_arrival(
        scores_side,
        slot_waits((queries,), {
            2: queries_near,
            4: lambda: tensor_far(0),
            5: lambda: forward(0, 0),
            6: lambda: forward(0, 1),
            7: lambda: forward(0, 2),
        }),
        {},
    )
    share_blocks()
    blocks.start()
    forward(0, 3)
    tensor_start(1)
    blocks.near()
    blocks.from_sibling(4)
    blocks.far()
    tensor_next(1)
    blocks.from_sibling(5, 6, 7)
    combine()

    def eight(step):
        def one(s, carry):
            step(s)
            return carry

        lax.fori_loop(0, 8, one, 0)

    eight(scale_attended)
    for k in range(4):
        attended.core_copy(k).start()
    tensor_near(1)

    def probs_step(s):
        scale_probs(s)
        events = {
            1: lambda: attended.merge(0),
            3: lambda: tensor_far(1),
            6: lambda: attended.merge(1),
            7: lambda: attended.merge(2),
        }
        for when in events:
            @pl.when(s == when)
            def _(when=when):
                events[when]()

    eight(probs_step)

    def form_output_grad(c):
        at, count = CHUNKS[c]
        for index in range(4):
            finish(c, 0, index)
        for index in range(4):
            finish(c, 1, index)
            add_row(c, index)
        rows = pl.ds(pl.multiple_of(me * F + at, 128), count)
        dall[rows, :] = low(dacc[:, tokens(c)].T)
        grads[c].start()

    def form_row_dots(c):
        for h in (0, 1):
            own = wide(low(dacc[rows_of(h), tokens(c)])) * att[rows_of(h), tokens(c)]
            row = jnp.sum(own, axis=0, keepdims=True)
            at = pl.ds(pl.multiple_of(me * 16 + h * 8, 8), 8)
            dots[c][at, :] = jnp.broadcast_to(row, (8, CHUNKS[c][1]))
        products[c].start()

    def run_gradients(c, events):
        def near():
            grads[c].near()
            products[c].near()

        scatter = query_grads[c]
        by_arrival(
            gradients(c),
            slot_waits((grads[c], products[c]), {2: near, **events}),
            {
                1: lambda: scatter.core_copy(3).start(),
                3: lambda: scatter.core_copy(2).start(),
                5: lambda: scatter.core_copy(0).start(),
                6: lambda: scatter.merge(0),
                7: lambda: scatter.core_copy(1).start(),
            },
        )

    form_output_grad(0)
    forward(1, 0)
    att[...] = attended.merge(3)
    form_row_dots(0)
    forward(1, 1)
    run_gradients(0, {3: lambda: forward(1, 2), 5: lambda: forward(1, 3)})
    query_grads[0].merge(2)
    query_grads[0].merge(1)
    form_output_grad(1)
    form_row_dots(1)
    gt[0, :, tokens(0)] = low(query_grads[0].merge(3))
    run_gradients(1, {})

    def to_gt(n, ref, scale):
        for h in (0, 1):
            gt[n, rows_of(h), :] = low((ref[h] * scale).T)

    query_grads[1].merge(2)
    to_gt(1, gk, SCALE)
    query_grads[1].merge(1)
    to_gt(2, gv, 1.0)
    gt[0, :, tokens(1)] = low(query_grads[1].merge(3))

    def drain(half):
        def one(i, carry):
            for kind in range(4):
                for c in (0, 1):
                    tensor_copy(c, half, 4 * i + kind, g, kind, g).wait_send()
            return carry

        lax.fori_loop(0, 5, one, 0)

    both(drain)

    def target(half, d, e):
        return block(1 - half, d, e)

    def part(half, d, e, skip=0, count=160):
        start = target(half, d, e) * 320 + half * 160 + skip
        return go.at[pl.ds(pl.multiple_of(start, 16), count)]

    def multiply(dz):
        def one(i, carry):
            rows = pl.ds(pl.multiple_of(ring(z, dz) * 1280 + i * F, F), F)
            total = dot(wq[rows, :], gt[0]) + dot(wk[rows, :], gt[1])
            go[rows, :] = low(total + dot(wv[rows, :], gt[2]))
            return carry

        lax.fori_loop(0, 2, one, 0)

    def first(m, half, d, e, step):
        n = half * 12 + m
        return pltpu.make_async_remote_copy(
            src_ref=part(half, d, e), dst_ref=in1.at[n], send_sem=s1.at[n], recv_sem=r1.at[n],
            device_id={"tensor": target(half, step, 0)}, device_id_type=MESH,
        )

    def second(m, half, e, skip, step):
        n = half * 6 + m
        return pltpu.make_async_remote_copy(
            src_ref=part(half, 0, e, skip, 80), dst_ref=in2.at[n], send_sem=s2.at[n], recv_sem=r2.at[n],
            device_id={"tensor": target(half, 0, step)}, device_id_type=MESH,
        )

    far = ((0, 2, 2, 1), (1, 2, 1, -1), (2, 2, 3, 1), (3, 2, 0, -1))
    alone = ((4, 1, 1, 1), (5, 3, 2, -1), (6, 1, 0, 1), (7, 3, 3, -1))
    summed = ((8, 1, 2, 1), (9, 3, 1, -1), (10, 1, 3, 1), (11, 3, 0, -1))

    def send(half, messages):
        for m, d, e, step in messages:
            first(m, half, d, e, step).start()

    multiply(2)
    send(0, far)
    send(1, (far[0], alone[1]))
    multiply(1)
    send(1, (far[1],))
    send(0, (alone[0], alone[2]))
    send(1, (alone[0], ))
    multiply(3)
    send(1, (far[2], alone[3]))
    send(0, (alone[1], alone[3]))
    multiply(0)
    send(1, (far[3], alone[2]))

    def pass_on(m, d, e, step):
        def one(half):
            first(m - 8, half, d, e, step).wait_recv()
            ref = part(half, d, e)
            ref[...] = low(wide(ref[...]) + wide(in1[half * 12 + m - 8]))
            first(m, half, d, e, step).start()

        both(one)

    for message in summed:
        pass_on(*message)

    def collect(half, e, up, down):
        first(up, half, 0, e, 1).wait_recv()
        first(down, half, 0, e, 1).wait_recv()
        return wide(part(half, 0, e)[...]) + wide(in1[half * 12 + up]) + wide(in1[half * 12 + down])

    def collect_far(half):
        total = collect(half, 2, 8, 5)
        part(half, 0, 2)[...] = low(total)
        second(0, half, 2, 0, 1).start()
        second(1, half, 2, 80, -1).start()

    def collect_next(half):
        total = collect(half, 1, 4, 9)
        part(half, 0, 1)[...] = low(total)
        second(2, half, 1, 80, 1).start()
        total_low = total[0:80]
        second(0, half, 1, 0, 1).wait_recv()
        part(half, 0, 1, 0, 80)[...] = low(total_low + wide(in2[half * 6]))
        second(3, half, 1, 0, 1).start()

    def collect_last(half):
        total = collect(half, 3, 10, 7)
        part(half, 0, 3)[...] = low(total)
        second(4, half, 3, 0, -1).start()
        total_high = total[80:160]
        second(1, half, 3, 80, -1).wait_recv()
        part(half, 0, 3, 80, 80)[...] = low(total_high + wide(in2[half * 6 + 1]))
        second(5, half, 3, 80, -1).start()

    def collect_own(half):
        total = collect(half, 0, 6, 11)
        for m in (2, 3, 4, 5):
            second(m, half, 0, 0, 1).wait_recv()
        at = pl.multiple_of(half * 160, 16)
        n = half * 6
        out_ref[pl.ds(at, 80), :] = low(total[0:80] + (wide(in2[n + 3]) + wide(in2[n + 4])))
        out_ref[pl.ds(at + 80, 80), :] = low(total[80:160] + (wide(in2[n + 2]) + wide(in2[n + 5])))

    for step in (collect_far, collect_next, collect_last, collect_own):
        both(step)

    def sent1(m, carry):
        first(m, 0, 0, 0, 1).wait_send()
        return carry

    def sent2(m, carry):
        second(m, 0, 0, 0, 1).wait_send()
        return carry

    lax.fori_loop(0, 24, sent1, 0)
    lax.fori_loop(0, 12, sent2, 0)
    for item in (queries, blocks, *grads, *products, attended, *query_grads):
        item.drain()


def per_device(queries, keys, values, grad_out, frame_map, band, w_query, w_key, w_value, w_out):
    vmem = pl.BlockSpec(memory_space=pltpu.VMEM)
    hbm = pl.BlockSpec(memory_space=pl.ANY)
    smem = pl.BlockSpec(memory_space=pltpu.SMEM)
    bf16, f32 = jnp.bfloat16, jnp.float32
    gathered = pltpu.VMEM((8 * F, 256), bf16)
    weight = pltpu.VMEM((5120, 256), bf16)
    own = pltpu.VMEM((F, 256), bf16)
    turned = pltpu.VMEM((256, F), bf16)
    heads = pltpu.VMEM((2, F, HD), f32)
    scattered = [
        pltpu.VMEM((*rows, width), bf16)
        for width in (F, CHUNKS[0][1], CHUNKS[1][1])
        for rows in ((8 * 256,), (4, 256), (2, 128), (2, 256))
    ]
    sems = pltpu.SemaphoreType.DMA
    return pl.pallas_call(
        kernel,
        out_shape=jax.ShapeDtypeStruct((320, F), jnp.bfloat16),
        in_specs=[smem] * 2 + [hbm] * 8,
        out_specs=vmem,
        scratch_shapes=[
            pltpu.VMEM((5120, F), jnp.bfloat16),
            pltpu.VMEM((256, 5120), bf16),
            weight, weight, weight, gathered, gathered, own, own, turned, turned,
            pltpu.VMEM((64, F), f32),
            pltpu.VMEM((256, F), f32),
            pltpu.VMEM((128, F), f32),
            pltpu.VMEM((128, CHUNKS[0][1]), f32),
            pltpu.VMEM((128, CHUNKS[1][1]), f32),
            pltpu.VMEM((2, 8, F, F), bf16),
            pltpu.VMEM((F, F), jnp.int32),
            pltpu.VMEM((256, F), f32),
            pltpu.VMEM((256, F), f32),
            heads, heads, *scattered,
            pltpu.VMEM((3, 256, F), bf16),
            pltpu.VMEM((24, 160, F), jnp.bfloat16),
            pltpu.VMEM((12, 80, F), jnp.bfloat16),
            sems((8,)), sems((80,)), sems((80,)), sems((8 * ARRAYS,)), sems((8 * ARRAYS,)),
            sems((30,)), sems((30,)),
            sems((24,)), sems((24,)), sems((12,)), sems((12,)),
        ],
        compiler_params=pltpu.CompilerParams(
            collective_id=0, has_side_effects=True, vmem_limit_bytes=64 * 1024 * 1024
        ),
        cost_estimate=pl.CostEstimate(
            flops=21_000_000_000, bytes_accessed=14_000_000, transcendentals=13_000_000
        ),
    )(frame_map, band, grad_out.T, w_out, queries, keys, values, w_query, w_key, w_value)


def solution(mesh):
    placed = (
        P("tm", "tensor"),
        P("tm", "tensor"),
        P("tm", "tensor"),
        P("tm", "tensor"),
        P(),
        P(),
        P(None, "tensor"),
        P(None, "tensor"),
        P(None, "tensor"),
        P("tensor", None),
    )
    return jax.shard_map(
        per_device, mesh=mesh, in_specs=placed, out_specs=P("tensor", "tm"), check_vma=False
    )
```

```python
import jax
import jax.numpy as jnp
from jax import lax
from jax.experimental import pallas as pl
from jax.experimental.pallas import tpu as pltpu
from jax.sharding import PartitionSpec as P

HD = 128
F = 640
SCALE = HD ** -0.5
POWER = SCALE * 1.4426950408889634
ARRAYS = 6
MESH = pl.DeviceIdType.MESH
NT = (((1,), (1,)), ((), ()))
masked_score = -1e30


def dot(a, b):
    return jnp.dot(a, b, preferred_element_type=jnp.float32)


def dot_nt(a, b):
    return lax.dot_general(a, b, NT, preferred_element_type=jnp.float32)


def ring(position, step):
    return lax.rem(position + step + 4, 4)


def low(value):
    return value.astype(jnp.bfloat16)


def wide(value):
    return value.astype(jnp.float32)


def kernel(
    frame_map, band, go_hbm, wo_hbm, q_hbm, k_hbm, v_hbm, wq_hbm, wk_hbm, wv_hbm, out_ref,
    go, wo, kall, qall, vall, dall, vown, logs, dots, p, pt, dist, dacc, att, gq,
    tops, sums, row_dot, sbuf, gt, in1, in2,
    load_sem, zs, zr, ys, yr, s1, r1, s2, r2,
):
    g = lax.axis_index("tensor")
    z, x = g // 4, g % 4
    me = lax.axis_index("tm")
    y, core = me // 2, me % 2
    my_frame = frame_map[me]

    def slot_rows(s):
        return pl.ds(pl.multiple_of(s * F, F), F)

    mine = slot_rows(me)

    def load(n, src, dst):
        return pltpu.make_async_copy(src, dst, load_sem.at[n])

    loads = [
        load(0, go_hbm, go.at[pl.ds(pl.multiple_of(g * 320, 320), 320)]),
        load(1, k_hbm, kall.at[mine]),
        load(2, q_hbm, qall.at[mine]),
        load(3, v_hbm, vall.at[mine]),
        load(4, v_hbm, vown),
        load(5, wo_hbm, wo),
    ]
    for item in loads:
        item.start()

    def block(half, d, e):
        zz = ring(z, d * half + e * (1 - half))
        xx = ring(x, d * (1 - half) + e * half)
        return zz * 4 + xx

    def tensor_copy(half, m, j, kind, target):
        start = j * 320 + half * 160 + (80 if kind == 3 else 0)
        ref = go.at[pl.ds(pl.multiple_of(start, 16), 160 if kind < 2 else 80)]
        n = half * 20 + m
        return pltpu.make_async_remote_copy(
            src_ref=ref, dst_ref=ref, send_sem=zs.at[n], recv_sem=zr.at[n],
            device_id={"tensor": target}, device_id_type=MESH,
        )

    def both(step):
        def one(half, carry):
            step(half)
            return carry

        lax.fori_loop(0, 2, one, 0)

    def spread(half, index, d):
        j = block(half, d, 0)
        m = 4 + 4 * index
        tensor_copy(half, m, j, 0, block(half, 0, 1)).start()
        tensor_copy(half, m + 1, j, 1, block(half, 0, -1)).start()

    def tensor_start(half):
        tensor_copy(half, 0, g, 0, block(half, 1, 0)).start()
        tensor_copy(half, 1, g, 1, block(half, -1, 0)).start()

    def tensor_next(half):
        spread(half, 0, 0)

    def tensor_near(half):
        j = block(half, -1, 0)
        tensor_copy(half, 0, j, 0, g).wait_recv()
        tensor_copy(half, 2, j, 2, block(half, 1, 0)).start()
        spread(half, 1, -1)
        j = block(half, 1, 0)
        tensor_copy(half, 1, j, 1, g).wait_recv()
        tensor_copy(half, 3, j, 3, block(half, -1, 0)).start()
        spread(half, 2, 1)

    def tensor_far(half):
        j = block(half, 2, 0)
        tensor_copy(half, 2, j, 2, g).wait_recv()
        tensor_copy(half, 3, j, 3, g).wait_recv()
        spread(half, 3, 2)

    offsets = (0, -1, 1, 2)

    def forward(index):
        def step(half):
            m, d = 4 + 4 * index, offsets[index]
            j = block(half, d, -1)
            tensor_copy(half, m, j, 0, g).wait_recv()
            tensor_copy(half, m + 2, j, 2, block(half, 0, 1)).start()
            j = block(half, d, 1)
            tensor_copy(half, m + 1, j, 1, g).wait_recv()
            tensor_copy(half, m + 3, j, 3, block(half, 0, -1)).start()

        both(step)

    def finish(half, index):
        m, d = 4 + 4 * index, offsets[index]
        j = block(half, d, 2)
        tensor_copy(half, m + 2, j, 2, g).wait_recv()
        tensor_copy(half, m + 3, j, 3, g).wait_recv()

    columns = (slice(0, 256), slice(256, 512), slice(512, 640))

    def add_row(index):
        cols = pl.ds(pl.multiple_of(ring(z, offsets[index]) * 1280, 1280), 1280)
        for at in columns:
            dacc[:, at] += dot(wo[:, cols], go[cols, at])

    sibling = y * 2 + 1 - core

    def at_y(step):
        return ring(y, step) * 2 + core

    class Gather:
        def __init__(self, array, ref, rows):
            self.array, self.ref, self.rows = array, ref, rows

        def copy(self, m, slot, target):
            start, count = slot * self.rows, self.rows
            if m in (2, 3):
                count = self.rows // 2
                start = start + (m - 2) * count
            ref = self.ref.at[pl.ds(pl.multiple_of(start, count), count)]
            n = self.array * 8 + m
            return pltpu.make_async_remote_copy(
                src_ref=ref, dst_ref=ref, send_sem=ys.at[n], recv_sem=yr.at[n],
                device_id={"tm": target}, device_id_type=MESH,
            )

        def start(self):
            self.copy(0, me, at_y(1)).start()
            self.copy(1, me, at_y(-1)).start()
            self.copy(4, me, sibling).start()

        def near(self):
            self.copy(0, at_y(-1), me).wait_recv()
            self.copy(2, at_y(-1), at_y(1)).start()
            self.copy(5, at_y(-1), sibling).start()
            self.copy(1, at_y(1), me).wait_recv()
            self.copy(3, at_y(1), at_y(-1)).start()
            self.copy(6, at_y(1), sibling).start()

        def far(self):
            self.copy(2, at_y(2), me).wait_recv()
            self.copy(3, at_y(2), me).wait_recv()
            self.copy(7, at_y(2), sibling).start()

        def from_sibling(self, *messages):
            for m in messages:
                slot = ring(y, (0, -1, 1, 2)[m - 4]) * 2 + 1 - core
                self.copy(m, slot, me).wait_recv()

        def drain(self):
            for m in range(8):
                self.copy(m, me, me).wait_send()

    keys, queries = Gather(0, kall, F), Gather(1, qall, F)
    values, grads = Gather(2, vall, F), Gather(3, dall, F)
    totals, products = Gather(4, logs, 16), Gather(5, dots, 16)

    def by_arrival(gathers, body, events):
        def step(i, carry):
            n = i // 2
            ring_at = (n + 1) // 2
            hop = (ring_at % 2) * (2 * n - 3) + (ring_at // 2) * 2
            waits = {
                0: lambda item: item.from_sibling(4),
                2: lambda item: item.from_sibling(5),
                4: lambda item: item.from_sibling(6),
                5: lambda item: item.far(),
                6: lambda item: item.from_sibling(7),
            }
            for when in range(8):
                if when in waits or when in events:
                    @pl.when(i == when)
                    def _(when=when):
                        if when in events:
                            events[when]()
                        if when in waits:
                            for item in gathers:
                                waits[when](item)

            body(ring(y, hop), i % 2)
            return carry

        lax.fori_loop(0, 8, step, 0)

    lane = lax.broadcasted_iota(jnp.int32, (F, HD), 1)

    def pair_rows(n):
        return pl.ds(pl.multiple_of(n * 2 * F, 2 * F), 2 * F)

    def head(ref, rows, h):
        return ref[rows, pl.ds(pl.multiple_of(h * HD, HD), HD)]

    def stat_row(ref, n, h):
        one = ref[pl.ds(pl.multiple_of(n * 32 + h * 8, 8), 8), :][0:1, :]
        two = ref[pl.ds(pl.multiple_of(n * 32 + 16 + h * 8, 8), 8), :][0:1, :]
        return jnp.concatenate([one, two], axis=1)

    def to_row(ref, h, column):
        rows = pl.ds(pl.multiple_of(me * 16 + h * 8, 8), 8)
        ref[rows, :] = jnp.broadcast_to(column, (F, HD)).T[0:8, :]

    def factor(h, n):
        return jnp.sum(jnp.where(lane == n, sums[h], 0.0), axis=1, keepdims=True)

    def tile(t):
        return slice(t * 128, (t + 1) * 128)

    def chunk_rows(n, c):
        return pl.ds(pl.multiple_of(n * 2 * F + c * 256, 256), 256)

    def over_chunks(left, ref, n, h, work):
        ready = dot_nt(left, head(ref, chunk_rows(n, 0), h))
        for c in range(5):
            coming = dot_nt(left, head(ref, chunk_rows(n, c + 1), h)) if c < 4 else None
            work(c, ready)
            ready = coming

    def keep(value, t, widths):
        return jnp.where(dist[:, tile(t % 5)] <= widths[t // 5], value, masked_score)

    def softmax(n, h):
        widths = [band[my_frame, frame_map[2 * n + k]] for k in (0, 1)]
        best = [jnp.full((F, HD), masked_score, jnp.float32)]

        def work(c, scores):
            for k in (0, 1):
                t = 2 * c + k
                kept = keep(scores[:, tile(k)], t, widths)
                sbuf[:, tile(t)] = kept
                best[0] = jnp.maximum(best[0], kept)

        over_chunks(head(qall, mine, h), kall, n, h, work)
        top = jnp.max(best[0], axis=1, keepdims=True) * POWER
        total = jnp.zeros((F, HD), jnp.float32)
        for t in range(10):
            shifted = jnp.exp2(sbuf[:, tile(t)] * POWER - top)
            p[h, n, :, tile(t)] = low(shifted)
            total = total + shifted
        total = jnp.sum(total, axis=1, keepdims=True)
        tops[h] = jnp.where(lane == n, top, tops[h])
        sums[h] = jnp.where(lane == n, total, sums[h])

    def combine():
        for h in (0, 1):
            top = jnp.max(tops[h], axis=1, keepdims=True)
            shares = jnp.exp2(tops[h] - top)
            total = jnp.sum(shares * sums[h], axis=1, keepdims=True)
            sums[h] = shares / total
            to_row(logs, h, top + jnp.log2(total))

    def key_side(n, h):
        widths = [band[frame_map[2 * n + k], my_frame] for k in (0, 1)]
        log_row = stat_row(logs, n, h)

        def work(c, scores):
            for k in (0, 1):
                t = 2 * c + k
                power = keep(scores[:, tile(k)] * POWER - log_row[:, tile(t)], t, widths)
                pt[h, n, :, tile(t)] = low(jnp.exp2(power))

        over_chunks(head(kall, mine, h), qall, n, h, work)

    def attend(n, h):
        att[h] += factor(h, n) * dot(p[h, n], head(vall, pair_rows(n), h))

    def query_grad(n, h):
        own = row_dot[h]
        total = [jnp.zeros((F, HD), jnp.float32)]

        def work(c, grad):
            grad = jnp.concatenate([low(grad[:, tile(k)] - own) for k in (0, 1)], axis=1)
            weight = p[h, n, :, c * 256:(c + 1) * 256]
            total[0] = total[0] + dot(weight * grad, head(kall, chunk_rows(n, c), h))

        over_chunks(head(dall, mine, h), vall, n, h, work)
        gq[h] += factor(h, n) * total[0]

    def key_grad(n, h):
        own_row = stat_row(dots, n, h)
        total = [jnp.zeros((F, HD), jnp.float32)] * 2

        def work(c, grad):
            at = slice(c * 256, (c + 1) * 256)
            weight = pt[h, n, :, at]
            total[1] = total[1] + dot(weight, head(dall, chunk_rows(n, c), h))
            grad = weight * low(grad - own_row[:, at])
            total[0] = total[0] + dot(grad, head(qall, chunk_rows(n, c), h))

        over_chunks(head(vown, slice(None), h), dall, n, h, work)
        gk[h] += total[0]
        gv[h] += total[1]

    barrier = pltpu.get_barrier_semaphore()
    for half in (0, 1):
        for step in (1, -1):
            pl.semaphore_signal(
                barrier, inc=1, device_id={"tensor": block(half, step, 0)}, device_id_type=MESH
            )
    for target in (at_y(1), at_y(-1), sibling):
        pl.semaphore_signal(barrier, inc=1, device_id={"tm": target}, device_id_type=MESH)
    loads[0].wait()
    loads[1].wait()
    pl.semaphore_wait(barrier, 7)
    both(tensor_start)
    keys.start()
    both(tensor_next)
    across = lax.broadcasted_iota(jnp.int32, (F, F), 0) - lax.broadcasted_iota(jnp.int32, (F, F), 1)
    dist[...] = jnp.abs(across)
    for ref in (dacc, att, gq, sums):
        ref[...] = jnp.zeros_like(ref)
    tops[...] = jnp.full_like(tops, masked_score)
    for item in loads[2:]:
        item.wait()

    def keys_near():
        both(tensor_near)
        keys.near()
        queries.start()

    by_arrival(
        (keys,), softmax,
        {2: keys_near, 5: lambda: both(tensor_far), 7: lambda: forward(0)},
    )
    combine()
    totals.start()

    def queries_near():
        queries.near()
        values.start()
        totals.near()

    by_arrival(
        (queries, totals), key_side,
        {2: queries_near, 4: lambda: forward(1), 7: lambda: forward(2)},
    )
    forward(3)

    def values_near():
        values.near()

    by_arrival((values,), attend, {2: values_near})
    for index in range(4):
        finish(0, index)
    for index in range(4):
        finish(1, index)
        add_row(index)
    dall[mine, :] = low(dacc[...].T)
    grads.start()
    for h in (0, 1):
        column = jnp.sum(wide(head(dall, mine, h)) * att[h], axis=1, keepdims=True)
        row_dot[h] = jnp.broadcast_to(column, (F, HD))
        to_row(dots, h, column)
    products.start()
    gk, gv = tops, att
    for ref in (gk, gv):
        ref[...] = jnp.zeros_like(ref)

    def query_step(i, carry):
        query_grad(i // 2, i % 2)

        @pl.when(i == 5)
        def _():
            grads.near()
            products.near()

        return carry

    lax.fori_loop(0, 8, query_step, 0)
    keys.drain()
    values.drain()
    loads = [load(0, wq_hbm, kall), load(1, wk_hbm, vall)]
    for item in loads:
        item.start()
    def to_gt(n, ref, scale):
        for h in (0, 1):
            gt[n * 256 + h * HD:n * 256 + (h + 1) * HD, :] = low((ref[h] * scale).T)

    to_gt(0, gq, SCALE)
    by_arrival((grads, products), key_grad, {})
    queries.drain()
    loads.append(load(2, wv_hbm, qall))
    loads[2].start()
    to_gt(1, gk, SCALE)
    to_gt(2, gv, 1.0)
    for item in loads:
        item.wait()

    def drain(half):
        def one(i, carry):
            for kind in range(4):
                tensor_copy(half, 4 * i + kind, g, kind, g).wait_send()
            return carry

        lax.fori_loop(0, 5, one, 0)

    both(drain)

    def target(half, d, e):
        return block(1 - half, d, e)

    def part(half, d, e, skip=0, count=160):
        start = target(half, d, e) * 320 + half * 160 + skip
        return go.at[pl.ds(pl.multiple_of(start, 16), count)]

    def multiply(dz):
        def one(i, carry):
            rows = pl.ds(pl.multiple_of(ring(z, dz) * 1280 + i * 320, 320), 320)
            left = jnp.concatenate([kall[rows, :], vall[rows, :], qall[rows, :]], axis=1)
            for at in columns:
                go[rows, at] = low(dot(left, gt[:, at]))
            return carry

        lax.fori_loop(0, 4, one, 0)

    def first(m, half, d, e, step):
        n = half * 12 + m
        return pltpu.make_async_remote_copy(
            src_ref=part(half, d, e), dst_ref=in1.at[n], send_sem=s1.at[n], recv_sem=r1.at[n],
            device_id={"tensor": target(half, step, 0)}, device_id_type=MESH,
        )

    def second(m, half, e, skip, step):
        n = half * 6 + m
        return pltpu.make_async_remote_copy(
            src_ref=part(half, 0, e, skip, 80), dst_ref=in2.at[n], send_sem=s2.at[n], recv_sem=r2.at[n],
            device_id={"tensor": target(half, 0, step)}, device_id_type=MESH,
        )

    far = ((0, 2, 2, 1), (1, 2, 1, -1), (2, 2, 3, 1), (3, 2, 0, -1))
    alone = ((4, 1, 1, 1), (5, 3, 2, -1), (6, 1, 0, 1), (7, 3, 3, -1))
    summed = ((8, 1, 2, 1), (9, 3, 1, -1), (10, 1, 3, 1), (11, 3, 0, -1))

    def send(half, messages):
        for m, d, e, step in messages:
            first(m, half, d, e, step).start()

    multiply(2)
    send(0, far)
    send(1, (far[0], alone[1]))
    multiply(1)
    send(1, (far[1],))
    send(0, (alone[0], alone[2]))
    send(1, (alone[0], ))
    multiply(3)
    send(1, (far[2], alone[3]))
    send(0, (alone[1], alone[3]))
    multiply(0)
    send(1, (far[3], alone[2]))

    def pass_on(m, d, e, step):
        def one(half):
            first(m - 8, half, d, e, step).wait_recv()
            ref = part(half, d, e)
            ref[...] = low(wide(ref[...]) + wide(in1[half * 12 + m - 8]))
            first(m, half, d, e, step).start()

        both(one)

    for message in summed:
        pass_on(*message)

    def collect(half, e, up, down):
        first(up, half, 0, e, 1).wait_recv()
        first(down, half, 0, e, 1).wait_recv()
        return wide(part(half, 0, e)[...]) + wide(in1[half * 12 + up]) + wide(in1[half * 12 + down])

    def collect_far(half):
        total = collect(half, 2, 8, 5)
        part(half, 0, 2)[...] = low(total)
        second(0, half, 2, 0, 1).start()
        second(1, half, 2, 80, -1).start()

    def collect_next(half):
        total = collect(half, 1, 4, 9)
        part(half, 0, 1)[...] = low(total)
        second(2, half, 1, 80, 1).start()
        total_low = total[0:80]
        second(0, half, 1, 0, 1).wait_recv()
        part(half, 0, 1, 0, 80)[...] = low(total_low + wide(in2[half * 6]))
        second(3, half, 1, 0, 1).start()

    def collect_last(half):
        total = collect(half, 3, 10, 7)
        part(half, 0, 3)[...] = low(total)
        second(4, half, 3, 0, -1).start()
        total_high = total[80:160]
        second(1, half, 3, 80, -1).wait_recv()
        part(half, 0, 3, 80, 80)[...] = low(total_high + wide(in2[half * 6 + 1]))
        second(5, half, 3, 80, -1).start()

    def collect_own(half):
        total = collect(half, 0, 6, 11)
        for m in (2, 3, 4, 5):
            second(m, half, 0, 0, 1).wait_recv()
        at = pl.multiple_of(half * 160, 16)
        n = half * 6
        out_ref[pl.ds(at, 80), :] = low(total[0:80] + (wide(in2[n + 3]) + wide(in2[n + 4])))
        out_ref[pl.ds(at + 80, 80), :] = low(total[80:160] + (wide(in2[n + 2]) + wide(in2[n + 5])))

    for step in (collect_far, collect_next, collect_last, collect_own):
        both(step)

    def sent1(m, carry):
        first(m, 0, 0, 0, 1).wait_send()
        return carry

    def sent2(m, carry):
        second(m, 0, 0, 0, 1).wait_send()
        return carry

    lax.fori_loop(0, 24, sent1, 0)
    lax.fori_loop(0, 12, sent2, 0)
    for item in (grads, totals, products):
        item.drain()


def per_device(queries, keys, values, grad_out, frame_map, band, w_query, w_key, w_value, w_out):
    vmem = pl.BlockSpec(memory_space=pltpu.VMEM)
    hbm = pl.BlockSpec(memory_space=pl.ANY)
    smem = pl.BlockSpec(memory_space=pltpu.SMEM)
    gathered = pltpu.VMEM((8 * F, 256), jnp.bfloat16)
    stats = pltpu.VMEM((128, F), jnp.float32)
    pairs = pltpu.VMEM((2, 4, F, 2 * F), jnp.bfloat16)
    heads = pltpu.VMEM((2, F, HD), jnp.float32)
    sems = pltpu.SemaphoreType.DMA
    return pl.pallas_call(
        kernel,
        out_shape=jax.ShapeDtypeStruct((320, F), jnp.bfloat16),
        in_specs=[smem] * 2 + [hbm] * 8,
        out_specs=vmem,
        scratch_shapes=[
            pltpu.VMEM((5120, F), jnp.bfloat16),
            pltpu.VMEM((256, 5120), jnp.bfloat16),
            gathered, gathered, gathered, gathered,
            pltpu.VMEM((F, 256), jnp.bfloat16),
            stats, stats,
            pairs, pairs,
            pltpu.VMEM((F, F), jnp.int32),
            pltpu.VMEM((256, F), jnp.float32),
            heads, heads, heads, heads, heads,
            pltpu.VMEM((F, 2 * F), jnp.float32),
            pltpu.VMEM((768, F), jnp.bfloat16),
            pltpu.VMEM((24, 160, F), jnp.bfloat16),
            pltpu.VMEM((12, 80, F), jnp.bfloat16),
            sems((6,)), sems((40,)), sems((40,)), sems((8 * ARRAYS,)), sems((8 * ARRAYS,)),
            sems((24,)), sems((24,)), sems((12,)), sems((12,)),
        ],
        compiler_params=pltpu.CompilerParams(
            collective_id=0, has_side_effects=True, vmem_limit_bytes=64 * 1024 * 1024
        ),
        cost_estimate=pl.CostEstimate(
            flops=21_000_000_000, bytes_accessed=14_000_000, transcendentals=13_000_000
        ),
    )(frame_map, band, grad_out.T, w_out, queries, keys, values, w_query, w_key, w_value)


def solution(mesh):
    placed = (
        P("tm", "tensor"),
        P("tm", "tensor"),
        P("tm", "tensor"),
        P("tm", "tensor"),
        P(),
        P(),
        P(None, "tensor"),
        P(None, "tensor"),
        P(None, "tensor"),
        P("tensor", None),
    )
    return jax.shard_map(
        per_device, mesh=mesh, in_specs=placed, out_specs=P("tensor", "tm"), check_vma=False
    )
```

```python
import jax
import jax.numpy as jnp
from jax import lax
from jax.experimental import pallas as pl
from jax.experimental.pallas import tpu as pltpu
from jax.sharding import PartitionSpec as P

HD = 128
F = 640
SCALE = HD ** -0.5
POWER = SCALE * 1.4426950408889634
CHUNKS = ((0, 384), (384, 256))
ARRAYS = 6
MESH = pl.DeviceIdType.MESH
NT = (((1,), (1,)), ((), ()))
masked_score = -1e30


def dot(a, b):
    return jnp.dot(a, b, preferred_element_type=jnp.float32)


def dot_nt(a, b):
    return lax.dot_general(a, b, NT, preferred_element_type=jnp.float32)


def ring(position, step):
    return lax.rem(position + step + 4, 4)


def low(value):
    return value.astype(jnp.bfloat16)


def wide(value):
    return value.astype(jnp.float32)


def kernel(
    frame_map, band, go_hbm, wo_hbm, q_hbm, k_hbm, v_hbm, wq_hbm, wk_hbm, wv_hbm, out_ref,
    go, wo, kall, qall, vall, dall, logs, dots, p, pt, dist, dacc, att, gq,
    tops, sums, row_dot, gt, wbuf, in1, in2,
    load_sem, zs, zr, ys, yr, wsem, s1, r1, s2, r2,
):
    g = lax.axis_index("tensor")
    z, x = g // 4, g % 4
    me = lax.axis_index("tm")
    y, core = me // 2, me % 2
    my_frame = frame_map[me]

    def slot_rows(s):
        return pl.ds(pl.multiple_of(s * F, F), F)

    mine = slot_rows(me)

    def load(n, src, dst):
        return pltpu.make_async_copy(src, dst, load_sem.at[n])

    loads = [
        load(0, go_hbm, go.at[pl.ds(pl.multiple_of(g * 320, 320), 320)]),
        load(1, k_hbm, kall.at[mine]),
        load(2, q_hbm, qall.at[mine]),
        load(3, v_hbm, vall.at[mine]),
        load(4, wo_hbm, wo),
    ]
    for item in loads:
        item.start()

    def block(half, d, e):
        zz = ring(z, d * half + e * (1 - half))
        xx = ring(x, d * (1 - half) + e * half)
        return zz * 4 + xx

    def tensor_copy(half, m, j, kind, target):
        start = j * 320 + half * 160 + (80 if kind == 3 else 0)
        ref = go.at[pl.ds(pl.multiple_of(start, 16), 160 if kind < 2 else 80)]
        n = half * 20 + m
        return pltpu.make_async_remote_copy(
            src_ref=ref, dst_ref=ref, send_sem=zs.at[n], recv_sem=zr.at[n],
            device_id={"tensor": target}, device_id_type=MESH,
        )

    def both(step):
        def one(half, carry):
            step(half)
            return carry

        lax.fori_loop(0, 2, one, 0)

    def spread(half, index, d):
        j = block(half, d, 0)
        m = 4 + 4 * index
        tensor_copy(half, m, j, 0, block(half, 0, 1)).start()
        tensor_copy(half, m + 1, j, 1, block(half, 0, -1)).start()

    def tensor_start(half):
        tensor_copy(half, 0, g, 0, block(half, 1, 0)).start()
        tensor_copy(half, 1, g, 1, block(half, -1, 0)).start()

    def tensor_next(half):
        spread(half, 0, 0)

    def tensor_near(half):
        j = block(half, -1, 0)
        tensor_copy(half, 0, j, 0, g).wait_recv()
        tensor_copy(half, 2, j, 2, block(half, 1, 0)).start()
        spread(half, 1, -1)
        j = block(half, 1, 0)
        tensor_copy(half, 1, j, 1, g).wait_recv()
        tensor_copy(half, 3, j, 3, block(half, -1, 0)).start()
        spread(half, 2, 1)

    def tensor_far(half):
        j = block(half, 2, 0)
        tensor_copy(half, 2, j, 2, g).wait_recv()
        tensor_copy(half, 3, j, 3, g).wait_recv()
        spread(half, 3, 2)

    offsets = (0, -1, 1, 2)

    def forward(index):
        def step(half):
            m, d = 4 + 4 * index, offsets[index]
            j = block(half, d, -1)
            tensor_copy(half, m, j, 0, g).wait_recv()
            tensor_copy(half, m + 2, j, 2, block(half, 0, 1)).start()
            j = block(half, d, 1)
            tensor_copy(half, m + 1, j, 1, g).wait_recv()
            tensor_copy(half, m + 3, j, 3, block(half, 0, -1)).start()

        both(step)

    def finish(half, index):
        m, d = 4 + 4 * index, offsets[index]
        j = block(half, d, 2)
        tensor_copy(half, m + 2, j, 2, g).wait_recv()
        tensor_copy(half, m + 3, j, 3, g).wait_recv()

    def add_row(index):
        cols = pl.ds(pl.multiple_of(ring(z, offsets[index]) * 1280, 1280), 1280)
        dacc[...] += dot(wo[:, cols], go[cols, :])

    sibling = y * 2 + 1 - core

    def at_y(step):
        return ring(y, step) * 2 + core

    class Gather:
        def __init__(self, array, ref, rows):
            self.array, self.ref, self.rows = array, ref, rows

        def copy(self, m, slot, target):
            start, count = slot * self.rows, self.rows
            if m in (2, 3):
                count = self.rows // 2
                start = start + (m - 2) * count
            ref = self.ref.at[pl.ds(pl.multiple_of(start, count), count)]
            n = self.array * 8 + m
            return pltpu.make_async_remote_copy(
                src_ref=ref, dst_ref=ref, send_sem=ys.at[n], recv_sem=yr.at[n],
                device_id={"tm": target}, device_id_type=MESH,
            )

        def start(self):
            self.copy(0, me, at_y(1)).start()
            self.copy(1, me, at_y(-1)).start()
            self.copy(4, me, sibling).start()

        def near(self):
            self.copy(0, at_y(-1), me).wait_recv()
            self.copy(2, at_y(-1), at_y(1)).start()
            self.copy(5, at_y(-1), sibling).start()
            self.copy(1, at_y(1), me).wait_recv()
            self.copy(3, at_y(1), at_y(-1)).start()
            self.copy(6, at_y(1), sibling).start()

        def far(self):
            self.copy(2, at_y(2), me).wait_recv()
            self.copy(3, at_y(2), me).wait_recv()
            self.copy(7, at_y(2), sibling).start()

        def from_sibling(self, *messages):
            for m in messages:
                slot = ring(y, (0, -1, 1, 2)[m - 4]) * 2 + 1 - core
                self.copy(m, slot, me).wait_recv()

        def drain(self):
            for m in range(8):
                self.copy(m, me, me).wait_send()

    keys, queries = Gather(0, kall, F), Gather(1, qall, F)
    values, grads = Gather(2, vall, F), Gather(3, dall, F)
    totals, products = Gather(4, logs, 16), Gather(5, dots, 16)

    def by_arrival(gathers, body, events):
        def step(n, carry):
            ring_at = (n + 2) // 4
            hop = (ring_at % 2) * (2 * (n % 2) - 1) + (ring_at // 2) * 2
            other = (1 - ring_at % 2) * (n % 2) + (ring_at % 2) * (((n + 2) // 2) % 2)
            slot = ring(y, hop) * 2 + (core + other) % 2
            waits = {
                1: lambda item: item.from_sibling(4),
                4: lambda item: item.from_sibling(5, 6),
                6: lambda item: item.far(),
                7: lambda item: item.from_sibling(7),
            }
            for when in range(8):
                if when in waits or when in events:
                    @pl.when(n == when)
                    def _(when=when):
                        if when in events:
                            events[when]()
                        if when in waits:
                            for item in gathers:
                                waits[when](item)

            body(slot)
            return carry

        lax.fori_loop(0, 8, step, 0)

    lane = lax.broadcasted_iota(jnp.int32, (F, HD), 1)

    def head(ref, rows, h):
        return ref[rows, h * HD:(h + 1) * HD]

    def stat_row(ref, s, h):
        return ref[pl.ds(pl.multiple_of(s * 16 + h * 8, 8), 8), :][0:1, :]

    def to_row(ref, h, column):
        rows = pl.ds(pl.multiple_of(me * 16 + h * 8, 8), 8)
        ref[rows, :] = jnp.broadcast_to(column, (F, HD)).T[0:8, :]

    def factor(h, s, at=0, count=F):
        own = sums[h, at:at + count, :]
        return jnp.sum(jnp.where(lane[at:at + count] == s, own, 0.0), axis=1, keepdims=True)

    def softmax(s):
        width = band[my_frame, frame_map[s]]
        for h in (0, 1):
            scores = dot_nt(head(qall, mine, h), head(kall, slot_rows(s), h))
            scores = jnp.where(dist[...] <= width, scores, masked_score)
            top = jnp.max(scores, axis=1, keepdims=True) * POWER
            shifted = jnp.exp2(scores * POWER - top)
            total = jnp.sum(shifted, axis=1, keepdims=True)
            p[h, s] = low(shifted)
            tops[h] = jnp.where(lane == s, top, tops[h])
            sums[h] = jnp.where(lane == s, total, sums[h])

    def combine():
        for h in (0, 1):
            top = jnp.max(tops[h], axis=1, keepdims=True)
            shares = jnp.exp2(tops[h] - top)
            total = jnp.sum(shares * sums[h], axis=1, keepdims=True)
            sums[h] = shares / total
            to_row(logs, h, top + jnp.log2(total))

    def key_side(s):
        width = band[frame_map[s], my_frame]
        for h in (0, 1):
            scores = dot_nt(head(kall, mine, h), head(qall, slot_rows(s), h))
            power = jnp.where(
                dist[...] <= width, scores * POWER - stat_row(logs, s, h), masked_score
            )
            pt[h, s] = low(jnp.exp2(power))

    def attend(s):
        for h in (0, 1):
            att[h] += factor(h, s) * dot(p[h, s], head(vall, slot_rows(s), h))

    def query_grad(c, s):
        at, count = CHUNKS[c]
        rows, own = pl.ds(at, count), pl.ds(pl.multiple_of(me * F + at, 128), count)
        for h in (0, 1):
            grad = dot_nt(head(dall, own, h), head(vall, slot_rows(s), h))
            grad = low(grad - jnp.concatenate([row_dot[h, rows, :]] * 5, axis=1))
            product = dot(p[h, s, rows, :] * grad, head(kall, slot_rows(s), h))
            gq[h, rows, :] += factor(h, s, at, count) * product

    def key_grad(c, s):
        at, count = CHUNKS[c]
        rows, own = pl.ds(at, count), pl.ds(pl.multiple_of(me * F + at, 128), count)
        for h in (0, 1):
            grad_rows = head(dall, slot_rows(s), h)
            weight = pt[h, s, rows, :]
            grad = low(dot_nt(head(vall, own, h), grad_rows) - stat_row(dots, s, h))
            gv[h, rows, :] += dot(weight, grad_rows)
            gk[h, rows, :] += dot(weight * grad, head(qall, slot_rows(s), h))

    barrier = pltpu.get_barrier_semaphore()
    for half in (0, 1):
        for step in (1, -1):
            pl.semaphore_signal(
                barrier, inc=1, device_id={"tensor": block(half, step, 0)}, device_id_type=MESH
            )
    for target in (at_y(1), at_y(-1), sibling):
        pl.semaphore_signal(barrier, inc=1, device_id={"tm": target}, device_id_type=MESH)
    loads[0].wait()
    loads[1].wait()
    pl.semaphore_wait(barrier, 7)
    both(tensor_start)
    keys.start()
    both(tensor_next)
    across = lax.broadcasted_iota(jnp.int32, (F, F), 0) - lax.broadcasted_iota(jnp.int32, (F, F), 1)
    dist[...] = jnp.abs(across)
    for ref in (dacc, att, gq, sums):
        ref[...] = jnp.zeros_like(ref)
    tops[...] = jnp.full_like(tops, masked_score)
    for item in loads[2:]:
        item.wait()

    def keys_near():
        both(tensor_near)
        keys.near()
        queries.start()

    by_arrival(
        (keys,), softmax,
        {2: keys_near, 5: lambda: both(tensor_far), 7: lambda: forward(0)},
    )
    combine()
    totals.start()

    def queries_near():
        queries.near()
        values.start()
        totals.near()

    by_arrival(
        (queries, totals), key_side,
        {2: queries_near, 4: lambda: forward(1), 7: lambda: forward(2)},
    )
    forward(3)

    def values_near():
        values.near()

    by_arrival((values,), attend, {2: values_near})
    for index in range(4):
        finish(0, index)
    for index in range(4):
        finish(1, index)
        add_row(index)
    dall[mine, :] = low(dacc[...].T)
    grads.start()
    for h in (0, 1):
        column = jnp.sum(wide(head(dall, mine, h)) * att[h], axis=1, keepdims=True)
        row_dot[h] = jnp.broadcast_to(column, (F, HD))
        to_row(dots, h, column)
    products.start()
    gk, gv = tops, att
    for ref in (gk, gv):
        ref[...] = jnp.zeros_like(ref)

    def to_gt(n, ref, scale, c):
        rows = pl.ds(*CHUNKS[c])
        for h in (0, 1):
            gt[n * 256 + h * HD:n * 256 + (h + 1) * HD, rows] = low((ref[h, rows, :] * scale).T)

    def drain(half):
        def one(i, carry):
            for kind in range(4):
                tensor_copy(half, 4 * i + kind, g, kind, g).wait_send()
            return carry

        lax.fori_loop(0, 5, one, 0)

    def target(half, d, e):
        return block(1 - half, d, e)

    def part(c, half, d, e, skip=0, count=160):
        start = target(half, d, e) * 320 + half * 160 + skip
        return go.at[pl.ds(pl.multiple_of(start, 16), count), pl.ds(*CHUNKS[c])]

    def got(c, ref, n):
        return wide(ref[n, :, pl.ds(*CHUNKS[c])])

    def first(c, m, half, d, e, step):
        n = half * 12 + m
        return pltpu.make_async_remote_copy(
            src_ref=part(c, half, d, e), dst_ref=in1.at[n, :, pl.ds(*CHUNKS[c])],
            send_sem=s1.at[c * 24 + n], recv_sem=r1.at[c * 24 + n],
            device_id={"tensor": target(half, step, 0)}, device_id_type=MESH,
        )

    def second(c, m, half, e, skip, step):
        n = half * 6 + m
        return pltpu.make_async_remote_copy(
            src_ref=part(c, half, 0, e, skip, 80), dst_ref=in2.at[n, :, pl.ds(*CHUNKS[c])],
            send_sem=s2.at[c * 12 + n], recv_sem=r2.at[c * 12 + n],
            device_id={"tensor": target(half, 0, step)}, device_id_type=MESH,
        )

    far = ((0, 2, 2, 1), (1, 2, 1, -1), (2, 2, 3, 1), (3, 2, 0, -1))
    alone = ((4, 1, 1, 1), (5, 3, 2, -1), (6, 1, 0, 1), (7, 3, 3, -1))
    summed = ((8, 1, 2, 1), (9, 3, 1, -1), (10, 1, 3, 1), (11, 3, 0, -1))

    def send(c, half, messages):
        for m, d, e, step in messages:
            first(c, m, half, d, e, step).start()

    def block_rows(j):
        k = j // 2
        dz = (k % 2) * (1 - k // 2) + (1 - k % 2) * (2 + k // 2)
        return pl.ds(pl.multiple_of(ring(z, dz) * 1280 + (j % 2) * F, F), F)

    def fetch(j):
        return [
            pltpu.make_async_copy(src.at[block_rows(j)], wbuf.at[j % 2, n], wsem.at[j % 2, n])
            for n, src in enumerate((wq_hbm, wk_hbm, wv_hbm))
        ]

    def start_fetch(j):
        for item in fetch(j):
            item.start()

    def multiply(c):
        tokens = pl.ds(*CHUNKS[c])

        def one(j, carry):
            for item in fetch(j):
                item.wait()

            @pl.when(j < 7)
            def _():
                start_fetch(j + 1)

            left = jnp.concatenate([wbuf[j % 2, n] for n in range(3)], axis=1)
            go[block_rows(j), tokens] = low(dot(left, gt[:, tokens]))
            events = {
                1: ((0, far), (1, (far[0], alone[1]))),
                3: ((1, (far[1], alone[0])), (0, (alone[0], alone[2]))),
                5: ((1, (far[2], alone[3])), (0, (alone[1], alone[3]))),
                7: ((1, (far[3], alone[2])),),
            }
            for when in events:
                @pl.when(j == when)
                def _(when=when):
                    for half, messages in events[when]:
                        send(c, half, messages)

            return carry

        lax.fori_loop(0, 8, one, 0)

    def pass_on(c, message):
        m, d, e, step = message

        def one(half):
            first(c, m - 8, half, d, e, step).wait_recv()
            ref = part(c, half, d, e)
            ref[...] = low(wide(ref[...]) + got(c, in1, half * 12 + m - 8))
            first(c, m, half, d, e, step).start()

        both(one)

    def collect(c, half, e, up, down):
        first(c, up, half, 0, e, 1).wait_recv()
        first(c, down, half, 0, e, 1).wait_recv()
        return wide(part(c, half, 0, e)[...]) + got(c, in1, half * 12 + up) + got(c, in1, half * 12 + down)

    def collect_far(c, half):
        part(c, half, 0, 2)[...] = low(collect(c, half, 2, 8, 5))
        second(c, 0, half, 2, 0, 1).start()
        second(c, 1, half, 2, 80, -1).start()

    def collect_next(c, half):
        total = collect(c, half, 1, 4, 9)
        part(c, half, 0, 1)[...] = low(total)
        second(c, 2, half, 1, 80, 1).start()
        second(c, 0, half, 1, 0, 1).wait_recv()
        part(c, half, 0, 1, 0, 80)[...] = low(total[0:80] + got(c, in2, half * 6))
        second(c, 3, half, 1, 0, 1).start()

    def collect_last(c, half):
        total = collect(c, half, 3, 10, 7)
        part(c, half, 0, 3)[...] = low(total)
        second(c, 4, half, 3, 0, -1).start()
        second(c, 1, half, 3, 80, -1).wait_recv()
        part(c, half, 0, 3, 80, 80)[...] = low(total[80:160] + got(c, in2, half * 6 + 1))
        second(c, 5, half, 3, 80, -1).start()

    def collect_own(c, half):
        total = collect(c, half, 0, 6, 11)
        for m in (2, 3, 4, 5):
            second(c, m, half, 0, 0, 1).wait_recv()
        at = pl.multiple_of(half * 160, 16)
        n, tokens = half * 6, pl.ds(*CHUNKS[c])
        out_ref[pl.ds(at, 80), tokens] = low(total[0:80] + (got(c, in2, n + 3) + got(c, in2, n + 4)))
        out_ref[pl.ds(at + 80, 80), tokens] = low(
            total[80:160] + (got(c, in2, n + 2) + got(c, in2, n + 5))
        )

    def scatter_steps(c):
        steps = [lambda message=message: pass_on(c, message) for message in summed]
        for collector in (collect_far, collect_next, collect_last, collect_own):
            steps.append(lambda collector=collector: both(lambda half: collector(c, half)))
        return steps

    def eight(body, events):
        def one(s, carry):
            body(s)
            for when in events:
                @pl.when(s == when)
                def _(when=when):
                    events[when]()

            return carry

        lax.fori_loop(0, 8, one, 0)

    def grads_near():
        grads.near()
        products.near()

    start_fetch(0)
    eight(lambda s: query_grad(0, s), {6: grads_near})
    to_gt(0, gq, SCALE, 0)
    both(drain)
    by_arrival((grads, products), lambda s: key_grad(0, s), {})
    to_gt(1, gk, SCALE, 0)
    to_gt(2, gv, 1.0, 0)
    multiply(0)
    start_fetch(0)
    steps = scatter_steps(0)
    eight(lambda s: query_grad(1, s), {3: steps[0], 4: steps[1], 5: steps[2], 6: steps[3]})
    to_gt(0, gq, SCALE, 1)
    eight(lambda s: key_grad(1, s), {1: steps[4], 3: steps[5], 5: steps[6], 7: steps[7]})
    to_gt(1, gk, SCALE, 1)
    to_gt(2, gv, 1.0, 1)
    multiply(1)
    for step in scatter_steps(1):
        step()

    def sent1(m, carry):
        for c in (0, 1):
            first(c, m, 0, 0, 0, 1).wait_send()
        return carry

    def sent2(m, carry):
        for c in (0, 1):
            second(c, m, 0, 0, 0, 1).wait_send()
        return carry

    lax.fori_loop(0, 24, sent1, 0)
    lax.fori_loop(0, 12, sent2, 0)
    for item in (keys, queries, values, grads, totals, products):
        item.drain()


def per_device(queries, keys, values, grad_out, frame_map, band, w_query, w_key, w_value, w_out):
    vmem = pl.BlockSpec(memory_space=pltpu.VMEM)
    hbm = pl.BlockSpec(memory_space=pl.ANY)
    smem = pl.BlockSpec(memory_space=pltpu.SMEM)
    gathered = pltpu.VMEM((8 * F, 256), jnp.bfloat16)
    stats = pltpu.VMEM((128, F), jnp.float32)
    pairs = pltpu.VMEM((2, 8, F, F), jnp.bfloat16)
    heads = pltpu.VMEM((2, F, HD), jnp.float32)
    sems = pltpu.SemaphoreType.DMA
    return pl.pallas_call(
        kernel,
        out_shape=jax.ShapeDtypeStruct((320, F), jnp.bfloat16),
        in_specs=[smem] * 2 + [hbm] * 8,
        out_specs=vmem,
        scratch_shapes=[
            pltpu.VMEM((5120, F), jnp.bfloat16),
            pltpu.VMEM((256, 5120), jnp.bfloat16),
            gathered, gathered, gathered, gathered,
            stats, stats,
            pairs, pairs,
            pltpu.VMEM((F, F), jnp.int32),
            pltpu.VMEM((256, F), jnp.float32),
            heads, heads, heads, heads, heads,
            pltpu.VMEM((768, F), jnp.bfloat16),
            pltpu.VMEM((2, 3, F, 256), jnp.bfloat16),
            pltpu.VMEM((24, 160, F), jnp.bfloat16),
            pltpu.VMEM((12, 80, F), jnp.bfloat16),
            sems((6,)), sems((40,)), sems((40,)), sems((8 * ARRAYS,)), sems((8 * ARRAYS,)),
            sems((2, 3)), sems((48,)), sems((48,)), sems((24,)), sems((24,)),
        ],
        compiler_params=pltpu.CompilerParams(
            collective_id=0, has_side_effects=True, vmem_limit_bytes=64 * 1024 * 1024
        ),
        cost_estimate=pl.CostEstimate(
            flops=21_000_000_000, bytes_accessed=14_000_000, transcendentals=13_000_000
        ),
    )(frame_map, band, grad_out.T, w_out, queries, keys, values, w_query, w_key, w_value)


def solution(mesh):
    placed = (
        P("tm", "tensor"),
        P("tm", "tensor"),
        P("tm", "tensor"),
        P("tm", "tensor"),
        P(),
        P(),
        P(None, "tensor"),
        P(None, "tensor"),
        P(None, "tensor"),
        P("tensor", None),
    )
    return jax.shard_map(
        per_device, mesh=mesh, in_specs=placed, out_specs=P("tensor", "tm"), check_vma=False
    )
```

```python
import jax
import jax.numpy as jnp
from jax import lax
from jax.experimental import pallas as pl
from jax.experimental.pallas import tpu as pltpu
from jax.sharding import PartitionSpec as P

HD = 128
F = 640
SCALE = HD ** -0.5
POWER = SCALE * 1.4426950408889634
ARRAYS = 6
MESH = pl.DeviceIdType.MESH
NT = (((1,), (1,)), ((), ()))
masked_score = -1e30


def dot(a, b):
    return jnp.dot(a, b, preferred_element_type=jnp.float32)


def dot_nt(a, b):
    return lax.dot_general(a, b, NT, preferred_element_type=jnp.float32)


def ring(position, step):
    return lax.rem(position + step + 4, 4)


def low(value):
    return value.astype(jnp.bfloat16)


def wide(value):
    return value.astype(jnp.float32)


def kernel(
    frame_map, band, go_hbm, wo_hbm, q_hbm, k_hbm, v_hbm, wq_hbm, wk_hbm, wv_hbm, out_ref,
    go, wo, kall, qall, vall, dall, vown, logs, dots, p, pt, dist, dacc, att, gq,
    tops, sums, row_dot, in1, in2,
    load_sem, zs, zr, ys, yr, s1, r1, s2, r2,
):
    g = lax.axis_index("tensor")
    z, x = g // 4, g % 4
    me = lax.axis_index("tm")
    y, core = me // 2, me % 2
    at_z = [z] + [ring(z, step) for step in (1, 2, 3)]
    at_x = [x] + [ring(x, step) for step in (1, 2, 3)]
    blocks = [[at_z[dz] * 4 + at_x[dx] for dx in range(4)] for dz in range(4)]
    block_rows = [[blocks[dz][dx] * 320 for dx in range(4)] for dz in range(4)]
    lines = [at_z[dz] * 1280 for dz in range(4)]
    slots = [[ring(y, hop) * 2 + c for c in (core, 1 - core)] for hop in range(4)]
    my_frame = frame_map[me]

    def slot_rows(s):
        return pl.ds(pl.multiple_of(s * F, F), F)

    mine = slot_rows(me)

    def load(n, src, dst):
        return pltpu.make_async_copy(src, dst, load_sem.at[n])

    loads = [
        load(0, go_hbm, go.at[pl.ds(pl.multiple_of(g * 320, 320), 320)]),
        load(1, k_hbm, kall.at[mine]),
        load(2, q_hbm, qall.at[mine]),
        load(3, v_hbm, vall.at[mine]),
        load(4, v_hbm, vown),
        load(5, wo_hbm, wo),
    ]
    for item in loads:
        item.start()

    def block(half, d, e):
        dz, dx = (d, e) if half else (e, d)
        return dz % 4, dx % 4

    def device(at):
        return (me, blocks[at[0]][at[1]])

    def tensor_copy(half, m, at, kind, target):
        start = block_rows[at[0]][at[1]] + (half * 160 + (80 if kind == 3 else 0))
        ref = go.at[pl.ds(pl.multiple_of(start, 16), 160 if kind < 2 else 80)]
        n = half * 20 + m
        return pltpu.make_async_remote_copy(
            src_ref=ref, dst_ref=ref, send_sem=zs.at[n], recv_sem=zr.at[n],
            device_id=device(target), device_id_type=MESH,
        )

    def both(step):
        for half in (0, 1):
            step(half)

    here = (0, 0)

    def spread(half, index, d):
        j = block(half, d, 0)
        m = 4 + 4 * index
        tensor_copy(half, m, j, 0, block(half, 0, 1)).start()
        tensor_copy(half, m + 1, j, 1, block(half, 0, -1)).start()

    def tensor_start(half):
        tensor_copy(half, 0, here, 0, block(half, 1, 0)).start()
        tensor_copy(half, 1, here, 1, block(half, -1, 0)).start()

    def tensor_next(half):
        spread(half, 0, 0)

    def tensor_near(half):
        j = block(half, -1, 0)
        tensor_copy(half, 0, j, 0, here).wait_recv()
        tensor_copy(half, 2, j, 2, block(half, 1, 0)).start()
        spread(half, 1, -1)
        j = block(half, 1, 0)
        tensor_copy(half, 1, j, 1, here).wait_recv()
        tensor_copy(half, 3, j, 3, block(half, -1, 0)).start()
        spread(half, 2, 1)

    def tensor_far(half):
        j = block(half, 2, 0)
        tensor_copy(half, 2, j, 2, here).wait_recv()
        tensor_copy(half, 3, j, 3, here).wait_recv()
        spread(half, 3, 2)

    offsets = (0, -1, 1, 2)

    def forward(index):
        def step(half):
            m, d = 4 + 4 * index, offsets[index]
            j = block(half, d, -1)
            tensor_copy(half, m, j, 0, here).wait_recv()
            tensor_copy(half, m + 2, j, 2, block(half, 0, 1)).start()
            j = block(half, d, 1)
            tensor_copy(half, m + 1, j, 1, here).wait_recv()
            tensor_copy(half, m + 3, j, 3, block(half, 0, -1)).start()

        both(step)

    def finish(half, index):
        m, d = 4 + 4 * index, offsets[index]
        j = block(half, d, 2)
        tensor_copy(half, m + 2, j, 2, here).wait_recv()
        tensor_copy(half, m + 3, j, 3, here).wait_recv()

    def add_row(index):
        cols = pl.ds(pl.multiple_of(lines[offsets[index] % 4], 1280), 1280)
        dacc[...] += dot(wo[:, cols], go[cols, :])

    sibling = slots[0][1]

    def at_y(step):
        return slots[step % 4][0]

    class Gather:
        def __init__(self, array, ref, rows):
            self.array, self.ref, self.rows = array, ref, rows

        def copy(self, m, slot, target):
            start, count = slot * self.rows, self.rows
            if m in (2, 3):
                count = self.rows // 2
                start = start + (m - 2) * count
            ref = self.ref.at[pl.ds(pl.multiple_of(start, count), count)]
            n = self.array * 8 + m
            return pltpu.make_async_remote_copy(
                src_ref=ref, dst_ref=ref, send_sem=ys.at[n], recv_sem=yr.at[n],
                device_id=(target, g), device_id_type=MESH,
            )

        def start(self):
            self.copy(0, me, at_y(1)).start()
            self.copy(1, me, at_y(-1)).start()
            self.copy(4, me, sibling).start()

        def near(self):
            self.copy(0, at_y(-1), me).wait_recv()
            self.copy(2, at_y(-1), at_y(1)).start()
            self.copy(5, at_y(-1), sibling).start()
            self.copy(1, at_y(1), me).wait_recv()
            self.copy(3, at_y(1), at_y(-1)).start()
            self.copy(6, at_y(1), sibling).start()

        def far(self):
            self.copy(2, at_y(2), me).wait_recv()
            self.copy(3, at_y(2), me).wait_recv()
            self.copy(7, at_y(2), sibling).start()

        def from_sibling(self, *messages):
            for m in messages:
                self.copy(m, slots[(0, -1, 1, 2)[m - 4] % 4][1], me).wait_recv()

        def drain(self):
            for m in range(8):
                self.copy(m, me, me).wait_send()

    keys, queries = Gather(0, kall, F), Gather(1, qall, F)
    values, grads = Gather(2, vall, F), Gather(3, dall, F)
    totals, products = Gather(4, logs, 16), Gather(5, dots, 16)

    def by_arrival(gathers, body, events):
        def step(n, carry):
            ring_at = lax.div(n + 2, 4)
            odd = lax.rem(n, 2)
            hop = lax.rem(ring_at, 2) * (2 * odd - 1) + lax.div(ring_at, 2) * 2
            other = (1 - lax.rem(ring_at, 2)) * odd + lax.rem(ring_at, 2) * lax.rem(lax.div(n + 2, 2), 2)
            slot = ring(y, hop) * 2 + lax.rem(core + other, 2)
            waits = {
                1: lambda item: item.from_sibling(4),
                4: lambda item: item.from_sibling(5, 6),
                6: lambda item: item.far(),
                7: lambda item: item.from_sibling(7),
            }
            for when in range(8):
                if when in waits or when in events:
                    @pl.when(n == when)
                    def _(when=when):
                        if when in events:
                            events[when]()
                        if when in waits:
                            for item in gathers:
                                waits[when](item)

            body(slot)
            return carry

        lax.fori_loop(0, 8, step, 0)

    lane = lax.broadcasted_iota(jnp.int32, (F, HD), 1)

    def head(ref, rows, h):
        return ref[rows, h * HD:(h + 1) * HD]

    def stat_row(ref, s, h):
        return ref[pl.ds(pl.multiple_of(s * 16 + h * 8, 8), 8), :][0:1, :]

    def to_row(ref, h, column):
        rows = pl.ds(pl.multiple_of(me * 16 + h * 8, 8), 8)
        ref[rows, :] = jnp.broadcast_to(column, (F, HD)).T[0:8, :]

    def factor(h, s):
        return jnp.sum(jnp.where(lane == s, sums[h], 0.0), axis=1, keepdims=True)

    def softmax(s):
        width = band[my_frame, frame_map[s]]
        for h in (0, 1):
            scores = dot_nt(head(qall, mine, h), head(kall, slot_rows(s), h))
            scores = jnp.where(dist[...] <= width, scores, masked_score)
            top = jnp.max(scores, axis=1, keepdims=True) * POWER
            shifted = jnp.exp2(scores * POWER - top)
            total = jnp.sum(shifted, axis=1, keepdims=True)
            p[h, s] = low(shifted)
            tops[h] = jnp.where(lane == s, top, tops[h])
            sums[h] = jnp.where(lane == s, total, sums[h])

    def combine():
        for h in (0, 1):
            top = jnp.max(tops[h], axis=1, keepdims=True)
            shares = jnp.exp2(tops[h] - top)
            total = jnp.sum(shares * sums[h], axis=1, keepdims=True)
            sums[h] = shares / total
            to_row(logs, h, top + jnp.log2(total))

    def key_side(s):
        width = band[frame_map[s], my_frame]
        for h in (0, 1):
            scores = dot_nt(head(kall, mine, h), head(qall, slot_rows(s), h))
            power = jnp.where(
                dist[...] <= width, scores * POWER - stat_row(logs, s, h), masked_score
            )
            pt[h, s] = low(jnp.exp2(power))

    def attend(s):
        for h in (0, 1):
            att[h] += factor(h, s) * dot(p[h, s], head(vall, slot_rows(s), h))

    def query_grad(s):
        for h in (0, 1):
            grad = dot_nt(head(dall, mine, h), head(vall, slot_rows(s), h))
            grad = wide(p[h, s]) * ((grad - row_dot[h, :, 0:1]) * factor(h, s))
            gq[h] += dot(low(grad), head(kall, slot_rows(s), h))

    def key_grad(s):
        for h in (0, 1):
            grad_rows = head(dall, slot_rows(s), h)
            weight = pt[h, s]
            grad = dot_nt(head(vown, slice(None), h), grad_rows)
            grad = wide(weight) * (grad - stat_row(dots, s, h))
            gv[h] += dot(weight, grad_rows)
            gk[h] += dot(low(grad), head(qall, slot_rows(s), h))

    barrier = pltpu.get_barrier_semaphore()
    for half in (0, 1):
        for step in (1, -1):
            pl.semaphore_signal(
                barrier, inc=1, device_id=device(block(half, step, 0)), device_id_type=MESH
            )
    for target in (at_y(1), at_y(-1), sibling):
        pl.semaphore_signal(barrier, inc=1, device_id=(target, g), device_id_type=MESH)
    loads[0].wait()
    loads[1].wait()
    pl.semaphore_wait(barrier, 7)
    both(tensor_start)
    keys.start()
    both(tensor_next)
    across = lax.broadcasted_iota(jnp.int32, (F, F), 0) - lax.broadcasted_iota(jnp.int32, (F, F), 1)
    dist[...] = jnp.abs(across)
    for ref in (dacc, att, gq, sums):
        ref[...] = jnp.zeros_like(ref)
    tops[...] = jnp.full_like(tops, masked_score)
    for item in loads[2:]:
        item.wait()

    def keys_near():
        both(tensor_near)
        keys.near()
        queries.start()

    by_arrival(
        (keys,), softmax,
        {2: keys_near, 5: lambda: both(tensor_far), 7: lambda: forward(0)},
    )
    combine()
    totals.start()

    def queries_near():
        queries.near()
        values.start()
        totals.near()

    by_arrival(
        (queries, totals), key_side,
        {2: queries_near, 4: lambda: forward(1), 7: lambda: forward(2)},
    )
    forward(3)

    def values_near():
        values.near()

    by_arrival((values,), attend, {2: values_near})
    for index in range(4):
        finish(0, index)
    for index in range(4):
        finish(1, index)
        add_row(index)
    dall[mine, :] = low(dacc[...].T)
    grads.start()
    for h in (0, 1):
        column = jnp.sum(wide(head(dall, mine, h)) * att[h], axis=1, keepdims=True)
        row_dot[h] = jnp.broadcast_to(column, (F, HD))
        to_row(dots, h, column)
    products.start()
    gk, gv = tops, att
    for ref in (gk, gv):
        ref[...] = jnp.zeros_like(ref)

    def query_step(s, carry):
        query_grad(s)

        @pl.when(s == 5)
        def _():
            grads.near()
            products.near()

        return carry

    lax.fori_loop(0, 8, query_step, 0)
    keys.drain()
    values.drain()
    loads = [load(0, wq_hbm, kall), load(1, wk_hbm, vall)]
    for item in loads:
        item.start()
    gt = [p.at[0, n, 0:256] for n in range(3)]

    def to_gt(n, ref, scale):
        for h in (0, 1):
            gt[n][h * HD:(h + 1) * HD, :] = low((ref[h] * scale).T)

    to_gt(0, gq, SCALE)
    by_arrival((grads, products), key_grad, {})
    queries.drain()
    loads.append(load(2, wv_hbm, qall))
    loads[2].start()
    to_gt(1, gk, SCALE)
    to_gt(2, gv, 1.0)
    for item in loads:
        item.wait()

    def drain(half):
        for i in range(5):
            for kind in range(4):
                tensor_copy(half, 4 * i + kind, here, kind, here).wait_send()

    both(drain)

    def target(half, d, e):
        return block(1 - half, d, e)

    def part(half, d, e, skip=0, count=160):
        dz, dx = target(half, d, e)
        start = block_rows[dz][dx] + (half * 160 + skip)
        return go.at[pl.ds(pl.multiple_of(start, 16), count)]

    def multiply(dz):
        def one(i, carry):
            rows = pl.ds(pl.multiple_of(lines[dz] + i * F, F), F)
            total = dot(kall[rows, :], gt[0][...]) + dot(vall[rows, :], gt[1][...])
            go[rows, :] = low(total + dot(qall[rows, :], gt[2][...]))
            return carry

        lax.fori_loop(0, 2, one, 0)

    def first(m, half, d, e, step):
        n = half * 12 + m
        return pltpu.make_async_remote_copy(
            src_ref=part(half, d, e), dst_ref=in1.at[n], send_sem=s1.at[n], recv_sem=r1.at[n],
            device_id=device(target(half, step, 0)), device_id_type=MESH,
        )

    def second(m, half, e, skip, step):
        n = half * 6 + m
        return pltpu.make_async_remote_copy(
            src_ref=part(half, 0, e, skip, 80), dst_ref=in2.at[n], send_sem=s2.at[n], recv_sem=r2.at[n],
            device_id=device(target(half, 0, step)), device_id_type=MESH,
        )

    far = ((0, 2, 2, 1), (1, 2, 1, -1), (2, 2, 3, 1), (3, 2, 0, -1))
    alone = ((4, 1, 1, 1), (5, 3, 2, -1), (6, 1, 0, 1), (7, 3, 3, -1))
    summed = ((8, 1, 2, 1), (9, 3, 1, -1), (10, 1, 3, 1), (11, 3, 0, -1))

    def send(half, messages):
        for m, d, e, step in messages:
            first(m, half, d, e, step).start()

    multiply(2)
    send(0, far)
    send(1, (far[0], alone[1]))
    multiply(1)
    send(1, (far[1],))
    send(0, (alone[0], alone[2]))
    send(1, (alone[0], ))
    multiply(3)
    send(1, (far[2], alone[3]))
    send(0, (alone[1], alone[3]))
    multiply(0)
    send(1, (far[3], alone[2]))

    def pass_on(m, d, e, step):
        def one(half):
            first(m - 8, half, d, e, step).wait_recv()
            ref = part(half, d, e)
            ref[...] = low(wide(ref[...]) + wide(in1[half * 12 + m - 8]))
            first(m, half, d, e, step).start()

        both(one)

    for message in summed:
        pass_on(*message)

    def collect(half, e, up, down):
        first(up, half, 0, e, 1).wait_recv()
        first(down, half, 0, e, 1).wait_recv()
        return wide(part(half, 0, e)[...]) + wide(in1[half * 12 + up]) + wide(in1[half * 12 + down])

    def collect_far(half):
        total = collect(half, 2, 8, 5)
        part(half, 0, 2)[...] = low(total)
        second(0, half, 2, 0, 1).start()
        second(1, half, 2, 80, -1).start()

    def collect_next(half):
        total = collect(half, 1, 4, 9)
        part(half, 0, 1)[...] = low(total)
        second(2, half, 1, 80, 1).start()
        total_low = total[0:80]
        second(0, half, 1, 0, 1).wait_recv()
        part(half, 0, 1, 0, 80)[...] = low(total_low + wide(in2[half * 6]))
        second(3, half, 1, 0, 1).start()

    def collect_last(half):
        total = collect(half, 3, 10, 7)
        part(half, 0, 3)[...] = low(total)
        second(4, half, 3, 0, -1).start()
        total_high = total[80:160]
        second(1, half, 3, 80, -1).wait_recv()
        part(half, 0, 3, 80, 80)[...] = low(total_high + wide(in2[half * 6 + 1]))
        second(5, half, 3, 80, -1).start()

    def collect_own(half):
        total = collect(half, 0, 6, 11)
        for m in (2, 3, 4, 5):
            second(m, half, 0, 0, 1).wait_recv()
        at = half * 160
        n = half * 6
        out_ref[pl.ds(at, 80), :] = low(total[0:80] + (wide(in2[n + 3]) + wide(in2[n + 4])))
        out_ref[pl.ds(at + 80, 80), :] = low(total[80:160] + (wide(in2[n + 2]) + wide(in2[n + 5])))

    for step in (collect_far, collect_next, collect_last, collect_own):
        both(step)

    for half in (0, 1):
        for m in range(12):
            first(m, half, 0, 0, 1).wait_send()
        for m in range(6):
            second(m, half, 0, 0, 1).wait_send()
    for item in (grads, totals, products):
        item.drain()


def per_device(queries, keys, values, grad_out, frame_map, band, w_query, w_key, w_value, w_out):
    vmem = pl.BlockSpec(memory_space=pltpu.VMEM)
    hbm = pl.BlockSpec(memory_space=pl.ANY)
    smem = pl.BlockSpec(memory_space=pltpu.SMEM)
    gathered = pltpu.VMEM((8 * F, 256), jnp.bfloat16)
    stats = pltpu.VMEM((128, F), jnp.float32)
    pairs = pltpu.VMEM((2, 8, F, F), jnp.bfloat16)
    heads = pltpu.VMEM((2, F, HD), jnp.float32)
    sems = pltpu.SemaphoreType.DMA
    return pl.pallas_call(
        kernel,
        out_shape=jax.ShapeDtypeStruct((320, F), jnp.bfloat16),
        in_specs=[smem] * 2 + [hbm] * 8,
        out_specs=vmem,
        scratch_shapes=[
            pltpu.VMEM((5120, F), jnp.bfloat16),
            pltpu.VMEM((256, 5120), jnp.bfloat16),
            gathered, gathered, gathered, gathered,
            pltpu.VMEM((F, 256), jnp.bfloat16),
            stats, stats,
            pairs, pairs,
            pltpu.VMEM((F, F), jnp.int32),
            pltpu.VMEM((256, F), jnp.float32),
            heads, heads, heads, heads, heads,
            pltpu.VMEM((24, 160, F), jnp.bfloat16),
            pltpu.VMEM((12, 80, F), jnp.bfloat16),
            sems((6,)), sems((40,)), sems((40,)), sems((8 * ARRAYS,)), sems((8 * ARRAYS,)),
            sems((24,)), sems((24,)), sems((12,)), sems((12,)),
        ],
        compiler_params=pltpu.CompilerParams(
            collective_id=0, has_side_effects=True, vmem_limit_bytes=64 * 1024 * 1024
        ),
        cost_estimate=pl.CostEstimate(
            flops=21_000_000_000, bytes_accessed=14_000_000, transcendentals=13_000_000
        ),
    )(frame_map, band, grad_out.T, w_out, queries, keys, values, w_query, w_key, w_value)


def solution(mesh):
    placed = (
        P("tm", "tensor"),
        P("tm", "tensor"),
        P("tm", "tensor"),
        P("tm", "tensor"),
        P(),
        P(),
        P(None, "tensor"),
        P(None, "tensor"),
        P(None, "tensor"),
        P("tensor", None),
    )
    return jax.shard_map(
        per_device, mesh=mesh, in_specs=placed, out_specs=P("tensor", "tm"), check_vma=False
    )
```

```python
import jax
import jax.numpy as jnp
from jax import lax
from jax.experimental import pallas as pl
from jax.experimental.pallas import tpu as pltpu
from jax.sharding import PartitionSpec as P

HD = 128
F = 640
SCALE = HD ** -0.5
POWER = SCALE * 1.4426950408889634
CHUNKS = ((0, 384), (384, 256))
ARRAYS = 6
MESH = pl.DeviceIdType.MESH
NT = (((1,), (1,)), ((), ()))
masked_score = -1e30


def dot(a, b):
    return jnp.dot(a, b, preferred_element_type=jnp.float32)


def dot_nt(a, b):
    return lax.dot_general(a, b, NT, preferred_element_type=jnp.float32)


def ring(position, step):
    return lax.rem(position + step + 4, 4)


def low(value):
    return value.astype(jnp.bfloat16)


def wide(value):
    return value.astype(jnp.float32)


def kernel(
    frame_map, band, go_hbm, wo_hbm, q_hbm, k_hbm, v_hbm, wq_hbm, wk_hbm, wv_hbm, out_ref,
    go, wo, kall, qall, vall, dall, logs, dots, p, pt, dist, dacc, att, gq,
    tops, sums, row_dot, gt, wbuf, in1, in2,
    load_sem, zs, zr, ys, yr, wsem, s1, r1, s2, r2,
):
    g = lax.axis_index("tensor")
    z, x = g // 4, g % 4
    me = lax.axis_index("tm")
    y, core = me // 2, me % 2
    my_frame = frame_map[me]

    def slot_rows(s):
        return pl.ds(pl.multiple_of(s * F, F), F)

    mine = slot_rows(me)

    def load(n, src, dst):
        return pltpu.make_async_copy(src, dst, load_sem.at[n])

    loads = [
        load(0, go_hbm, go.at[pl.ds(pl.multiple_of(g * 320, 320), 320)]),
        load(1, k_hbm, kall.at[mine]),
        load(2, q_hbm, qall.at[mine]),
        load(3, v_hbm, vall.at[mine]),
        load(4, wo_hbm, wo),
    ]
    for item in loads:
        item.start()

    def block(half, d, e):
        zz = ring(z, d * half + e * (1 - half))
        xx = ring(x, d * (1 - half) + e * half)
        return zz * 4 + xx

    def tensor_copy(half, m, j, kind, target):
        start = j * 320 + half * 160 + (80 if kind == 3 else 0)
        ref = go.at[pl.ds(pl.multiple_of(start, 16), 160 if kind < 2 else 80)]
        n = half * 20 + m
        return pltpu.make_async_remote_copy(
            src_ref=ref, dst_ref=ref, send_sem=zs.at[n], recv_sem=zr.at[n],
            device_id={"tensor": target}, device_id_type=MESH,
        )

    def both(step):
        def one(half, carry):
            step(half)
            return carry

        lax.fori_loop(0, 2, one, 0)

    def spread(half, index, d):
        j = block(half, d, 0)
        m = 4 + 4 * index
        tensor_copy(half, m, j, 0, block(half, 0, 1)).start()
        tensor_copy(half, m + 1, j, 1, block(half, 0, -1)).start()

    def tensor_start(half):
        tensor_copy(half, 0, g, 0, block(half, 1, 0)).start()
        tensor_copy(half, 1, g, 1, block(half, -1, 0)).start()

    def tensor_next(half):
        spread(half, 0, 0)

    def tensor_near(half):
        j = block(half, -1, 0)
        tensor_copy(half, 0, j, 0, g).wait_recv()
        tensor_copy(half, 2, j, 2, block(half, 1, 0)).start()
        spread(half, 1, -1)
        j = block(half, 1, 0)
        tensor_copy(half, 1, j, 1, g).wait_recv()
        tensor_copy(half, 3, j, 3, block(half, -1, 0)).start()
        spread(half, 2, 1)

    def tensor_far(half):
        j = block(half, 2, 0)
        tensor_copy(half, 2, j, 2, g).wait_recv()
        tensor_copy(half, 3, j, 3, g).wait_recv()
        spread(half, 3, 2)

    offsets = (0, -1, 1, 2)

    def forward(index):
        def step(half):
            m, d = 4 + 4 * index, offsets[index]
            j = block(half, d, -1)
            tensor_copy(half, m, j, 0, g).wait_recv()
            tensor_copy(half, m + 2, j, 2, block(half, 0, 1)).start()
            j = block(half, d, 1)
            tensor_copy(half, m + 1, j, 1, g).wait_recv()
            tensor_copy(half, m + 3, j, 3, block(half, 0, -1)).start()

        both(step)

    def finish(half, index):
        m, d = 4 + 4 * index, offsets[index]
        j = block(half, d, 2)
        tensor_copy(half, m + 2, j, 2, g).wait_recv()
        tensor_copy(half, m + 3, j, 3, g).wait_recv()

    def add_row(index):
        cols = pl.ds(pl.multiple_of(ring(z, offsets[index]) * 1280, 1280), 1280)
        dacc[...] += dot(wo[:, cols], go[cols, :])

    sibling = y * 2 + 1 - core

    def at_y(step):
        return ring(y, step) * 2 + core

    class Gather:
        def __init__(self, array, ref, rows):
            self.array, self.ref, self.rows = array, ref, rows

        def copy(self, m, slot, target):
            start, count = slot * self.rows, self.rows
            if m in (2, 3):
                count = self.rows // 2
                start = start + (m - 2) * count
            ref = self.ref.at[pl.ds(pl.multiple_of(start, count), count)]
            n = self.array * 8 + m
            return pltpu.make_async_remote_copy(
                src_ref=ref, dst_ref=ref, send_sem=ys.at[n], recv_sem=yr.at[n],
                device_id={"tm": target}, device_id_type=MESH,
            )

        def start(self):
            self.copy(0, me, at_y(1)).start()
            self.copy(1, me, at_y(-1)).start()
            self.copy(4, me, sibling).start()

        def near(self):
            self.copy(0, at_y(-1), me).wait_recv()
            self.copy(2, at_y(-1), at_y(1)).start()
            self.copy(5, at_y(-1), sibling).start()
            self.copy(1, at_y(1), me).wait_recv()
            self.copy(3, at_y(1), at_y(-1)).start()
            self.copy(6, at_y(1), sibling).start()

        def far(self):
            self.copy(2, at_y(2), me).wait_recv()
            self.copy(3, at_y(2), me).wait_recv()
            self.copy(7, at_y(2), sibling).start()

        def from_sibling(self, *messages):
            for m in messages:
                slot = ring(y, (0, -1, 1, 2)[m - 4]) * 2 + 1 - core
                self.copy(m, slot, me).wait_recv()

        def drain(self):
            for m in range(8):
                self.copy(m, me, me).wait_send()

    keys, queries = Gather(0, kall, F), Gather(1, qall, F)
    values, grads = Gather(2, vall, F), Gather(3, dall, F)
    totals, products = Gather(4, logs, 16), Gather(5, dots, 16)

    def by_arrival(gathers, body, events):
        def step(n, carry):
            ring_at = (n + 2) // 4
            hop = (ring_at % 2) * (2 * (n % 2) - 1) + (ring_at // 2) * 2
            other = (1 - ring_at % 2) * (n % 2) + (ring_at % 2) * (((n + 2) // 2) % 2)
            slot = ring(y, hop) * 2 + (core + other) % 2
            waits = {
                1: lambda item: item.from_sibling(4),
                4: lambda item: item.from_sibling(5, 6),
                6: lambda item: item.far(),
                7: lambda item: item.from_sibling(7),
            }
            for when in range(8):
                if when in waits or when in events:
                    @pl.when(n == when)
                    def _(when=when):
                        if when in events:
                            events[when]()
                        if when in waits:
                            for item in gathers:
                                waits[when](item)

            body(slot)
            return carry

        lax.fori_loop(0, 8, step, 0)

    lane = lax.broadcasted_iota(jnp.int32, (F, HD), 1)

    def head(ref, rows, h):
        return ref[rows, h * HD:(h + 1) * HD]

    def stat_row(ref, s, h):
        return ref[pl.ds(pl.multiple_of(s * 16 + h * 8, 8), 8), :][0:1, :]

    def to_row(ref, h, column):
        rows = pl.ds(pl.multiple_of(me * 16 + h * 8, 8), 8)
        ref[rows, :] = jnp.broadcast_to(column, (F, HD)).T[0:8, :]

    def factor(h, s, at=0, count=F):
        own = sums[h, at:at + count, :]
        return jnp.sum(jnp.where(lane[at:at + count] == s, own, 0.0), axis=1, keepdims=True)

    def softmax(s):
        width = band[my_frame, frame_map[s]]
        for h in (0, 1):
            scores = dot_nt(head(qall, mine, h), head(kall, slot_rows(s), h))
            scores = jnp.where(dist[...] <= width, scores, masked_score)
            top = jnp.max(scores, axis=1, keepdims=True) * POWER
            shifted = jnp.exp2(scores * POWER - top)
            total = jnp.sum(shifted, axis=1, keepdims=True)
            p[h, s] = low(shifted)
            tops[h] = jnp.where(lane == s, top, tops[h])
            sums[h] = jnp.where(lane == s, total, sums[h])

    def combine():
        for h in (0, 1):
            top = jnp.max(tops[h], axis=1, keepdims=True)
            shares = jnp.exp2(tops[h] - top)
            total = jnp.sum(shares * sums[h], axis=1, keepdims=True)
            sums[h] = shares / total
            to_row(logs, h, top + jnp.log2(total))

    def key_side(s):
        width = band[frame_map[s], my_frame]
        for h in (0, 1):
            scores = dot_nt(head(kall, mine, h), head(qall, slot_rows(s), h))
            power = jnp.where(
                dist[...] <= width, scores * POWER - stat_row(logs, s, h), masked_score
            )
            pt[h, s] = low(jnp.exp2(power))

    def attend(s):
        for h in (0, 1):
            att[h] += factor(h, s) * dot(p[h, s], head(vall, slot_rows(s), h))

    def query_grad(c, s):
        at, count = CHUNKS[c]
        rows, own = pl.ds(at, count), pl.ds(pl.multiple_of(me * F + at, 128), count)
        for h in (0, 1):
            grad = dot_nt(head(dall, own, h), head(vall, slot_rows(s), h))
            grad = low(grad - jnp.concatenate([row_dot[h, rows, :]] * 5, axis=1))
            product = dot(p[h, s, rows, :] * grad, head(kall, slot_rows(s), h))
            gq[h, rows, :] += factor(h, s, at, count) * product

    def key_grad(c, s):
        at, count = CHUNKS[c]
        rows, own = pl.ds(at, count), pl.ds(pl.multiple_of(me * F + at, 128), count)
        for h in (0, 1):
            grad_rows = head(dall, slot_rows(s), h)
            weight = pt[h, s, rows, :]
            grad = low(dot_nt(head(vall, own, h), grad_rows) - stat_row(dots, s, h))
            gv[h, rows, :] += dot(weight, grad_rows)
            gk[h, rows, :] += dot(weight * grad, head(qall, slot_rows(s), h))

    barrier = pltpu.get_barrier_semaphore()
    for half in (0, 1):
        for step in (1, -1):
            pl.semaphore_signal(
                barrier, inc=1, device_id={"tensor": block(half, step, 0)}, device_id_type=MESH
            )
    for target in (at_y(1), at_y(-1), sibling):
        pl.semaphore_signal(barrier, inc=1, device_id={"tm": target}, device_id_type=MESH)
    loads[0].wait()
    loads[1].wait()
    pl.semaphore_wait(barrier, 7)
    both(tensor_start)
    keys.start()
    both(tensor_next)
    across = lax.broadcasted_iota(jnp.int32, (F, F), 0) - lax.broadcasted_iota(jnp.int32, (F, F), 1)
    dist[...] = jnp.abs(across)
    for ref in (dacc, att, gq, sums):
        ref[...] = jnp.zeros_like(ref)
    tops[...] = jnp.full_like(tops, masked_score)
    for item in loads[2:]:
        item.wait()

    def keys_near():
        both(tensor_near)
        keys.near()
        queries.start()

    by_arrival(
        (keys,), softmax,
        {2: keys_near, 5: lambda: both(tensor_far), 7: lambda: forward(0)},
    )
    combine()
    totals.start()

    def queries_near():
        queries.near()
        values.start()
        totals.near()

    by_arrival(
        (queries, totals), key_side,
        {2: queries_near, 4: lambda: forward(1), 7: lambda: forward(2)},
    )
    forward(3)

    def values_near():
        values.near()

    by_arrival((values,), attend, {2: values_near})
    for index in range(4):
        finish(0, index)
    for index in range(4):
        finish(1, index)
        add_row(index)
    dall[mine, :] = low(dacc[...].T)
    grads.start()
    for h in (0, 1):
        column = jnp.sum(wide(head(dall, mine, h)) * att[h], axis=1, keepdims=True)
        row_dot[h] = jnp.broadcast_to(column, (F, HD))
        to_row(dots, h, column)
    products.start()
    gk, gv = tops, att
    for ref in (gk, gv):
        ref[...] = jnp.zeros_like(ref)

    def to_gt(n, ref, scale, c):
        rows = pl.ds(*CHUNKS[c])
        for h in (0, 1):
            gt[n * 256 + h * HD:n * 256 + (h + 1) * HD, rows] = low((ref[h, rows, :] * scale).T)

    def drain(half):
        def one(i, carry):
            for kind in range(4):
                tensor_copy(half, 4 * i + kind, g, kind, g).wait_send()
            return carry

        lax.fori_loop(0, 5, one, 0)

    def target(half, d, e):
        return block(1 - half, d, e)

    def part(c, half, d, e, skip=0, count=160):
        start = target(half, d, e) * 320 + half * 160 + skip
        return go.at[pl.ds(pl.multiple_of(start, 16), count), pl.ds(*CHUNKS[c])]

    def got(c, ref, n):
        return wide(ref[n, :, pl.ds(*CHUNKS[c])])

    def first(c, m, half, d, e, step):
        n = half * 12 + m
        return pltpu.make_async_remote_copy(
            src_ref=part(c, half, d, e), dst_ref=in1.at[n, :, pl.ds(*CHUNKS[c])],
            send_sem=s1.at[c * 24 + n], recv_sem=r1.at[c * 24 + n],
            device_id={"tensor": target(half, step, 0)}, device_id_type=MESH,
        )

    def second(c, m, half, e, skip, step):
        n = half * 6 + m
        return pltpu.make_async_remote_copy(
            src_ref=part(c, half, 0, e, skip, 80), dst_ref=in2.at[n, :, pl.ds(*CHUNKS[c])],
            send_sem=s2.at[c * 12 + n], recv_sem=r2.at[c * 12 + n],
            device_id={"tensor": target(half, 0, step)}, device_id_type=MESH,
        )

    far = ((0, 2, 2, 1), (1, 2, 1, -1), (2, 2, 3, 1), (3, 2, 0, -1))
    alone = ((4, 1, 1, 1), (5, 3, 2, -1), (6, 1, 0, 1), (7, 3, 3, -1))
    summed = ((8, 1, 2, 1), (9, 3, 1, -1), (10, 1, 3, 1), (11, 3, 0, -1))

    def send(c, half, messages):
        for m, d, e, step in messages:
            first(c, m, half, d, e, step).start()

    def block_rows(j):
        k = j // 2
        dz = (k % 2) * (1 - k // 2) + (1 - k % 2) * (2 + k // 2)
        return pl.ds(pl.multiple_of(ring(z, dz) * 1280 + (j % 2) * F, F), F)

    def fetch(j):
        return [
            pltpu.make_async_copy(src.at[block_rows(j)], wbuf.at[j % 3, n], wsem.at[j % 3, n])
            for n, src in enumerate((wq_hbm, wk_hbm, wv_hbm))
        ]

    def start_fetch(j):
        for item in fetch(j):
            item.start()

    def multiply(c):
        tokens = pl.ds(*CHUNKS[c])

        def one(j, carry):
            for item in fetch(j):
                item.wait()

            left = jnp.concatenate([wbuf[j % 3, n] for n in range(3)], axis=1)
            go[block_rows(j), tokens] = low(dot(left, gt[:, tokens]))

            @pl.when(j < 5)
            def _():
                start_fetch(j + 3)

            events = {
                1: ((0, far), (1, (far[0], alone[1]))),
                3: ((1, (far[1], alone[0])), (0, (alone[0], alone[2]))),
                5: ((1, (far[2], alone[3])), (0, (alone[1], alone[3]))),
                7: ((1, (far[3], alone[2])),),
            }
            for when in events:
                @pl.when(j == when)
                def _(when=when):
                    for half, messages in events[when]:
                        send(c, half, messages)

            return carry

        lax.fori_loop(0, 8, one, 0)

    def pass_on(c, message):
        m, d, e, step = message

        def one(half):
            first(c, m - 8, half, d, e, step).wait_recv()
            ref = part(c, half, d, e)
            ref[...] = low(wide(ref[...]) + got(c, in1, half * 12 + m - 8))
            first(c, m, half, d, e, step).start()

        both(one)

    def collect(c, half, e, up, down):
        first(c, up, half, 0, e, 1).wait_recv()
        first(c, down, half, 0, e, 1).wait_recv()
        return wide(part(c, half, 0, e)[...]) + got(c, in1, half * 12 + up) + got(c, in1, half * 12 + down)

    def collect_far(c, half):
        part(c, half, 0, 2)[...] = low(collect(c, half, 2, 8, 5))
        second(c, 0, half, 2, 0, 1).start()
        second(c, 1, half, 2, 80, -1).start()

    def collect_next(c, half):
        total = collect(c, half, 1, 4, 9)
        part(c, half, 0, 1)[...] = low(total)
        second(c, 2, half, 1, 80, 1).start()
        second(c, 0, half, 1, 0, 1).wait_recv()
        part(c, half, 0, 1, 0, 80)[...] = low(total[0:80] + got(c, in2, half * 6))
        second(c, 3, half, 1, 0, 1).start()

    def collect_last(c, half):
        total = collect(c, half, 3, 10, 7)
        part(c, half, 0, 3)[...] = low(total)
        second(c, 4, half, 3, 0, -1).start()
        second(c, 1, half, 3, 80, -1).wait_recv()
        part(c, half, 0, 3, 80, 80)[...] = low(total[80:160] + got(c, in2, half * 6 + 1))
        second(c, 5, half, 3, 80, -1).start()

    def collect_own(c, half):
        total = collect(c, half, 0, 6, 11)
        for m in (2, 3, 4, 5):
            second(c, m, half, 0, 0, 1).wait_recv()
        at = pl.multiple_of(half * 160, 16)
        n, tokens = half * 6, pl.ds(*CHUNKS[c])
        out_ref[pl.ds(at, 80), tokens] = low(total[0:80] + (got(c, in2, n + 3) + got(c, in2, n + 4)))
        out_ref[pl.ds(at + 80, 80), tokens] = low(
            total[80:160] + (got(c, in2, n + 2) + got(c, in2, n + 5))
        )

    def scatter_steps(c):
        steps = [lambda message=message: pass_on(c, message) for message in summed]
        for collector in (collect_far, collect_next, collect_last, collect_own):
            steps.append(lambda collector=collector: both(lambda half: collector(c, half)))
        return steps

    def eight(body, events):
        def one(s, carry):
            body(s)
            for when in events:
                @pl.when(s == when)
                def _(when=when):
                    events[when]()

            return carry

        lax.fori_loop(0, 8, one, 0)

    def grads_near():
        grads.near()
        products.near()

    for j in range(3):
        start_fetch(j)
    eight(lambda s: query_grad(0, s), {6: grads_near})
    to_gt(0, gq, SCALE, 0)
    both(drain)
    by_arrival((grads, products), lambda s: key_grad(0, s), {})
    to_gt(1, gk, SCALE, 0)
    to_gt(2, gv, 1.0, 0)
    multiply(0)
    for j in range(3):
        start_fetch(j)
    steps = scatter_steps(0)
    eight(lambda s: query_grad(1, s), {4: steps[0], 5: steps[1], 6: steps[2], 7: steps[3]})
    to_gt(0, gq, SCALE, 1)
    eight(lambda s: key_grad(1, s), {6: steps[4]})
    to_gt(1, gk, SCALE, 1)
    to_gt(2, gv, 1.0, 1)
    multiply(1)
    for step in steps[5:] + scatter_steps(1):
        step()

    def sent1(m, carry):
        for c in (0, 1):
            first(c, m, 0, 0, 0, 1).wait_send()
        return carry

    def sent2(m, carry):
        for c in (0, 1):
            second(c, m, 0, 0, 0, 1).wait_send()
        return carry

    lax.fori_loop(0, 24, sent1, 0)
    lax.fori_loop(0, 12, sent2, 0)
    for item in (keys, queries, values, grads, totals, products):
        item.drain()


def per_device(queries, keys, values, grad_out, frame_map, band, w_query, w_key, w_value, w_out):
    vmem = pl.BlockSpec(memory_space=pltpu.VMEM)
    hbm = pl.BlockSpec(memory_space=pl.ANY)
    smem = pl.BlockSpec(memory_space=pltpu.SMEM)
    gathered = pltpu.VMEM((8 * F, 256), jnp.bfloat16)
    stats = pltpu.VMEM((128, F), jnp.float32)
    pairs = pltpu.VMEM((2, 8, F, F), jnp.bfloat16)
    heads = pltpu.VMEM((2, F, HD), jnp.float32)
    sems = pltpu.SemaphoreType.DMA
    return pl.pallas_call(
        kernel,
        out_shape=jax.ShapeDtypeStruct((320, F), jnp.bfloat16),
        in_specs=[smem] * 2 + [hbm] * 8,
        out_specs=vmem,
        scratch_shapes=[
            pltpu.VMEM((5120, F), jnp.bfloat16),
            pltpu.VMEM((256, 5120), jnp.bfloat16),
            gathered, gathered, gathered, gathered,
            stats, stats,
            pairs, pairs,
            pltpu.VMEM((F, F), jnp.int32),
            pltpu.VMEM((256, F), jnp.float32),
            heads, heads, heads, heads, heads,
            pltpu.VMEM((768, F), jnp.bfloat16),
            pltpu.VMEM((3, 3, F, 256), jnp.bfloat16),
            pltpu.VMEM((24, 160, F), jnp.bfloat16),
            pltpu.VMEM((12, 80, F), jnp.bfloat16),
            sems((6,)), sems((40,)), sems((40,)), sems((8 * ARRAYS,)), sems((8 * ARRAYS,)),
            sems((3, 3)), sems((48,)), sems((48,)), sems((24,)), sems((24,)),
        ],
        compiler_params=pltpu.CompilerParams(
            collective_id=0, has_side_effects=True, vmem_limit_bytes=64 * 1024 * 1024
        ),
        cost_estimate=pl.CostEstimate(
            flops=21_000_000_000, bytes_accessed=14_000_000, transcendentals=13_000_000
        ),
    )(frame_map, band, grad_out.T, w_out, queries, keys, values, w_query, w_key, w_value)


def solution(mesh):
    placed = (
        P("tm", "tensor"),
        P("tm", "tensor"),
        P("tm", "tensor"),
        P("tm", "tensor"),
        P(),
        P(),
        P(None, "tensor"),
        P(None, "tensor"),
        P(None, "tensor"),
        P("tensor", None),
    )
    return jax.shard_map(
        per_device, mesh=mesh, in_specs=placed, out_specs=P("tensor", "tm"), check_vma=False
    )
```

```python
import jax
import jax.numpy as jnp
from jax import lax
from jax.experimental import pallas as pl
from jax.experimental.pallas import tpu as pltpu
from jax.sharding import PartitionSpec as P

HD = 128
F = 640
SCALE = HD ** -0.5
POWER = SCALE * 1.4426950408889634
CHUNKS = ((0, 384), (384, 256))
ARRAYS = 6
MESH = pl.DeviceIdType.MESH
NT = (((1,), (1,)), ((), ()))
masked_score = -1e30


def dot(a, b):
    return jnp.dot(a, b, preferred_element_type=jnp.float32)


def dot_nt(a, b):
    return lax.dot_general(a, b, NT, preferred_element_type=jnp.float32)


def ring(position, step):
    return lax.rem(position + step + 4, 4)


def low(value):
    return value.astype(jnp.bfloat16)


def wide(value):
    return value.astype(jnp.float32)


def kernel(
    frame_map, band, go_hbm, wo_hbm, q_hbm, k_hbm, v_hbm, wq_hbm, wk_hbm, wv_hbm, out_ref,
    go, wo, kall, qall, vall, dall, logs, dots, p, pt, dist, dacc, att, gq,
    tops, sums, row_dot, gt, wbuf, in1, in2,
    load_sem, zs, zr, ys, yr, wsem, s1, r1, s2, r2,
):
    g = lax.axis_index("tensor")
    z, x = g // 4, g % 4
    me = lax.axis_index("tm")
    y, core = me // 2, me % 2
    my_frame = frame_map[me]

    def slot_rows(s):
        return pl.ds(pl.multiple_of(s * F, F), F)

    mine = slot_rows(me)

    def load(n, src, dst):
        return pltpu.make_async_copy(src, dst, load_sem.at[n])

    loads = [
        load(0, go_hbm, go.at[pl.ds(pl.multiple_of(g * 320, 320), 320)]),
        load(1, k_hbm, kall.at[mine]),
        load(2, q_hbm, qall.at[mine]),
        load(3, v_hbm, vall.at[mine]),
        load(4, wo_hbm, wo),
    ]
    for item in loads:
        item.start()

    def block(half, d, e):
        zz = ring(z, d * half + e * (1 - half))
        xx = ring(x, d * (1 - half) + e * half)
        return zz * 4 + xx

    def tensor_copy(half, m, j, kind, target):
        start = j * 320 + half * 160 + (80 if kind == 3 else 0)
        ref = go.at[pl.ds(pl.multiple_of(start, 16), 160 if kind < 2 else 80)]
        n = half * 20 + m
        return pltpu.make_async_remote_copy(
            src_ref=ref, dst_ref=ref, send_sem=zs.at[n], recv_sem=zr.at[n],
            device_id={"tensor": target}, device_id_type=MESH,
        )

    def both(step):
        def one(half, carry):
            step(half)
            return carry

        lax.fori_loop(0, 2, one, 0)

    def spread(half, index, d):
        j = block(half, d, 0)
        m = 4 + 4 * index
        tensor_copy(half, m, j, 0, block(half, 0, 1)).start()
        tensor_copy(half, m + 1, j, 1, block(half, 0, -1)).start()

    def tensor_start(half):
        tensor_copy(half, 0, g, 0, block(half, 1, 0)).start()
        tensor_copy(half, 1, g, 1, block(half, -1, 0)).start()

    def tensor_next(half):
        spread(half, 0, 0)

    def tensor_near(half):
        j = block(half, -1, 0)
        tensor_copy(half, 0, j, 0, g).wait_recv()
        tensor_copy(half, 2, j, 2, block(half, 1, 0)).start()
        spread(half, 1, -1)
        j = block(half, 1, 0)
        tensor_copy(half, 1, j, 1, g).wait_recv()
        tensor_copy(half, 3, j, 3, block(half, -1, 0)).start()
        spread(half, 2, 1)

    def tensor_far(half):
        j = block(half, 2, 0)
        tensor_copy(half, 2, j, 2, g).wait_recv()
        tensor_copy(half, 3, j, 3, g).wait_recv()
        spread(half, 3, 2)

    offsets = (0, -1, 1, 2)

    def forward(index):
        def step(half):
            m, d = 4 + 4 * index, offsets[index]
            j = block(half, d, -1)
            tensor_copy(half, m, j, 0, g).wait_recv()
            tensor_copy(half, m + 2, j, 2, block(half, 0, 1)).start()
            j = block(half, d, 1)
            tensor_copy(half, m + 1, j, 1, g).wait_recv()
            tensor_copy(half, m + 3, j, 3, block(half, 0, -1)).start()

        both(step)

    def finish(half, index):
        m, d = 4 + 4 * index, offsets[index]
        j = block(half, d, 2)
        tensor_copy(half, m + 2, j, 2, g).wait_recv()
        tensor_copy(half, m + 3, j, 3, g).wait_recv()

    def add_row(index):
        cols = pl.ds(pl.multiple_of(ring(z, offsets[index]) * 1280, 1280), 1280)
        dacc[...] += dot(wo[:, cols], go[cols, :])

    sibling = y * 2 + 1 - core

    def at_y(step):
        return ring(y, step) * 2 + core

    class Gather:
        def __init__(self, array, ref, rows):
            self.array, self.ref, self.rows = array, ref, rows

        def copy(self, m, slot, target):
            start, count = slot * self.rows, self.rows
            if m in (2, 3):
                count = self.rows // 2
                start = start + (m - 2) * count
            ref = self.ref.at[pl.ds(pl.multiple_of(start, count), count)]
            n = self.array * 8 + m
            return pltpu.make_async_remote_copy(
                src_ref=ref, dst_ref=ref, send_sem=ys.at[n], recv_sem=yr.at[n],
                device_id={"tm": target}, device_id_type=MESH,
            )

        def start(self):
            self.copy(0, me, at_y(1)).start()
            self.copy(1, me, at_y(-1)).start()
            self.copy(4, me, sibling).start()

        def near(self):
            self.copy(0, at_y(-1), me).wait_recv()
            self.copy(2, at_y(-1), at_y(1)).start()
            self.copy(5, at_y(-1), sibling).start()
            self.copy(1, at_y(1), me).wait_recv()
            self.copy(3, at_y(1), at_y(-1)).start()
            self.copy(6, at_y(1), sibling).start()

        def far(self):
            self.copy(2, at_y(2), me).wait_recv()
            self.copy(3, at_y(2), me).wait_recv()
            self.copy(7, at_y(2), sibling).start()

        def from_sibling(self, *messages):
            for m in messages:
                slot = ring(y, (0, -1, 1, 2)[m - 4]) * 2 + 1 - core
                self.copy(m, slot, me).wait_recv()

        def drain(self):
            for m in range(8):
                self.copy(m, me, me).wait_send()

    keys, queries = Gather(0, kall, F), Gather(1, qall, F)
    values, grads = Gather(2, vall, F), Gather(3, dall, F)
    totals, products = Gather(4, logs, 16), Gather(5, dots, 16)

    def by_arrival(gathers, body, events):
        def step(n, carry):
            ring_at = (n + 2) // 4
            hop = (ring_at % 2) * (2 * (n % 2) - 1) + (ring_at // 2) * 2
            other = (1 - ring_at % 2) * (n % 2) + (ring_at % 2) * (((n + 2) // 2) % 2)
            slot = ring(y, hop) * 2 + (core + other) % 2
            waits = {
                1: lambda item: item.from_sibling(4),
                4: lambda item: item.from_sibling(5, 6),
                6: lambda item: item.far(),
                7: lambda item: item.from_sibling(7),
            }
            for when in range(8):
                if when in waits or when in events:
                    @pl.when(n == when)
                    def _(when=when):
                        if when in events:
                            events[when]()
                        if when in waits:
                            for item in gathers:
                                waits[when](item)

            body(slot)
            return carry

        lax.fori_loop(0, 8, step, 0)

    lane = lax.broadcasted_iota(jnp.int32, (F, HD), 1)

    def head(ref, rows, h):
        return ref[rows, h * HD:(h + 1) * HD]

    def stat_row(ref, s, h):
        return ref[pl.ds(pl.multiple_of(s * 16 + h * 8, 8), 8), :][0:1, :]

    def to_row(ref, h, column):
        rows = pl.ds(pl.multiple_of(me * 16 + h * 8, 8), 8)
        ref[rows, :] = jnp.broadcast_to(column, (F, HD)).T[0:8, :]

    def factor(h, s, at=0, count=F):
        own = sums[h, at:at + count, :]
        return jnp.sum(jnp.where(lane[at:at + count] == s, own, 0.0), axis=1, keepdims=True)

    def softmax(s):
        width = band[my_frame, frame_map[s]]
        for h in (0, 1):
            scores = dot_nt(head(qall, mine, h), head(kall, slot_rows(s), h))
            scores = jnp.where(dist[...] <= width, scores, masked_score)
            top = jnp.max(scores, axis=1, keepdims=True) * POWER
            shifted = jnp.exp2(scores * POWER - top)
            total = jnp.sum(shifted, axis=1, keepdims=True)
            p[h, s] = low(shifted)
            tops[h] = jnp.where(lane == s, top, tops[h])
            sums[h] = jnp.where(lane == s, total, sums[h])

    def combine():
        for h in (0, 1):
            top = jnp.max(tops[h], axis=1, keepdims=True)
            shares = jnp.exp2(tops[h] - top)
            total = jnp.sum(shares * sums[h], axis=1, keepdims=True)
            sums[h] = shares / total
            to_row(logs, h, top + jnp.log2(total))

    def key_side(s):
        width = band[frame_map[s], my_frame]
        for h in (0, 1):
            scores = dot_nt(head(kall, mine, h), head(qall, slot_rows(s), h))
            power = jnp.where(
                dist[...] <= width, scores * POWER - stat_row(logs, s, h), masked_score
            )
            pt[h, s] = low(jnp.exp2(power))

    def attend(s):
        for h in (0, 1):
            att[h] += factor(h, s) * dot(p[h, s], head(vall, slot_rows(s), h))

    def query_grad(c, s):
        at, count = CHUNKS[c]
        rows, own = pl.ds(at, count), pl.ds(pl.multiple_of(me * F + at, 128), count)
        for h in (0, 1):
            grad = dot_nt(head(dall, own, h), head(vall, slot_rows(s), h))
            grad = low(grad - jnp.concatenate([row_dot[h, rows, :]] * 5, axis=1))
            product = dot(p[h, s, rows, :] * grad, head(kall, slot_rows(s), h))
            gq[h, rows, :] += factor(h, s, at, count) * product

    def key_grad(c, s):
        at, count = CHUNKS[c]
        rows, own = pl.ds(at, count), pl.ds(pl.multiple_of(me * F + at, 128), count)
        for h in (0, 1):
            grad_rows = head(dall, slot_rows(s), h)
            weight = pt[h, s, rows, :]
            grad = low(dot_nt(head(vall, own, h), grad_rows) - stat_row(dots, s, h))
            gv[h, rows, :] += dot(weight, grad_rows)
            gk[h, rows, :] += dot(weight * grad, head(qall, slot_rows(s), h))

    barrier = pltpu.get_barrier_semaphore()
    for half in (0, 1):
        for step in (1, -1):
            pl.semaphore_signal(
                barrier, inc=1, device_id={"tensor": block(half, step, 0)}, device_id_type=MESH
            )
    for target in (at_y(1), at_y(-1), sibling):
        pl.semaphore_signal(barrier, inc=1, device_id={"tm": target}, device_id_type=MESH)
    loads[0].wait()
    loads[1].wait()
    pl.semaphore_wait(barrier, 7)
    both(tensor_start)
    keys.start()
    both(tensor_next)
    across = lax.broadcasted_iota(jnp.int32, (F, F), 0) - lax.broadcasted_iota(jnp.int32, (F, F), 1)
    dist[...] = jnp.abs(across)
    for ref in (dacc, att, gq, sums):
        ref[...] = jnp.zeros_like(ref)
    tops[...] = jnp.full_like(tops, masked_score)
    for item in loads[2:]:
        item.wait()

    def keys_near():
        both(tensor_near)
        keys.near()
        queries.start()

    by_arrival(
        (keys,), softmax,
        {2: keys_near, 5: lambda: both(tensor_far), 7: lambda: forward(0)},
    )
    combine()
    totals.start()
    queries.near()
    values.start()
    totals.near()
    by_arrival(
        (queries, totals), key_side,
        {3: lambda: forward(1), 5: lambda: forward(2), 7: lambda: forward(3)},
    )
    values.near()
    by_arrival((values,), attend, {})
    for index in range(4):
        finish(0, index)
    for index in range(4):
        finish(1, index)
        add_row(index)
    dall[mine, :] = low(dacc[...].T)
    grads.start()
    for h in (0, 1):
        column = jnp.sum(wide(head(dall, mine, h)) * att[h], axis=1, keepdims=True)
        row_dot[h] = jnp.broadcast_to(column, (F, HD))
        to_row(dots, h, column)
    products.start()
    gk, gv = tops, att
    for ref in (gk, gv):
        ref[...] = jnp.zeros_like(ref)

    def to_gt(n, ref, scale, c):
        rows = pl.ds(*CHUNKS[c])
        for h in (0, 1):
            gt[n * 256 + h * HD:n * 256 + (h + 1) * HD, rows] = low((ref[h, rows, :] * scale).T)

    def drain(half):
        def one(i, carry):
            for kind in range(4):
                tensor_copy(half, 4 * i + kind, g, kind, g).wait_send()
            return carry

        lax.fori_loop(0, 5, one, 0)

    def target(half, d, e):
        return block(1 - half, d, e)

    def part(c, half, d, e, skip=0, count=160):
        start = target(half, d, e) * 320 + half * 160 + skip
        return go.at[pl.ds(pl.multiple_of(start, 16), count), pl.ds(*CHUNKS[c])]

    def got(c, ref, n):
        return wide(ref[n, :, pl.ds(*CHUNKS[c])])

    def first(c, m, half, d, e, step):
        n = half * 12 + m
        return pltpu.make_async_remote_copy(
            src_ref=part(c, half, d, e), dst_ref=in1.at[n, :, pl.ds(*CHUNKS[c])],
            send_sem=s1.at[c * 24 + n], recv_sem=r1.at[c * 24 + n],
            device_id={"tensor": target(half, step, 0)}, device_id_type=MESH,
        )

    def second(c, m, half, e, skip, step):
        n = half * 6 + m
        return pltpu.make_async_remote_copy(
            src_ref=part(c, half, 0, e, skip, 80), dst_ref=in2.at[n, :, pl.ds(*CHUNKS[c])],
            send_sem=s2.at[c * 12 + n], recv_sem=r2.at[c * 12 + n],
            device_id={"tensor": target(half, 0, step)}, device_id_type=MESH,
        )

    far = ((0, 2, 2, 1), (1, 2, 1, -1), (2, 2, 3, 1), (3, 2, 0, -1))
    alone = ((4, 1, 1, 1), (5, 3, 2, -1), (6, 1, 0, 1), (7, 3, 3, -1))
    summed = ((8, 1, 2, 1), (9, 3, 1, -1), (10, 1, 3, 1), (11, 3, 0, -1))

    def send(c, half, messages):
        for m, d, e, step in messages:
            first(c, m, half, d, e, step).start()

    def block_rows(j):
        k = j // 2
        dz = (k % 2) * (1 - k // 2) + (1 - k % 2) * (2 + k // 2)
        return pl.ds(pl.multiple_of(ring(z, dz) * 1280 + (j % 2) * F, F), F)

    def fetch(j):
        return [
            pltpu.make_async_copy(src.at[block_rows(j)], wbuf.at[j % 3, n], wsem.at[j % 3, n])
            for n, src in enumerate((wq_hbm, wk_hbm, wv_hbm))
        ]

    def start_fetch(j):
        for item in fetch(j):
            item.start()

    def multiply(c):
        tokens = pl.ds(*CHUNKS[c])

        def one(j, carry):
            for item in fetch(j):
                item.wait()

            left = jnp.concatenate([wbuf[j % 3, n] for n in range(3)], axis=1)
            go[block_rows(j), tokens] = low(dot(left, gt[:, tokens]))

            @pl.when(j < 5)
            def _():
                start_fetch(j + 3)

            events = {
                1: ((0, far), (1, (far[0], alone[1]))),
                3: ((1, (far[1], alone[0])), (0, (alone[0], alone[2]))),
                5: ((1, (far[2], alone[3])), (0, (alone[1], alone[3]))),
                7: ((1, (far[3], alone[2])),),
            }
            for when in events:
                @pl.when(j == when)
                def _(when=when):
                    for half, messages in events[when]:
                        send(c, half, messages)

            return carry

        lax.fori_loop(0, 8, one, 0)

    def pass_on(c, message):
        m, d, e, step = message

        def one(half):
            first(c, m - 8, half, d, e, step).wait_recv()
            ref = part(c, half, d, e)
            ref[...] = low(wide(ref[...]) + got(c, in1, half * 12 + m - 8))
            first(c, m, half, d, e, step).start()

        both(one)

    def collect(c, half, e, up, down):
        first(c, up, half, 0, e, 1).wait_recv()
        first(c, down, half, 0, e, 1).wait_recv()
        return wide(part(c, half, 0, e)[...]) + got(c, in1, half * 12 + up) + got(c, in1, half * 12 + down)

    def collect_far(c, half):
        part(c, half, 0, 2)[...] = low(collect(c, half, 2, 8, 5))
        second(c, 0, half, 2, 0, 1).start()
        second(c, 1, half, 2, 80, -1).start()

    def collect_next(c, half):
        total = collect(c, half, 1, 4, 9)
        part(c, half, 0, 1)[...] = low(total)
        second(c, 2, half, 1, 80, 1).start()
        second(c, 0, half, 1, 0, 1).wait_recv()
        part(c, half, 0, 1, 0, 80)[...] = low(total[0:80] + got(c, in2, half * 6))
        second(c, 3, half, 1, 0, 1).start()

    def collect_last(c, half):
        total = collect(c, half, 3, 10, 7)
        part(c, half, 0, 3)[...] = low(total)
        second(c, 4, half, 3, 0, -1).start()
        second(c, 1, half, 3, 80, -1).wait_recv()
        part(c, half, 0, 3, 80, 80)[...] = low(total[80:160] + got(c, in2, half * 6 + 1))
        second(c, 5, half, 3, 80, -1).start()

    def collect_own(c, half):
        total = collect(c, half, 0, 6, 11)
        for m in (2, 3, 4, 5):
            second(c, m, half, 0, 0, 1).wait_recv()
        at = pl.multiple_of(half * 160, 16)
        n, tokens = half * 6, pl.ds(*CHUNKS[c])
        out_ref[pl.ds(at, 80), tokens] = low(total[0:80] + (got(c, in2, n + 3) + got(c, in2, n + 4)))
        out_ref[pl.ds(at + 80, 80), tokens] = low(
            total[80:160] + (got(c, in2, n + 2) + got(c, in2, n + 5))
        )

    def scatter_steps(c):
        steps = [lambda message=message: pass_on(c, message) for message in summed]
        for collector in (collect_far, collect_next, collect_last, collect_own):
            steps.append(lambda collector=collector: both(lambda half: collector(c, half)))
        return steps

    def eight(body, events):
        def one(s, carry):
            body(s)
            for when in events:
                @pl.when(s == when)
                def _(when=when):
                    events[when]()

            return carry

        lax.fori_loop(0, 8, one, 0)

    def grads_near():
        grads.near()
        products.near()

    for j in range(3):
        start_fetch(j)
    eight(lambda s: query_grad(0, s), {7: grads_near})
    to_gt(0, gq, SCALE, 0)
    both(drain)
    by_arrival((grads, products), lambda s: key_grad(0, s), {})
    to_gt(1, gk, SCALE, 0)
    to_gt(2, gv, 1.0, 0)
    multiply(0)
    for j in range(3):
        start_fetch(j)
    steps = scatter_steps(0)
    eight(lambda s: query_grad(1, s), {4: steps[0], 5: steps[1], 6: steps[2], 7: steps[3]})
    to_gt(0, gq, SCALE, 1)
    eight(lambda s: key_grad(1, s), {6: steps[4]})
    to_gt(1, gk, SCALE, 1)
    to_gt(2, gv, 1.0, 1)
    multiply(1)
    for step in steps[5:] + scatter_steps(1):
        step()

    def sent1(m, carry):
        for c in (0, 1):
            first(c, m, 0, 0, 0, 1).wait_send()
        return carry

    def sent2(m, carry):
        for c in (0, 1):
            second(c, m, 0, 0, 0, 1).wait_send()
        return carry

    lax.fori_loop(0, 24, sent1, 0)
    lax.fori_loop(0, 12, sent2, 0)
    for item in (keys, queries, values, grads, totals, products):
        item.drain()


def per_device(queries, keys, values, grad_out, frame_map, band, w_query, w_key, w_value, w_out):
    vmem = pl.BlockSpec(memory_space=pltpu.VMEM)
    hbm = pl.BlockSpec(memory_space=pl.ANY)
    smem = pl.BlockSpec(memory_space=pltpu.SMEM)
    gathered = pltpu.VMEM((8 * F, 256), jnp.bfloat16)
    stats = pltpu.VMEM((128, F), jnp.float32)
    pairs = pltpu.VMEM((2, 8, F, F), jnp.bfloat16)
    heads = pltpu.VMEM((2, F, HD), jnp.float32)
    sems = pltpu.SemaphoreType.DMA
    return pl.pallas_call(
        kernel,
        out_shape=jax.ShapeDtypeStruct((320, F), jnp.bfloat16),
        in_specs=[smem] * 2 + [hbm] * 8,
        out_specs=vmem,
        scratch_shapes=[
            pltpu.VMEM((5120, F), jnp.bfloat16),
            pltpu.VMEM((256, 5120), jnp.bfloat16),
            gathered, gathered, gathered, gathered,
            stats, stats,
            pairs, pairs,
            pltpu.VMEM((F, F), jnp.int32),
            pltpu.VMEM((256, F), jnp.float32),
            heads, heads, heads, heads, heads,
            pltpu.VMEM((768, F), jnp.bfloat16),
            pltpu.VMEM((3, 3, F, 256), jnp.bfloat16),
            pltpu.VMEM((24, 160, F), jnp.bfloat16),
            pltpu.VMEM((12, 80, F), jnp.bfloat16),
            sems((6,)), sems((40,)), sems((40,)), sems((8 * ARRAYS,)), sems((8 * ARRAYS,)),
            sems((3, 3)), sems((48,)), sems((48,)), sems((24,)), sems((24,)),
        ],
        compiler_params=pltpu.CompilerParams(
            collective_id=0, has_side_effects=True, vmem_limit_bytes=64 * 1024 * 1024
        ),
        cost_estimate=pl.CostEstimate(
            flops=21_000_000_000, bytes_accessed=14_000_000, transcendentals=13_000_000
        ),
    )(frame_map, band, grad_out.T, w_out, queries, keys, values, w_query, w_key, w_value)


def solution(mesh):
    placed = (
        P("tm", "tensor"),
        P("tm", "tensor"),
        P("tm", "tensor"),
        P("tm", "tensor"),
        P(),
        P(),
        P(None, "tensor"),
        P(None, "tensor"),
        P(None, "tensor"),
        P("tensor", None),
    )
    return jax.shard_map(
        per_device, mesh=mesh, in_specs=placed, out_specs=P("tensor", "tm"), check_vma=False
    )
```

```python
import jax
import jax.numpy as jnp
from jax import lax
from jax.experimental import pallas as pl
from jax.experimental.pallas import tpu as pltpu
from jax.sharding import PartitionSpec as P

HD = 128
F = 640
SCALE = HD ** -0.5
POWER = SCALE * 1.4426950408889634
CHUNKS = ((0, 384), (384, 256))
ARRAYS = 6
MESH = pl.DeviceIdType.MESH
NT = (((1,), (1,)), ((), ()))
masked_score = -1e30


def dot(a, b):
    return jnp.dot(a, b, preferred_element_type=jnp.float32)


def dot_nt(a, b):
    return lax.dot_general(a, b, NT, preferred_element_type=jnp.float32)


def ring(position, step):
    return lax.rem(position + step + 4, 4)


def low(value):
    return value.astype(jnp.bfloat16)


def wide(value):
    return value.astype(jnp.float32)


def kernel(
    frame_map, band, go_hbm, wo_hbm, q_hbm, k_hbm, v_hbm, wq_hbm, wk_hbm, wv_hbm, out_ref,
    go, wo, kall, qall, vall, dall, logs, dots, p, pt, dist, dacc, att, gq,
    tops, sums, row_dot, gt, wbuf, in1, in2,
    load_sem, zs, zr, ys, yr, wsem, s1, r1, s2, r2,
):
    g = lax.axis_index("tensor")
    z, x = g // 4, g % 4
    me = lax.axis_index("tm")
    y, core = me // 2, me % 2
    my_frame = frame_map[me]

    def slot_rows(s):
        return pl.ds(pl.multiple_of(s * F, F), F)

    mine = slot_rows(me)

    def load(n, src, dst):
        return pltpu.make_async_copy(src, dst, load_sem.at[n])

    loads = [
        load(0, go_hbm, go.at[pl.ds(pl.multiple_of(g * 320, 320), 320)]),
        load(1, k_hbm, kall.at[mine]),
        load(2, q_hbm, qall.at[mine]),
        load(3, v_hbm, vall.at[mine]),
        load(4, wo_hbm, wo),
    ]
    for item in loads:
        item.start()

    def block(half, d, e):
        zz = ring(z, d * half + e * (1 - half))
        xx = ring(x, d * (1 - half) + e * half)
        return zz * 4 + xx

    def tensor_copy(half, m, j, kind, target):
        start = j * 320 + half * 160 + (80 if kind == 3 else 0)
        ref = go.at[pl.ds(pl.multiple_of(start, 16), 160 if kind < 2 else 80)]
        n = half * 20 + m
        return pltpu.make_async_remote_copy(
            src_ref=ref, dst_ref=ref, send_sem=zs.at[n], recv_sem=zr.at[n],
            device_id={"tensor": target}, device_id_type=MESH,
        )

    def both(step):
        def one(half, carry):
            step(half)
            return carry

        lax.fori_loop(0, 2, one, 0)

    def spread(half, index, d):
        j = block(half, d, 0)
        m = 4 + 4 * index
        tensor_copy(half, m, j, 0, block(half, 0, 1)).start()
        tensor_copy(half, m + 1, j, 1, block(half, 0, -1)).start()

    def tensor_start(half):
        tensor_copy(half, 0, g, 0, block(half, 1, 0)).start()
        tensor_copy(half, 1, g, 1, block(half, -1, 0)).start()

    def tensor_next(half):
        spread(half, 0, 0)

    def tensor_near(half):
        j = block(half, -1, 0)
        tensor_copy(half, 0, j, 0, g).wait_recv()
        tensor_copy(half, 2, j, 2, block(half, 1, 0)).start()
        spread(half, 1, -1)
        j = block(half, 1, 0)
        tensor_copy(half, 1, j, 1, g).wait_recv()
        tensor_copy(half, 3, j, 3, block(half, -1, 0)).start()
        spread(half, 2, 1)

    def tensor_far(half):
        j = block(half, 2, 0)
        tensor_copy(half, 2, j, 2, g).wait_recv()
        tensor_copy(half, 3, j, 3, g).wait_recv()
        spread(half, 3, 2)

    offsets = (0, -1, 1, 2)

    def forward(index):
        def step(half):
            m, d = 4 + 4 * index, offsets[index]
            j = block(half, d, -1)
            tensor_copy(half, m, j, 0, g).wait_recv()
            tensor_copy(half, m + 2, j, 2, block(half, 0, 1)).start()
            j = block(half, d, 1)
            tensor_copy(half, m + 1, j, 1, g).wait_recv()
            tensor_copy(half, m + 3, j, 3, block(half, 0, -1)).start()

        both(step)

    def finish(half, index):
        m, d = 4 + 4 * index, offsets[index]
        j = block(half, d, 2)
        tensor_copy(half, m + 2, j, 2, g).wait_recv()
        tensor_copy(half, m + 3, j, 3, g).wait_recv()

    def add_row(index):
        cols = pl.ds(pl.multiple_of(ring(z, offsets[index]) * 1280, 1280), 1280)
        dacc[...] += dot(wo[:, cols], go[cols, :])

    sibling = y * 2 + 1 - core

    def at_y(step):
        return ring(y, step) * 2 + core

    class Gather:
        def __init__(self, array, ref, rows):
            self.array, self.ref, self.rows = array, ref, rows

        def copy(self, m, slot, target):
            start, count = slot * self.rows, self.rows
            if m in (2, 3):
                count = self.rows // 2
                start = start + (m - 2) * count
            ref = self.ref.at[pl.ds(pl.multiple_of(start, count), count)]
            n = self.array * 8 + m
            return pltpu.make_async_remote_copy(
                src_ref=ref, dst_ref=ref, send_sem=ys.at[n], recv_sem=yr.at[n],
                device_id={"tm": target}, device_id_type=MESH,
            )

        def start(self):
            self.copy(0, me, at_y(1)).start()
            self.copy(1, me, at_y(-1)).start()
            self.copy(4, me, sibling).start()

        def near(self):
            self.copy(0, at_y(-1), me).wait_recv()
            self.copy(2, at_y(-1), at_y(1)).start()
            self.copy(5, at_y(-1), sibling).start()
            self.copy(1, at_y(1), me).wait_recv()
            self.copy(3, at_y(1), at_y(-1)).start()
            self.copy(6, at_y(1), sibling).start()

        def far(self):
            self.copy(2, at_y(2), me).wait_recv()
            self.copy(3, at_y(2), me).wait_recv()
            self.copy(7, at_y(2), sibling).start()

        def from_sibling(self, *messages):
            for m in messages:
                slot = ring(y, (0, -1, 1, 2)[m - 4]) * 2 + 1 - core
                self.copy(m, slot, me).wait_recv()

        def drain(self):
            for m in range(8):
                self.copy(m, me, me).wait_send()

    keys, queries = Gather(0, kall, F), Gather(1, qall, F)
    values, grads = Gather(2, vall, F), Gather(3, dall, F)
    totals, products = Gather(4, logs, 16), Gather(5, dots, 16)

    def by_arrival(gathers, body, events):
        def step(n, carry):
            ring_at = (n + 2) // 4
            hop = (ring_at % 2) * (2 * (n % 2) - 1) + (ring_at // 2) * 2
            other = (1 - ring_at % 2) * (n % 2) + (ring_at % 2) * (((n + 2) // 2) % 2)
            slot = ring(y, hop) * 2 + (core + other) % 2
            waits = {
                1: lambda item: item.from_sibling(4),
                4: lambda item: item.from_sibling(5, 6),
                6: lambda item: item.far(),
                7: lambda item: item.from_sibling(7),
            }
            for when in range(8):
                if when in waits or when in events:
                    @pl.when(n == when)
                    def _(when=when):
                        if when in events:
                            events[when]()
                        if when in waits:
                            for item in gathers:
                                waits[when](item)

            body(slot)
            return carry

        lax.fori_loop(0, 8, step, 0)

    lane = lax.broadcasted_iota(jnp.int32, (F, HD), 1)

    def head(ref, rows, h):
        return ref[rows, h * HD:(h + 1) * HD]

    def stat_row(ref, s, h):
        return ref[pl.ds(pl.multiple_of(s * 16 + h * 8, 8), 8), :][0:1, :]

    def to_row(ref, h, column):
        rows = pl.ds(pl.multiple_of(me * 16 + h * 8, 8), 8)
        ref[rows, :] = jnp.broadcast_to(column, (F, HD)).T[0:8, :]

    def factor(h, s, at=0, count=F):
        own = sums[h, at:at + count, :]
        return jnp.sum(jnp.where(lane[at:at + count] == s, own, 0.0), axis=1, keepdims=True)

    def softmax(s):
        width = band[my_frame, frame_map[s]]
        for h in (0, 1):
            scores = dot_nt(head(qall, mine, h), head(kall, slot_rows(s), h))
            scores = jnp.where(dist[...] <= width, scores, masked_score)
            top = jnp.max(scores, axis=1, keepdims=True) * POWER
            shifted = jnp.exp2(scores * POWER - top)
            total = jnp.sum(shifted, axis=1, keepdims=True)
            p[h, s] = low(shifted)
            tops[h] = jnp.where(lane == s, top, tops[h])
            sums[h] = jnp.where(lane == s, total, sums[h])

    def combine():
        for h in (0, 1):
            top = jnp.max(tops[h], axis=1, keepdims=True)
            shares = jnp.exp2(tops[h] - top)
            total = jnp.sum(shares * sums[h], axis=1, keepdims=True)
            sums[h] = shares / total
            to_row(logs, h, top + jnp.log2(total))

    def key_side(s):
        width = band[frame_map[s], my_frame]
        for h in (0, 1):
            scores = dot_nt(head(kall, mine, h), head(qall, slot_rows(s), h))
            power = jnp.where(
                dist[...] <= width, scores * POWER - stat_row(logs, s, h), masked_score
            )
            pt[h, s] = low(jnp.exp2(power))

    def attend(s):
        for h in (0, 1):
            att[h] += factor(h, s) * dot(p[h, s], head(vall, slot_rows(s), h))

    def query_grad(c, s):
        at, count = CHUNKS[c]
        rows, own = pl.ds(at, count), pl.ds(pl.multiple_of(me * F + at, 128), count)
        for h in (0, 1):
            grad = dot_nt(head(dall, own, h), head(vall, slot_rows(s), h))
            grad = low(grad - jnp.concatenate([row_dot[h, rows, :]] * 5, axis=1))
            product = dot(p[h, s, rows, :] * grad, head(kall, slot_rows(s), h))
            gq[h, rows, :] += factor(h, s, at, count) * product

    def key_grad(c, s):
        at, count = CHUNKS[c]
        rows, own = pl.ds(at, count), pl.ds(pl.multiple_of(me * F + at, 128), count)
        for h in (0, 1):
            grad_rows = head(dall, slot_rows(s), h)
            weight = pt[h, s, rows, :]
            grad = low(dot_nt(head(vall, own, h), grad_rows) - stat_row(dots, s, h))
            gv[h, rows, :] += dot(weight, grad_rows)
            gk[h, rows, :] += dot(weight * grad, head(qall, slot_rows(s), h))

    barrier = pltpu.get_barrier_semaphore()
    for half in (0, 1):
        for step in (1, -1):
            pl.semaphore_signal(
                barrier, inc=1, device_id={"tensor": block(half, step, 0)}, device_id_type=MESH
            )
    for target in (at_y(1), at_y(-1), sibling):
        pl.semaphore_signal(barrier, inc=1, device_id={"tm": target}, device_id_type=MESH)
    loads[0].wait()
    loads[1].wait()
    pl.semaphore_wait(barrier, 7)
    both(tensor_start)
    keys.start()
    both(tensor_next)
    across = lax.broadcasted_iota(jnp.int32, (F, F), 0) - lax.broadcasted_iota(jnp.int32, (F, F), 1)
    dist[...] = jnp.abs(across)
    for ref in (dacc, att, gq, sums):
        ref[...] = jnp.zeros_like(ref)
    tops[...] = jnp.full_like(tops, masked_score)
    for item in loads[2:]:
        item.wait()

    def keys_near():
        both(tensor_near)
        keys.near()
        queries.start()

    by_arrival(
        (keys,), softmax,
        {2: keys_near, 5: lambda: both(tensor_far), 7: lambda: forward(0)},
    )
    queries.near()
    values.start()
    combine()
    totals.start()
    totals.near()
    by_arrival(
        (queries, totals), key_side,
        {3: lambda: forward(1), 5: lambda: forward(2), 7: lambda: forward(3)},
    )
    values.near()

    def near_row(index):
        finish(1, index)
        add_row(index)

    near_row(0)
    by_arrival((values,), attend, {4: lambda: near_row(1), 6: lambda: near_row(2)})
    for index in range(4):
        finish(0, index)
    near_row(3)
    dall[mine, :] = low(dacc[...].T)
    grads.start()
    for h in (0, 1):
        column = jnp.sum(wide(head(dall, mine, h)) * att[h], axis=1, keepdims=True)
        row_dot[h] = jnp.broadcast_to(column, (F, HD))
        to_row(dots, h, column)
    products.start()
    gk, gv = tops, att
    for ref in (gk, gv):
        ref[...] = jnp.zeros_like(ref)

    def to_gt(n, ref, scale, c):
        rows = pl.ds(*CHUNKS[c])
        for h in (0, 1):
            gt[n * 256 + h * HD:n * 256 + (h + 1) * HD, rows] = low((ref[h, rows, :] * scale).T)

    def drain(half):
        def one(i, carry):
            for kind in range(4):
                tensor_copy(half, 4 * i + kind, g, kind, g).wait_send()
            return carry

        lax.fori_loop(0, 5, one, 0)

    def target(half, d, e):
        return block(1 - half, d, e)

    def part(c, half, d, e, skip=0, count=160):
        start = target(half, d, e) * 320 + half * 160 + skip
        return go.at[pl.ds(pl.multiple_of(start, 16), count), pl.ds(*CHUNKS[c])]

    def got(c, ref, n):
        return wide(ref[n, :, pl.ds(*CHUNKS[c])])

    def first(c, m, half, d, e, step):
        n = half * 12 + m
        return pltpu.make_async_remote_copy(
            src_ref=part(c, half, d, e), dst_ref=in1.at[n, :, pl.ds(*CHUNKS[c])],
            send_sem=s1.at[c * 24 + n], recv_sem=r1.at[c * 24 + n],
            device_id={"tensor": target(half, step, 0)}, device_id_type=MESH,
        )

    def second(c, m, half, e, skip, step):
        n = half * 6 + m
        return pltpu.make_async_remote_copy(
            src_ref=part(c, half, 0, e, skip, 80), dst_ref=in2.at[n, :, pl.ds(*CHUNKS[c])],
            send_sem=s2.at[c * 12 + n], recv_sem=r2.at[c * 12 + n],
            device_id={"tensor": target(half, 0, step)}, device_id_type=MESH,
        )

    far = ((0, 2, 2, 1), (1, 2, 1, -1), (2, 2, 3, 1), (3, 2, 0, -1))
    alone = ((4, 1, 1, 1), (5, 3, 2, -1), (6, 1, 0, 1), (7, 3, 3, -1))
    summed = ((8, 1, 2, 1), (9, 3, 1, -1), (10, 1, 3, 1), (11, 3, 0, -1))

    def send(c, half, messages):
        for m, d, e, step in messages:
            first(c, m, half, d, e, step).start()

    def block_rows(j):
        k = j // 2
        dz = (k % 2) * (1 - k // 2) + (1 - k % 2) * (2 + k // 2)
        return pl.ds(pl.multiple_of(ring(z, dz) * 1280 + (j % 2) * F, F), F)

    def fetch(j):
        return [
            pltpu.make_async_copy(src.at[block_rows(j)], wbuf.at[j % 3, n], wsem.at[j % 3, n])
            for n, src in enumerate((wq_hbm, wk_hbm, wv_hbm))
        ]

    def start_fetch(j):
        for item in fetch(j):
            item.start()

    def multiply(c):
        tokens = pl.ds(*CHUNKS[c])

        def one(j, carry):
            for item in fetch(j):
                item.wait()

            left = jnp.concatenate([wbuf[j % 3, n] for n in range(3)], axis=1)
            go[block_rows(j), tokens] = low(dot(left, gt[:, tokens]))

            @pl.when(j < 5)
            def _():
                start_fetch(j + 3)

            events = {
                1: ((0, far), (1, (far[0], alone[1]))),
                3: ((1, (far[1], alone[0])), (0, (alone[0], alone[2]))),
                5: ((1, (far[2], alone[3])), (0, (alone[1], alone[3]))),
                7: ((1, (far[3], alone[2])),),
            }
            for when in events:
                @pl.when(j == when)
                def _(when=when):
                    for half, messages in events[when]:
                        send(c, half, messages)

            return carry

        lax.fori_loop(0, 8, one, 0)

    def pass_on(c, message):
        m, d, e, step = message

        def one(half):
            first(c, m - 8, half, d, e, step).wait_recv()
            ref = part(c, half, d, e)
            ref[...] = low(wide(ref[...]) + got(c, in1, half * 12 + m - 8))
            first(c, m, half, d, e, step).start()

        both(one)

    def collect(c, half, e, up, down):
        first(c, up, half, 0, e, 1).wait_recv()
        first(c, down, half, 0, e, 1).wait_recv()
        return wide(part(c, half, 0, e)[...]) + got(c, in1, half * 12 + up) + got(c, in1, half * 12 + down)

    def collect_far(c, half):
        part(c, half, 0, 2)[...] = low(collect(c, half, 2, 8, 5))
        second(c, 0, half, 2, 0, 1).start()
        second(c, 1, half, 2, 80, -1).start()

    def collect_next(c, half):
        part(c, half, 0, 1)[...] = low(collect(c, half, 1, 4, 9))
        second(c, 2, half, 1, 80, 1).start()

    def collect_last(c, half):
        part(c, half, 0, 3)[...] = low(collect(c, half, 3, 10, 7))
        second(c, 4, half, 3, 0, -1).start()

    def add_next(c, half):
        second(c, 0, half, 1, 0, 1).wait_recv()
        ref = part(c, half, 0, 1, 0, 80)
        ref[...] = low(wide(ref[...]) + got(c, in2, half * 6))
        second(c, 3, half, 1, 0, 1).start()

    def add_last(c, half):
        second(c, 1, half, 3, 80, -1).wait_recv()
        ref = part(c, half, 0, 3, 80, 80)
        ref[...] = low(wide(ref[...]) + got(c, in2, half * 6 + 1))
        second(c, 5, half, 3, 80, -1).start()

    def collect_own(c, half):
        total = collect(c, half, 0, 6, 11)
        for m in (2, 3, 4, 5):
            second(c, m, half, 0, 0, 1).wait_recv()
        at = pl.multiple_of(half * 160, 16)
        n, tokens = half * 6, pl.ds(*CHUNKS[c])
        out_ref[pl.ds(at, 80), tokens] = low(total[0:80] + (got(c, in2, n + 3) + got(c, in2, n + 4)))
        out_ref[pl.ds(at + 80, 80), tokens] = low(
            total[80:160] + (got(c, in2, n + 2) + got(c, in2, n + 5))
        )

    def scatter_steps(c):
        steps = [lambda message=message: pass_on(c, message) for message in summed]
        for collector in (collect_far, collect_next, collect_last, add_next, add_last, collect_own):
            steps.append(lambda collector=collector: both(lambda half: collector(c, half)))
        return steps

    def eight(body, events):
        def one(s, carry):
            body(s)
            for when in events:
                @pl.when(s == when)
                def _(when=when):
                    events[when]()

            return carry

        lax.fori_loop(0, 8, one, 0)

    def grads_near():
        grads.near()
        products.near()

    for j in range(3):
        start_fetch(j)
    eight(lambda s: query_grad(0, s), {7: grads_near})
    to_gt(0, gq, SCALE, 0)
    both(drain)
    by_arrival((grads, products), lambda s: key_grad(0, s), {})
    to_gt(1, gk, SCALE, 0)
    to_gt(2, gv, 1.0, 0)
    multiply(0)
    for j in range(3):
        start_fetch(j)
    steps = scatter_steps(0)
    eight(lambda s: query_grad(1, s), {4: steps[0], 5: steps[1], 6: steps[2], 7: steps[3]})
    to_gt(0, gq, SCALE, 1)
    eight(lambda s: key_grad(1, s), {6: steps[4]})
    to_gt(1, gk, SCALE, 1)
    to_gt(2, gv, 1.0, 1)
    multiply(1)
    rest = scatter_steps(1)
    for step in steps[5:9] + rest[:4] + steps[9:] + rest[4:]:
        step()

    def sent1(m, carry):
        for c in (0, 1):
            first(c, m, 0, 0, 0, 1).wait_send()
        return carry

    def sent2(m, carry):
        for c in (0, 1):
            second(c, m, 0, 0, 0, 1).wait_send()
        return carry

    lax.fori_loop(0, 24, sent1, 0)
    lax.fori_loop(0, 12, sent2, 0)
    for item in (keys, queries, values, grads, totals, products):
        item.drain()


def per_device(queries, keys, values, grad_out, frame_map, band, w_query, w_key, w_value, w_out):
    vmem = pl.BlockSpec(memory_space=pltpu.VMEM)
    hbm = pl.BlockSpec(memory_space=pl.ANY)
    smem = pl.BlockSpec(memory_space=pltpu.SMEM)
    gathered = pltpu.VMEM((8 * F, 256), jnp.bfloat16)
    stats = pltpu.VMEM((128, F), jnp.float32)
    pairs = pltpu.VMEM((2, 8, F, F), jnp.bfloat16)
    heads = pltpu.VMEM((2, F, HD), jnp.float32)
    sems = pltpu.SemaphoreType.DMA
    return pl.pallas_call(
        kernel,
        out_shape=jax.ShapeDtypeStruct((320, F), jnp.bfloat16),
        in_specs=[smem] * 2 + [hbm] * 8,
        out_specs=vmem,
        scratch_shapes=[
            pltpu.VMEM((5120, F), jnp.bfloat16),
            pltpu.VMEM((256, 5120), jnp.bfloat16),
            gathered, gathered, gathered, gathered,
            stats, stats,
            pairs, pairs,
            pltpu.VMEM((F, F), jnp.int32),
            pltpu.VMEM((256, F), jnp.float32),
            heads, heads, heads, heads, heads,
            pltpu.VMEM((768, F), jnp.bfloat16),
            pltpu.VMEM((3, 3, F, 256), jnp.bfloat16),
            pltpu.VMEM((24, 160, F), jnp.bfloat16),
            pltpu.VMEM((12, 80, F), jnp.bfloat16),
            sems((6,)), sems((40,)), sems((40,)), sems((8 * ARRAYS,)), sems((8 * ARRAYS,)),
            sems((3, 3)), sems((48,)), sems((48,)), sems((24,)), sems((24,)),
        ],
        compiler_params=pltpu.CompilerParams(
            collective_id=0, has_side_effects=True, vmem_limit_bytes=64 * 1024 * 1024
        ),
        cost_estimate=pl.CostEstimate(
            flops=21_000_000_000, bytes_accessed=14_000_000, transcendentals=13_000_000
        ),
    )(frame_map, band, grad_out.T, w_out, queries, keys, values, w_query, w_key, w_value)


def solution(mesh):
    placed = (
        P("tm", "tensor"),
        P("tm", "tensor"),
        P("tm", "tensor"),
        P("tm", "tensor"),
        P(),
        P(),
        P(None, "tensor"),
        P(None, "tensor"),
        P(None, "tensor"),
        P("tensor", None),
    )
    return jax.shard_map(
        per_device, mesh=mesh, in_specs=placed, out_specs=P("tensor", "tm"), check_vma=False
    )
```

```python
import jax
import jax.numpy as jnp
from jax import lax
from jax.experimental import pallas as pl
from jax.experimental.pallas import tpu as pltpu
from jax.sharding import PartitionSpec as P

HD = 128
F = 640
SCALE = HD ** -0.5
POWER = SCALE * 1.4426950408889634
CHUNKS = ((0, 256), (256, 384))
ARRAYS = 6
MESH = pl.DeviceIdType.MESH
NT = (((1,), (1,)), ((), ()))
masked_score = -1e30


def dot(a, b):
    return jnp.dot(a, b, preferred_element_type=jnp.float32)


def dot_nt(a, b):
    return lax.dot_general(a, b, NT, preferred_element_type=jnp.float32)


def ring(position, step):
    return lax.rem(position + step + 4, 4)


def low(value):
    return value.astype(jnp.bfloat16)


def wide(value):
    return value.astype(jnp.float32)


def kernel(
    frame_map, band, go_hbm, wo_hbm, q_hbm, k_hbm, v_hbm, wq_hbm, wk_hbm, wv_hbm, out_ref,
    go, wo, kall, qall, vall, dall, logs, dots, p, pt, dist, dacc, att, gq,
    tops, sums, row_dot, gt, wbuf, in1, in2,
    load_sem, zs, zr, ys, yr, wsem, s1, r1, s2, r2,
):
    g = lax.axis_index("tensor")
    z, x = g // 4, g % 4
    me = lax.axis_index("tm")
    y, core = me // 2, me % 2
    my_frame = frame_map[me]

    def slot_rows(s):
        return pl.ds(pl.multiple_of(s * F, F), F)

    mine = slot_rows(me)

    def load(n, src, dst):
        return pltpu.make_async_copy(src, dst, load_sem.at[n])

    loads = [
        load(0, go_hbm, go.at[pl.ds(pl.multiple_of(g * 320, 320), 320)]),
        load(1, k_hbm, kall.at[mine]),
        load(2, q_hbm, qall.at[mine]),
        load(3, v_hbm, vall.at[mine]),
        load(4, wo_hbm, wo),
    ]
    for item in loads:
        item.start()

    def block(half, d, e):
        zz = ring(z, d * half + e * (1 - half))
        xx = ring(x, d * (1 - half) + e * half)
        return zz * 4 + xx

    def tensor_copy(half, m, j, kind, target):
        start = j * 320 + half * 160 + (80 if kind == 3 else 0)
        ref = go.at[pl.ds(pl.multiple_of(start, 16), 160 if kind < 2 else 80)]
        n = half * 20 + m
        return pltpu.make_async_remote_copy(
            src_ref=ref, dst_ref=ref, send_sem=zs.at[n], recv_sem=zr.at[n],
            device_id={"tensor": target}, device_id_type=MESH,
        )

    def both(step):
        def one(half, carry):
            step(half)
            return carry

        lax.fori_loop(0, 2, one, 0)

    def spread(half, index, d):
        j = block(half, d, 0)
        m = 4 + 4 * index
        tensor_copy(half, m, j, 0, block(half, 0, 1)).start()
        tensor_copy(half, m + 1, j, 1, block(half, 0, -1)).start()

    def tensor_start(half):
        tensor_copy(half, 0, g, 0, block(half, 1, 0)).start()
        tensor_copy(half, 1, g, 1, block(half, -1, 0)).start()

    def tensor_next(half):
        spread(half, 0, 0)

    def tensor_near(half):
        j = block(half, -1, 0)
        tensor_copy(half, 0, j, 0, g).wait_recv()
        tensor_copy(half, 2, j, 2, block(half, 1, 0)).start()
        spread(half, 1, -1)
        j = block(half, 1, 0)
        tensor_copy(half, 1, j, 1, g).wait_recv()
        tensor_copy(half, 3, j, 3, block(half, -1, 0)).start()
        spread(half, 2, 1)

    def tensor_far(half):
        j = block(half, 2, 0)
        tensor_copy(half, 2, j, 2, g).wait_recv()
        tensor_copy(half, 3, j, 3, g).wait_recv()
        spread(half, 3, 2)

    offsets = (0, -1, 1, 2)

    def forward(index):
        def step(half):
            m, d = 4 + 4 * index, offsets[index]
            j = block(half, d, -1)
            tensor_copy(half, m, j, 0, g).wait_recv()
            tensor_copy(half, m + 2, j, 2, block(half, 0, 1)).start()
            j = block(half, d, 1)
            tensor_copy(half, m + 1, j, 1, g).wait_recv()
            tensor_copy(half, m + 3, j, 3, block(half, 0, -1)).start()

        both(step)

    def finish(half, index):
        m, d = 4 + 4 * index, offsets[index]
        j = block(half, d, 2)
        tensor_copy(half, m + 2, j, 2, g).wait_recv()
        tensor_copy(half, m + 3, j, 3, g).wait_recv()

    def add_row(index):
        cols = pl.ds(pl.multiple_of(ring(z, offsets[index]) * 1280, 1280), 1280)
        dacc[...] += dot(wo[:, cols], go[cols, :])

    sibling = y * 2 + 1 - core

    def at_y(step):
        return ring(y, step) * 2 + core

    class Gather:
        def __init__(self, array, ref, rows):
            self.array, self.ref, self.rows = array, ref, rows

        def copy(self, m, slot, target):
            start, count = slot * self.rows, self.rows
            if m in (2, 3):
                count = self.rows // 2
                start = start + (m - 2) * count
            ref = self.ref.at[pl.ds(pl.multiple_of(start, count), count)]
            n = self.array * 8 + m
            return pltpu.make_async_remote_copy(
                src_ref=ref, dst_ref=ref, send_sem=ys.at[n], recv_sem=yr.at[n],
                device_id={"tm": target}, device_id_type=MESH,
            )

        def start(self):
            self.copy(0, me, at_y(1)).start()
            self.copy(1, me, at_y(-1)).start()
            self.copy(4, me, sibling).start()

        def near(self):
            self.copy(0, at_y(-1), me).wait_recv()
            self.copy(2, at_y(-1), at_y(1)).start()
            self.copy(5, at_y(-1), sibling).start()
            self.copy(1, at_y(1), me).wait_recv()
            self.copy(3, at_y(1), at_y(-1)).start()
            self.copy(6, at_y(1), sibling).start()

        def far(self):
            self.copy(2, at_y(2), me).wait_recv()
            self.copy(3, at_y(2), me).wait_recv()
            self.copy(7, at_y(2), sibling).start()

        def from_sibling(self, *messages):
            for m in messages:
                slot = ring(y, (0, -1, 1, 2)[m - 4]) * 2 + 1 - core
                self.copy(m, slot, me).wait_recv()

        def drain(self):
            for m in range(8):
                self.copy(m, me, me).wait_send()

    keys, queries = Gather(0, kall, F), Gather(1, qall, F)
    values, grads = Gather(2, vall, F), Gather(3, dall, F)
    totals, products = Gather(4, logs, 16), Gather(5, dots, 16)

    def by_arrival(gathers, body, events):
        def step(n, carry):
            ring_at = (n + 2) // 4
            hop = (ring_at % 2) * (2 * (n % 2) - 1) + (ring_at // 2) * 2
            other = (1 - ring_at % 2) * (n % 2) + (ring_at % 2) * (((n + 2) // 2) % 2)
            slot = ring(y, hop) * 2 + (core + other) % 2
            waits = {
                1: lambda item: item.from_sibling(4),
                4: lambda item: item.from_sibling(5, 6),
                6: lambda item: item.far(),
                7: lambda item: item.from_sibling(7),
            }
            for when in range(8):
                if when in waits or when in events:
                    @pl.when(n == when)
                    def _(when=when):
                        if when in events:
                            events[when]()
                        if when in waits:
                            for item in gathers:
                                waits[when](item)

            body(slot)
            return carry

        lax.fori_loop(0, 8, step, 0)

    lane = lax.broadcasted_iota(jnp.int32, (F, HD), 1)

    def head(ref, rows, h):
        return ref[rows, h * HD:(h + 1) * HD]

    def stat_row(ref, s, h):
        return ref[pl.ds(pl.multiple_of(s * 16 + h * 8, 8), 8), :][0:1, :]

    def to_row(ref, h, column):
        rows = pl.ds(pl.multiple_of(me * 16 + h * 8, 8), 8)
        ref[rows, :] = jnp.broadcast_to(column, (F, HD)).T[0:8, :]

    def factor(h, s, at=0, count=F):
        own = sums[h, at:at + count, :]
        return jnp.sum(jnp.where(lane[at:at + count] == s, own, 0.0), axis=1, keepdims=True)

    def softmax(s):
        width = band[my_frame, frame_map[s]]
        for h in (0, 1):
            scores = dot_nt(head(qall, mine, h), head(kall, slot_rows(s), h))
            scores = jnp.where(dist[...] <= width, scores, masked_score)
            top = jnp.max(scores, axis=1, keepdims=True) * POWER
            shifted = jnp.exp2(scores * POWER - top)
            total = jnp.sum(shifted, axis=1, keepdims=True)
            p[h, s] = low(shifted)
            tops[h] = jnp.where(lane == s, top, tops[h])
            sums[h] = jnp.where(lane == s, total, sums[h])

    def combine():
        for h in (0, 1):
            top = jnp.max(tops[h], axis=1, keepdims=True)
            shares = jnp.exp2(tops[h] - top)
            total = jnp.sum(shares * sums[h], axis=1, keepdims=True)
            sums[h] = shares / total
            to_row(logs, h, top + jnp.log2(total))

    def key_side(s):
        width = band[frame_map[s], my_frame]
        for h in (0, 1):
            scores = dot_nt(head(kall, mine, h), head(qall, slot_rows(s), h))
            power = jnp.where(
                dist[...] <= width, scores * POWER - stat_row(logs, s, h), masked_score
            )
            pt[h, s] = low(jnp.exp2(power))

    def attend(s):
        for h in (0, 1):
            att[h] += factor(h, s) * dot(p[h, s], head(vall, slot_rows(s), h))

    def query_grad(c, s):
        at, count = CHUNKS[c]
        rows, own = pl.ds(at, count), pl.ds(pl.multiple_of(me * F + at, 128), count)
        for h in (0, 1):
            grad = dot_nt(head(dall, own, h), head(vall, slot_rows(s), h))
            grad = low(grad - jnp.concatenate([row_dot[h, rows, :]] * 5, axis=1))
            product = dot(p[h, s, rows, :] * grad, head(kall, slot_rows(s), h))
            gq[h, rows, :] += factor(h, s, at, count) * product

    def key_grad(c, s):
        at, count = CHUNKS[c]
        rows, own = pl.ds(at, count), pl.ds(pl.multiple_of(me * F + at, 128), count)
        for h in (0, 1):
            grad_rows = head(dall, slot_rows(s), h)
            weight = pt[h, s, rows, :]
            grad = low(dot_nt(head(vall, own, h), grad_rows) - stat_row(dots, s, h))
            gv[h, rows, :] += dot(weight, grad_rows)
            gk[h, rows, :] += dot(weight * grad, head(qall, slot_rows(s), h))

    barrier = pltpu.get_barrier_semaphore()
    for half in (0, 1):
        for step in (1, -1):
            pl.semaphore_signal(
                barrier, inc=1, device_id={"tensor": block(half, step, 0)}, device_id_type=MESH
            )
    for target in (at_y(1), at_y(-1), sibling):
        pl.semaphore_signal(barrier, inc=1, device_id={"tm": target}, device_id_type=MESH)
    loads[0].wait()
    loads[1].wait()
    pl.semaphore_wait(barrier, 7)
    both(tensor_start)
    keys.start()
    both(tensor_next)
    across = lax.broadcasted_iota(jnp.int32, (F, F), 0) - lax.broadcasted_iota(jnp.int32, (F, F), 1)
    dist[...] = jnp.abs(across)
    for ref in (dacc, att, gq, sums):
        ref[...] = jnp.zeros_like(ref)
    tops[...] = jnp.full_like(tops, masked_score)
    for item in loads[2:]:
        item.wait()

    def keys_near():
        both(tensor_near)
        keys.near()
        queries.start()

    by_arrival(
        (keys,), softmax,
        {2: keys_near, 5: lambda: both(tensor_far), 7: lambda: forward(0)},
    )
    queries.near()
    values.start()
    combine()
    totals.start()
    totals.near()
    by_arrival(
        (queries, totals), key_side,
        {3: lambda: forward(1), 5: lambda: forward(2), 7: lambda: forward(3)},
    )
    values.near()

    def near_row(index):
        finish(1, index)
        add_row(index)

    near_row(0)
    by_arrival((values,), attend, {4: lambda: near_row(1), 6: lambda: near_row(2)})
    for index in range(4):
        finish(0, index)
    near_row(3)
    dall[mine, :] = low(dacc[...].T)
    grads.start()
    for h in (0, 1):
        column = jnp.sum(wide(head(dall, mine, h)) * att[h], axis=1, keepdims=True)
        row_dot[h] = jnp.broadcast_to(column, (F, HD))
        to_row(dots, h, column)
    products.start()
    gk, gv = tops, att
    for ref in (gk, gv):
        ref[...] = jnp.zeros_like(ref)

    def to_gt(n, ref, scale, c):
        rows = pl.ds(*CHUNKS[c])
        for h in (0, 1):
            gt[n * 256 + h * HD:n * 256 + (h + 1) * HD, rows] = low((ref[h, rows, :] * scale).T)

    def drain(half):
        def one(i, carry):
            for kind in range(4):
                tensor_copy(half, 4 * i + kind, g, kind, g).wait_send()
            return carry

        lax.fori_loop(0, 5, one, 0)

    def target(half, d, e):
        return block(1 - half, d, e)

    def part(c, half, d, e, skip=0, count=160):
        start = target(half, d, e) * 320 + half * 160 + skip
        return go.at[pl.ds(pl.multiple_of(start, 16), count), pl.ds(*CHUNKS[c])]

    def got(c, ref, n):
        return wide(ref[n, :, pl.ds(*CHUNKS[c])])

    def first(c, m, half, d, e, step):
        n = half * 12 + m
        return pltpu.make_async_remote_copy(
            src_ref=part(c, half, d, e), dst_ref=in1.at[n, :, pl.ds(*CHUNKS[c])],
            send_sem=s1.at[c * 24 + n], recv_sem=r1.at[c * 24 + n],
            device_id={"tensor": target(half, step, 0)}, device_id_type=MESH,
        )

    def second(c, m, half, e, skip, step):
        n = half * 6 + m
        return pltpu.make_async_remote_copy(
            src_ref=part(c, half, 0, e, skip, 80), dst_ref=in2.at[n, :, pl.ds(*CHUNKS[c])],
            send_sem=s2.at[c * 12 + n], recv_sem=r2.at[c * 12 + n],
            device_id={"tensor": target(half, 0, step)}, device_id_type=MESH,
        )

    far = ((0, 2, 2, 1), (1, 2, 1, -1), (2, 2, 3, 1), (3, 2, 0, -1))
    alone = ((4, 1, 1, 1), (5, 3, 2, -1), (6, 1, 0, 1), (7, 3, 3, -1))
    summed = ((8, 1, 2, 1), (9, 3, 1, -1), (10, 1, 3, 1), (11, 3, 0, -1))

    def send(c, half, messages):
        for m, d, e, step in messages:
            first(c, m, half, d, e, step).start()

    def block_rows(j):
        k = j // 2
        dz = (k % 2) * (1 - k // 2) + (1 - k % 2) * (2 + k // 2)
        return pl.ds(pl.multiple_of(ring(z, dz) * 1280 + (j % 2) * F, F), F)

    def fetch(j):
        return [
            pltpu.make_async_copy(src.at[block_rows(j)], wbuf.at[j % 3, n], wsem.at[j % 3, n])
            for n, src in enumerate((wq_hbm, wk_hbm, wv_hbm))
        ]

    def start_fetch(j):
        for item in fetch(j):
            item.start()

    def multiply(c):
        tokens = pl.ds(*CHUNKS[c])

        def one(j, carry):
            for item in fetch(j):
                item.wait()

            left = jnp.concatenate([wbuf[j % 3, n] for n in range(3)], axis=1)
            go[block_rows(j), tokens] = low(dot(left, gt[:, tokens]))

            @pl.when(j < 5)
            def _():
                start_fetch(j + 3)

            events = {
                1: ((0, far), (1, (far[0], alone[1]))),
                3: ((1, (far[1], alone[0])), (0, (alone[0], alone[2]))),
                5: ((1, (far[2], alone[3])), (0, (alone[1], alone[3]))),
                7: ((1, (far[3], alone[2])),),
            }
            for when in events:
                @pl.when(j == when)
                def _(when=when):
                    for half, messages in events[when]:
                        send(c, half, messages)

            return carry

        lax.fori_loop(0, 8, one, 0)

    def pass_on(c, message):
        m, d, e, step = message

        def one(half):
            first(c, m - 8, half, d, e, step).wait_recv()
            ref = part(c, half, d, e)
            ref[...] = low(wide(ref[...]) + got(c, in1, half * 12 + m - 8))
            first(c, m, half, d, e, step).start()

        both(one)

    def collect(c, half, e, up, down):
        first(c, up, half, 0, e, 1).wait_recv()
        first(c, down, half, 0, e, 1).wait_recv()
        return wide(part(c, half, 0, e)[...]) + got(c, in1, half * 12 + up) + got(c, in1, half * 12 + down)

    def collect_far(c, half):
        part(c, half, 0, 2)[...] = low(collect(c, half, 2, 8, 5))
        second(c, 0, half, 2, 0, 1).start()
        second(c, 1, half, 2, 80, -1).start()

    def collect_next(c, half):
        part(c, half, 0, 1)[...] = low(collect(c, half, 1, 4, 9))
        second(c, 2, half, 1, 80, 1).start()

    def collect_last(c, half):
        part(c, half, 0, 3)[...] = low(collect(c, half, 3, 10, 7))
        second(c, 4, half, 3, 0, -1).start()

    def add_next(c, half):
        second(c, 0, half, 1, 0, 1).wait_recv()
        ref = part(c, half, 0, 1, 0, 80)
        ref[...] = low(wide(ref[...]) + got(c, in2, half * 6))
        second(c, 3, half, 1, 0, 1).start()

    def add_last(c, half):
        second(c, 1, half, 3, 80, -1).wait_recv()
        ref = part(c, half, 0, 3, 80, 80)
        ref[...] = low(wide(ref[...]) + got(c, in2, half * 6 + 1))
        second(c, 5, half, 3, 80, -1).start()

    def collect_own(c, half):
        total = collect(c, half, 0, 6, 11)
        for m in (2, 3, 4, 5):
            second(c, m, half, 0, 0, 1).wait_recv()
        at = pl.multiple_of(half * 160, 16)
        n, tokens = half * 6, pl.ds(*CHUNKS[c])
        out_ref[pl.ds(at, 80), tokens] = low(total[0:80] + (got(c, in2, n + 3) + got(c, in2, n + 4)))
        out_ref[pl.ds(at + 80, 80), tokens] = low(
            total[80:160] + (got(c, in2, n + 2) + got(c, in2, n + 5))
        )

    def scatter_steps(c):
        steps = [lambda message=message: pass_on(c, message) for message in summed]
        for collector in (collect_far, collect_next, collect_last, add_next, add_last, collect_own):
            steps.append(lambda collector=collector: both(lambda half: collector(c, half)))
        return steps

    def eight(body, events):
        def one(s, carry):
            body(s)
            for when in events:
                @pl.when(s == when)
                def _(when=when):
                    events[when]()

            return carry

        lax.fori_loop(0, 8, one, 0)

    def grads_near():
        grads.near()
        products.near()

    for j in range(3):
        start_fetch(j)
    eight(lambda s: query_grad(0, s), {7: grads_near})
    to_gt(0, gq, SCALE, 0)
    both(drain)
    by_arrival((grads, products), lambda s: key_grad(0, s), {})
    to_gt(1, gk, SCALE, 0)
    to_gt(2, gv, 1.0, 0)
    multiply(0)
    for j in range(3):
        start_fetch(j)
    steps = scatter_steps(0)
    eight(lambda s: query_grad(1, s), {4: steps[0], 5: steps[1], 6: steps[2], 7: steps[3]})
    to_gt(0, gq, SCALE, 1)
    eight(lambda s: key_grad(1, s), {6: steps[4]})
    to_gt(1, gk, SCALE, 1)
    to_gt(2, gv, 1.0, 1)
    multiply(1)
    rest = scatter_steps(1)
    for step in steps[5:9] + rest[:4] + steps[9:] + rest[4:]:
        step()

    def sent1(m, carry):
        for c in (0, 1):
            first(c, m, 0, 0, 0, 1).wait_send()
        return carry

    def sent2(m, carry):
        for c in (0, 1):
            second(c, m, 0, 0, 0, 1).wait_send()
        return carry

    lax.fori_loop(0, 24, sent1, 0)
    lax.fori_loop(0, 12, sent2, 0)
    for item in (keys, queries, values, grads, totals, products):
        item.drain()


def per_device(queries, keys, values, grad_out, frame_map, band, w_query, w_key, w_value, w_out):
    vmem = pl.BlockSpec(memory_space=pltpu.VMEM)
    hbm = pl.BlockSpec(memory_space=pl.ANY)
    smem = pl.BlockSpec(memory_space=pltpu.SMEM)
    gathered = pltpu.VMEM((8 * F, 256), jnp.bfloat16)
    stats = pltpu.VMEM((128, F), jnp.float32)
    pairs = pltpu.VMEM((2, 8, F, F), jnp.bfloat16)
    heads = pltpu.VMEM((2, F, HD), jnp.float32)
    sems = pltpu.SemaphoreType.DMA
    return pl.pallas_call(
        kernel,
        out_shape=jax.ShapeDtypeStruct((320, F), jnp.bfloat16),
        in_specs=[smem] * 2 + [hbm] * 8,
        out_specs=vmem,
        scratch_shapes=[
            pltpu.VMEM((5120, F), jnp.bfloat16),
            pltpu.VMEM((256, 5120), jnp.bfloat16),
            gathered, gathered, gathered, gathered,
            stats, stats,
            pairs, pairs,
            pltpu.VMEM((F, F), jnp.int32),
            pltpu.VMEM((256, F), jnp.float32),
            heads, heads, heads, heads, heads,
            pltpu.VMEM((768, F), jnp.bfloat16),
            pltpu.VMEM((3, 3, F, 256), jnp.bfloat16),
            pltpu.VMEM((24, 160, F), jnp.bfloat16),
            pltpu.VMEM((12, 80, F), jnp.bfloat16),
            sems((6,)), sems((40,)), sems((40,)), sems((8 * ARRAYS,)), sems((8 * ARRAYS,)),
            sems((3, 3)), sems((48,)), sems((48,)), sems((24,)), sems((24,)),
        ],
        compiler_params=pltpu.CompilerParams(
            collective_id=0, has_side_effects=True, vmem_limit_bytes=64 * 1024 * 1024
        ),
        cost_estimate=pl.CostEstimate(
            flops=21_000_000_000, bytes_accessed=14_000_000, transcendentals=13_000_000
        ),
    )(frame_map, band, grad_out.T, w_out, queries, keys, values, w_query, w_key, w_value)


def solution(mesh):
    placed = (
        P("tm", "tensor"),
        P("tm", "tensor"),
        P("tm", "tensor"),
        P("tm", "tensor"),
        P(),
        P(),
        P(None, "tensor"),
        P(None, "tensor"),
        P(None, "tensor"),
        P("tensor", None),
    )
    return jax.shard_map(
        per_device, mesh=mesh, in_specs=placed, out_specs=P("tensor", "tm"), check_vma=False
    )
```

```python
import jax
import jax.numpy as jnp
from jax import lax
from jax.experimental import pallas as pl
from jax.experimental.pallas import tpu as pltpu
from jax.sharding import PartitionSpec as P

HD = 128
F = 640
SCALE = HD ** -0.5
POWER = SCALE * 1.4426950408889634
CHUNKS = ((0, 512), (512, 128))
ARRAYS = 6
MESH = pl.DeviceIdType.MESH
NT = (((1,), (1,)), ((), ()))
masked_score = -1e30


def dot(a, b):
    return jnp.dot(a, b, preferred_element_type=jnp.float32)


def dot_nt(a, b):
    return lax.dot_general(a, b, NT, preferred_element_type=jnp.float32)


def ring(position, step):
    return lax.rem(position + step + 4, 4)


def low(value):
    return value.astype(jnp.bfloat16)


def wide(value):
    return value.astype(jnp.float32)


def kernel(
    frame_map, band, go_hbm, wo_hbm, q_hbm, k_hbm, v_hbm, wq_hbm, wk_hbm, wv_hbm, out_ref,
    go, wo, kall, qall, vall, dall, logs, dots, p, pt, dist, dacc, att, gq,
    tops, sums, row_dot, gt, wbuf, in1, in2,
    load_sem, zs, zr, ys, yr, wsem, s1, r1, s2, r2,
):
    g = lax.axis_index("tensor")
    z, x = g // 4, g % 4
    me = lax.axis_index("tm")
    y, core = me // 2, me % 2
    my_frame = frame_map[me]

    def slot_rows(s):
        return pl.ds(pl.multiple_of(s * F, F), F)

    mine = slot_rows(me)

    def load(n, src, dst):
        return pltpu.make_async_copy(src, dst, load_sem.at[n])

    loads = [
        load(0, go_hbm, go.at[pl.ds(pl.multiple_of(g * 320, 320), 320)]),
        load(1, k_hbm, kall.at[mine]),
        load(2, q_hbm, qall.at[mine]),
        load(3, v_hbm, vall.at[mine]),
        load(4, wo_hbm, wo),
    ]
    for item in loads:
        item.start()

    def block(half, d, e):
        zz = ring(z, d * half + e * (1 - half))
        xx = ring(x, d * (1 - half) + e * half)
        return zz * 4 + xx

    def tensor_copy(half, m, j, kind, target):
        start = j * 320 + half * 160 + (80 if kind == 3 else 0)
        ref = go.at[pl.ds(pl.multiple_of(start, 16), 160 if kind < 2 else 80)]
        n = half * 20 + m
        return pltpu.make_async_remote_copy(
            src_ref=ref, dst_ref=ref, send_sem=zs.at[n], recv_sem=zr.at[n],
            device_id={"tensor": target}, device_id_type=MESH,
        )

    def both(step):
        def one(half, carry):
            step(half)
            return carry

        lax.fori_loop(0, 2, one, 0)

    def spread(half, index, d):
        j = block(half, d, 0)
        m = 4 + 4 * index
        tensor_copy(half, m, j, 0, block(half, 0, 1)).start()
        tensor_copy(half, m + 1, j, 1, block(half, 0, -1)).start()

    def tensor_start(half):
        tensor_copy(half, 0, g, 0, block(half, 1, 0)).start()
        tensor_copy(half, 1, g, 1, block(half, -1, 0)).start()

    def tensor_next(half):
        spread(half, 0, 0)

    def tensor_near(half):
        j = block(half, -1, 0)
        tensor_copy(half, 0, j, 0, g).wait_recv()
        tensor_copy(half, 2, j, 2, block(half, 1, 0)).start()
        spread(half, 1, -1)
        j = block(half, 1, 0)
        tensor_copy(half, 1, j, 1, g).wait_recv()
        tensor_copy(half, 3, j, 3, block(half, -1, 0)).start()
        spread(half, 2, 1)

    def tensor_far(half):
        j = block(half, 2, 0)
        tensor_copy(half, 2, j, 2, g).wait_recv()
        tensor_copy(half, 3, j, 3, g).wait_recv()
        spread(half, 3, 2)

    offsets = (0, -1, 1, 2)

    def forward(index):
        def step(half):
            m, d = 4 + 4 * index, offsets[index]
            j = block(half, d, -1)
            tensor_copy(half, m, j, 0, g).wait_recv()
            tensor_copy(half, m + 2, j, 2, block(half, 0, 1)).start()
            j = block(half, d, 1)
            tensor_copy(half, m + 1, j, 1, g).wait_recv()
            tensor_copy(half, m + 3, j, 3, block(half, 0, -1)).start()

        both(step)

    def finish(half, index):
        m, d = 4 + 4 * index, offsets[index]
        j = block(half, d, 2)
        tensor_copy(half, m + 2, j, 2, g).wait_recv()
        tensor_copy(half, m + 3, j, 3, g).wait_recv()

    def add_row(index):
        cols = pl.ds(pl.multiple_of(ring(z, offsets[index]) * 1280, 1280), 1280)
        dacc[...] += dot(wo[:, cols], go[cols, :])

    sibling = y * 2 + 1 - core

    def at_y(step):
        return ring(y, step) * 2 + core

    class Gather:
        def __init__(self, array, ref, rows):
            self.array, self.ref, self.rows = array, ref, rows

        def copy(self, m, slot, target):
            start, count = slot * self.rows, self.rows
            if m in (2, 3):
                count = self.rows // 2
                start = start + (m - 2) * count
            ref = self.ref.at[pl.ds(pl.multiple_of(start, count), count)]
            n = self.array * 8 + m
            return pltpu.make_async_remote_copy(
                src_ref=ref, dst_ref=ref, send_sem=ys.at[n], recv_sem=yr.at[n],
                device_id={"tm": target}, device_id_type=MESH,
            )

        def start(self):
            self.copy(0, me, at_y(1)).start()
            self.copy(1, me, at_y(-1)).start()
            self.copy(4, me, sibling).start()

        def near(self):
            self.copy(0, at_y(-1), me).wait_recv()
            self.copy(2, at_y(-1), at_y(1)).start()
            self.copy(5, at_y(-1), sibling).start()
            self.copy(1, at_y(1), me).wait_recv()
            self.copy(3, at_y(1), at_y(-1)).start()
            self.copy(6, at_y(1), sibling).start()

        def far(self):
            self.copy(2, at_y(2), me).wait_recv()
            self.copy(3, at_y(2), me).wait_recv()
            self.copy(7, at_y(2), sibling).start()

        def from_sibling(self, *messages):
            for m in messages:
                slot = ring(y, (0, -1, 1, 2)[m - 4]) * 2 + 1 - core
                self.copy(m, slot, me).wait_recv()

        def drain(self):
            for m in range(8):
                self.copy(m, me, me).wait_send()

    keys, queries = Gather(0, kall, F), Gather(1, qall, F)
    values, grads = Gather(2, vall, F), Gather(3, dall, F)
    totals, products = Gather(4, logs, 16), Gather(5, dots, 16)

    def by_arrival(gathers, body, events):
        def step(n, carry):
            ring_at = (n + 2) // 4
            hop = (ring_at % 2) * (2 * (n % 2) - 1) + (ring_at // 2) * 2
            other = (1 - ring_at % 2) * (n % 2) + (ring_at % 2) * (((n + 2) // 2) % 2)
            slot = ring(y, hop) * 2 + (core + other) % 2
            waits = {
                1: lambda item: item.from_sibling(4),
                4: lambda item: item.from_sibling(5, 6),
                6: lambda item: item.far(),
                7: lambda item: item.from_sibling(7),
            }
            for when in range(8):
                if when in waits or when in events:
                    @pl.when(n == when)
                    def _(when=when):
                        if when in events:
                            events[when]()
                        if when in waits:
                            for item in gathers:
                                waits[when](item)

            body(slot)
            return carry

        lax.fori_loop(0, 8, step, 0)

    lane = lax.broadcasted_iota(jnp.int32, (F, HD), 1)

    def head(ref, rows, h):
        return ref[rows, h * HD:(h + 1) * HD]

    def stat_row(ref, s, h):
        return ref[pl.ds(pl.multiple_of(s * 16 + h * 8, 8), 8), :][0:1, :]

    def to_row(ref, h, column):
        rows = pl.ds(pl.multiple_of(me * 16 + h * 8, 8), 8)
        ref[rows, :] = jnp.broadcast_to(column, (F, HD)).T[0:8, :]

    def factor(h, s, at=0, count=F):
        own = sums[h, at:at + count, :]
        return jnp.sum(jnp.where(lane[at:at + count] == s, own, 0.0), axis=1, keepdims=True)

    def softmax(s):
        width = band[my_frame, frame_map[s]]
        for h in (0, 1):
            scores = dot_nt(head(qall, mine, h), head(kall, slot_rows(s), h))
            scores = jnp.where(dist[...] <= width, scores, masked_score)
            top = jnp.max(scores, axis=1, keepdims=True) * POWER
            shifted = jnp.exp2(scores * POWER - top)
            total = jnp.sum(shifted, axis=1, keepdims=True)
            p[h, s] = low(shifted)
            tops[h] = jnp.where(lane == s, top, tops[h])
            sums[h] = jnp.where(lane == s, total, sums[h])

    def combine():
        for h in (0, 1):
            top = jnp.max(tops[h], axis=1, keepdims=True)
            shares = jnp.exp2(tops[h] - top)
            total = jnp.sum(shares * sums[h], axis=1, keepdims=True)
            sums[h] = shares / total
            to_row(logs, h, top + jnp.log2(total))

    def key_side(s):
        width = band[frame_map[s], my_frame]
        for h in (0, 1):
            scores = dot_nt(head(kall, mine, h), head(qall, slot_rows(s), h))
            power = jnp.where(
                dist[...] <= width, scores * POWER - stat_row(logs, s, h), masked_score
            )
            pt[h, s] = low(jnp.exp2(power))

    def attend(s):
        for h in (0, 1):
            att[h] += factor(h, s) * dot(p[h, s], head(vall, slot_rows(s), h))

    def query_grad(c, s):
        at, count = CHUNKS[c]
        rows, own = pl.ds(at, count), pl.ds(pl.multiple_of(me * F + at, 128), count)
        for h in (0, 1):
            grad = dot_nt(head(dall, own, h), head(vall, slot_rows(s), h))
            grad = low(grad - jnp.concatenate([row_dot[h, rows, :]] * 5, axis=1))
            product = dot(p[h, s, rows, :] * grad, head(kall, slot_rows(s), h))
            gq[h, rows, :] += factor(h, s, at, count) * product

    def key_grad(c, s):
        at, count = CHUNKS[c]
        rows, own = pl.ds(at, count), pl.ds(pl.multiple_of(me * F + at, 128), count)
        for h in (0, 1):
            grad_rows = head(dall, slot_rows(s), h)
            weight = pt[h, s, rows, :]
            grad = low(dot_nt(head(vall, own, h), grad_rows) - stat_row(dots, s, h))
            gv[h, rows, :] += dot(weight, grad_rows)
            gk[h, rows, :] += dot(weight * grad, head(qall, slot_rows(s), h))

    barrier = pltpu.get_barrier_semaphore()
    for half in (0, 1):
        for step in (1, -1):
            pl.semaphore_signal(
                barrier, inc=1, device_id={"tensor": block(half, step, 0)}, device_id_type=MESH
            )
    for target in (at_y(1), at_y(-1), sibling):
        pl.semaphore_signal(barrier, inc=1, device_id={"tm": target}, device_id_type=MESH)
    loads[0].wait()
    loads[1].wait()
    pl.semaphore_wait(barrier, 7)
    both(tensor_start)
    keys.start()
    both(tensor_next)
    across = lax.broadcasted_iota(jnp.int32, (F, F), 0) - lax.broadcasted_iota(jnp.int32, (F, F), 1)
    dist[...] = jnp.abs(across)
    for ref in (dacc, att, gq, sums):
        ref[...] = jnp.zeros_like(ref)
    tops[...] = jnp.full_like(tops, masked_score)
    for item in loads[2:]:
        item.wait()

    def keys_near():
        both(tensor_near)
        keys.near()
        queries.start()

    by_arrival(
        (keys,), softmax,
        {2: keys_near, 5: lambda: both(tensor_far), 7: lambda: forward(0)},
    )
    queries.near()
    values.start()
    combine()
    totals.start()
    totals.near()
    by_arrival(
        (queries, totals), key_side,
        {3: lambda: forward(1), 5: lambda: forward(2), 7: lambda: forward(3)},
    )
    values.near()

    def near_row(index):
        finish(1, index)
        add_row(index)

    near_row(0)
    by_arrival((values,), attend, {4: lambda: near_row(1), 6: lambda: near_row(2)})
    for index in range(4):
        finish(0, index)
    near_row(3)
    dall[mine, :] = low(dacc[...].T)
    grads.start()
    for h in (0, 1):
        column = jnp.sum(wide(head(dall, mine, h)) * att[h], axis=1, keepdims=True)
        row_dot[h] = jnp.broadcast_to(column, (F, HD))
        to_row(dots, h, column)
    products.start()
    gk, gv = tops, att
    for ref in (gk, gv):
        ref[...] = jnp.zeros_like(ref)

    def to_gt(n, ref, scale, c):
        rows = pl.ds(*CHUNKS[c])
        for h in (0, 1):
            gt[n * 256 + h * HD:n * 256 + (h + 1) * HD, rows] = low((ref[h, rows, :] * scale).T)

    def drain(half):
        def one(i, carry):
            for kind in range(4):
                tensor_copy(half, 4 * i + kind, g, kind, g).wait_send()
            return carry

        lax.fori_loop(0, 5, one, 0)

    def target(half, d, e):
        return block(1 - half, d, e)

    def part(c, half, d, e, skip=0, count=160):
        start = target(half, d, e) * 320 + half * 160 + skip
        return go.at[pl.ds(pl.multiple_of(start, 16), count), pl.ds(*CHUNKS[c])]

    def got(c, ref, n):
        return wide(ref[n, :, pl.ds(*CHUNKS[c])])

    def first(c, m, half, d, e, step):
        n = half * 12 + m
        return pltpu.make_async_remote_copy(
            src_ref=part(c, half, d, e), dst_ref=in1.at[n, :, pl.ds(*CHUNKS[c])],
            send_sem=s1.at[c * 24 + n], recv_sem=r1.at[c * 24 + n],
            device_id={"tensor": target(half, step, 0)}, device_id_type=MESH,
        )

    def second(c, m, half, e, skip, step):
        n = half * 6 + m
        return pltpu.make_async_remote_copy(
            src_ref=part(c, half, 0, e, skip, 80), dst_ref=in2.at[n, :, pl.ds(*CHUNKS[c])],
            send_sem=s2.at[c * 12 + n], recv_sem=r2.at[c * 12 + n],
            device_id={"tensor": target(half, 0, step)}, device_id_type=MESH,
        )

    far = ((0, 2, 2, 1), (1, 2, 1, -1), (2, 2, 3, 1), (3, 2, 0, -1))
    alone = ((4, 1, 1, 1), (5, 3, 2, -1), (6, 1, 0, 1), (7, 3, 3, -1))
    summed = ((8, 1, 2, 1), (9, 3, 1, -1), (10, 1, 3, 1), (11, 3, 0, -1))

    def send(c, half, messages):
        for m, d, e, step in messages:
            first(c, m, half, d, e, step).start()

    def block_rows(j):
        k = j // 2
        dz = (k % 2) * (1 - k // 2) + (1 - k % 2) * (2 + k // 2)
        return pl.ds(pl.multiple_of(ring(z, dz) * 1280 + (j % 2) * F, F), F)

    def fetch(j):
        return [
            pltpu.make_async_copy(src.at[block_rows(j)], wbuf.at[j % 3, n], wsem.at[j % 3, n])
            for n, src in enumerate((wq_hbm, wk_hbm, wv_hbm))
        ]

    def start_fetch(j):
        for item in fetch(j):
            item.start()

    def multiply(c):
        tokens = pl.ds(*CHUNKS[c])

        def one(j, carry):
            for item in fetch(j):
                item.wait()

            left = jnp.concatenate([wbuf[j % 3, n] for n in range(3)], axis=1)
            go[block_rows(j), tokens] = low(dot(left, gt[:, tokens]))

            @pl.when(j < 5)
            def _():
                start_fetch(j + 3)

            events = {
                1: ((0, far), (1, (far[0], alone[1]))),
                3: ((1, (far[1], alone[0])), (0, (alone[0], alone[2]))),
                5: ((1, (far[2], alone[3])), (0, (alone[1], alone[3]))),
                7: ((1, (far[3], alone[2])),),
            }
            for when in events:
                @pl.when(j == when)
                def _(when=when):
                    for half, messages in events[when]:
                        send(c, half, messages)

            return carry

        lax.fori_loop(0, 8, one, 0)

    def pass_on(c, message):
        m, d, e, step = message

        def one(half):
            first(c, m - 8, half, d, e, step).wait_recv()
            ref = part(c, half, d, e)
            ref[...] = low(wide(ref[...]) + got(c, in1, half * 12 + m - 8))
            first(c, m, half, d, e, step).start()

        both(one)

    def collect(c, half, e, up, down):
        first(c, up, half, 0, e, 1).wait_recv()
        first(c, down, half, 0, e, 1).wait_recv()
        return wide(part(c, half, 0, e)[...]) + got(c, in1, half * 12 + up) + got(c, in1, half * 12 + down)

    def collect_far(c, half):
        part(c, half, 0, 2)[...] = low(collect(c, half, 2, 8, 5))
        second(c, 0, half, 2, 0, 1).start()
        second(c, 1, half, 2, 80, -1).start()

    def collect_next(c, half):
        part(c, half, 0, 1)[...] = low(collect(c, half, 1, 4, 9))
        second(c, 2, half, 1, 80, 1).start()

    def collect_last(c, half):
        part(c, half, 0, 3)[...] = low(collect(c, half, 3, 10, 7))
        second(c, 4, half, 3, 0, -1).start()

    def add_next(c, half):
        second(c, 0, half, 1, 0, 1).wait_recv()
        ref = part(c, half, 0, 1, 0, 80)
        ref[...] = low(wide(ref[...]) + got(c, in2, half * 6))
        second(c, 3, half, 1, 0, 1).start()

    def add_last(c, half):
        second(c, 1, half, 3, 80, -1).wait_recv()
        ref = part(c, half, 0, 3, 80, 80)
        ref[...] = low(wide(ref[...]) + got(c, in2, half * 6 + 1))
        second(c, 5, half, 3, 80, -1).start()

    def collect_own(c, half):
        total = collect(c, half, 0, 6, 11)
        for m in (2, 3, 4, 5):
            second(c, m, half, 0, 0, 1).wait_recv()
        at = pl.multiple_of(half * 160, 16)
        n, tokens = half * 6, pl.ds(*CHUNKS[c])
        out_ref[pl.ds(at, 80), tokens] = low(total[0:80] + (got(c, in2, n + 3) + got(c, in2, n + 4)))
        out_ref[pl.ds(at + 80, 80), tokens] = low(
            total[80:160] + (got(c, in2, n + 2) + got(c, in2, n + 5))
        )

    def scatter_steps(c):
        steps = [lambda message=message: pass_on(c, message) for message in summed]
        for collector in (collect_far, collect_next, collect_last, add_next, add_last, collect_own):
            steps.append(lambda collector=collector: both(lambda half: collector(c, half)))
        return steps

    def eight(body, events):
        def one(s, carry):
            body(s)
            for when in events:
                @pl.when(s == when)
                def _(when=when):
                    events[when]()

            return carry

        lax.fori_loop(0, 8, one, 0)

    def grads_near():
        grads.near()
        products.near()

    for j in range(3):
        start_fetch(j)
    eight(lambda s: query_grad(0, s), {7: grads_near})
    to_gt(0, gq, SCALE, 0)
    both(drain)
    by_arrival((grads, products), lambda s: key_grad(0, s), {})
    to_gt(1, gk, SCALE, 0)
    to_gt(2, gv, 1.0, 0)
    multiply(0)
    for j in range(3):
        start_fetch(j)
    steps = scatter_steps(0)
    eight(lambda s: query_grad(1, s), {4: steps[0], 5: steps[1], 6: steps[2], 7: steps[3]})
    to_gt(0, gq, SCALE, 1)
    eight(lambda s: key_grad(1, s), {6: steps[4]})
    to_gt(1, gk, SCALE, 1)
    to_gt(2, gv, 1.0, 1)
    multiply(1)
    rest = scatter_steps(1)
    for step in steps[5:9] + rest[:4] + steps[9:] + rest[4:]:
        step()

    def sent1(m, carry):
        for c in (0, 1):
            first(c, m, 0, 0, 0, 1).wait_send()
        return carry

    def sent2(m, carry):
        for c in (0, 1):
            second(c, m, 0, 0, 0, 1).wait_send()
        return carry

    lax.fori_loop(0, 24, sent1, 0)
    lax.fori_loop(0, 12, sent2, 0)
    for item in (keys, queries, values, grads, totals, products):
        item.drain()


def per_device(queries, keys, values, grad_out, frame_map, band, w_query, w_key, w_value, w_out):
    vmem = pl.BlockSpec(memory_space=pltpu.VMEM)
    hbm = pl.BlockSpec(memory_space=pl.ANY)
    smem = pl.BlockSpec(memory_space=pltpu.SMEM)
    gathered = pltpu.VMEM((8 * F, 256), jnp.bfloat16)
    stats = pltpu.VMEM((128, F), jnp.float32)
    pairs = pltpu.VMEM((2, 8, F, F), jnp.bfloat16)
    heads = pltpu.VMEM((2, F, HD), jnp.float32)
    sems = pltpu.SemaphoreType.DMA
    return pl.pallas_call(
        kernel,
        out_shape=jax.ShapeDtypeStruct((320, F), jnp.bfloat16),
        in_specs=[smem] * 2 + [hbm] * 8,
        out_specs=vmem,
        scratch_shapes=[
            pltpu.VMEM((5120, F), jnp.bfloat16),
            pltpu.VMEM((256, 5120), jnp.bfloat16),
            gathered, gathered, gathered, gathered,
            stats, stats,
            pairs, pairs,
            pltpu.VMEM((F, F), jnp.int32),
            pltpu.VMEM((256, F), jnp.float32),
            heads, heads, heads, heads, heads,
            pltpu.VMEM((768, F), jnp.bfloat16),
            pltpu.VMEM((3, 3, F, 256), jnp.bfloat16),
            pltpu.VMEM((24, 160, F), jnp.bfloat16),
            pltpu.VMEM((12, 80, F), jnp.bfloat16),
            sems((6,)), sems((40,)), sems((40,)), sems((8 * ARRAYS,)), sems((8 * ARRAYS,)),
            sems((3, 3)), sems((48,)), sems((48,)), sems((24,)), sems((24,)),
        ],
        compiler_params=pltpu.CompilerParams(
            collective_id=0, has_side_effects=True, vmem_limit_bytes=64 * 1024 * 1024
        ),
        cost_estimate=pl.CostEstimate(
            flops=21_000_000_000, bytes_accessed=14_000_000, transcendentals=13_000_000
        ),
    )(frame_map, band, grad_out.T, w_out, queries, keys, values, w_query, w_key, w_value)


def solution(mesh):
    placed = (
        P("tm", "tensor"),
        P("tm", "tensor"),
        P("tm", "tensor"),
        P("tm", "tensor"),
        P(),
        P(),
        P(None, "tensor"),
        P(None, "tensor"),
        P(None, "tensor"),
        P("tensor", None),
    )
    return jax.shard_map(
        per_device, mesh=mesh, in_specs=placed, out_specs=P("tensor", "tm"), check_vma=False
    )
```
